32 devices in a mesh: section: 4 (over z), dp: 2 (over x), mp: 4 (over y, core).
Axes of the slice: x: 2, y: 2, z: 4, core: 2. Of those that a mesh axis runs over, the one named last changes fastest.
Arguments:
- inputs: bfloat16 [8, 512, 768], P('dp', 'mp'), may hold values from -7 to 7
- attn_qkv: bfloat16 [3, 768, 768], P(None, None, 'mp'), may hold values from -0.21875 to 0.21875
- attn_out: bfloat16 [768, 768], P('mp'), may hold values from -0.875 to 0.875
- conv_in: bfloat16 [2, 768, 768], P(None, None, 'mp'), may hold values from -0.21875 to 0.21875
- conv_kernel: bfloat16 [7, 768], P(None, 'mp'), may hold values from -3 to 3
- conv_out: bfloat16 [768, 768], P('mp'), may hold values from -0.3125 to 0.3125
- ffn_up: bfloat16 [2, 768, 3072], P(None, None, 'mp'), may hold values from -0.21875 to 0.21875
- ffn_down: bfloat16 [2, 3072, 768], P(None, 'mp'), may hold values from -0.15625 to 0.15625
- norm_gain: float32 [4, 768], replicated, may hold values from 0.5 to 1.5
- norm_bias: float32 [4, 768], replicated, may hold values from -1.5 to 1.5
- kernel_half: int32 [1], replicated, may hold values from 1 to 3
- batch_plan: int32 [2, 2, 2], replicated, may hold values from -1 to 3, as said below
- masked_positions: int32 [8, 77], P('dp'), may hold values from 0 to 511, as said below
- out_grad: bfloat16 [8, 77, 768], P('dp'), may hold values from -6 to 6
Outputs:
- layer_out: bfloat16 [8, 512, 768], P('dp', 'mp')
- input_grad: float32 [8, 512, 768], P('dp', 'mp')
- grad_attn_qkv: float32 [3, 768, 768], P(None, None, 'mp')
- grad_attn_out: float32 [768, 768], P('mp')
- grad_conv_in: float32 [2, 768, 768], P(None, None, 'mp')
- grad_conv_kernel: float32 [7, 768], P(None, 'mp')
- grad_conv_out: float32 [768, 768], P('mp')
- grad_ffn_up: float32 [2, 768, 3072], P(None, None, 'mp')
- grad_ffn_down: float32 [2, 3072, 768], P(None, 'mp')
- grad_norm_gain: float32 [4, 768], replicated
- grad_norm_bias: float32 [4, 768], replicated
- stream_rms: float32 [2, 8], replicated
The draws below stay inside these ranges and needn't reach their ends.
Inputs may be any that keep to these rules, and one draw needn't show every extreme that they name: In each replica batch_plan[r, m, 0] over m is a permutation of 0 to 1. batch_plan[r, m, 1] is -1 or a slot from 2 to 3; in a replica the paired micro-batches use the slots 2, 3 and so on, each once. Some replica pairs every micro-batch and some replica has a micro-batch of one sequence. `masked_positions`: positions of one sequence are distinct.
All inputs are finite; a program needn't handle non-finite values.
Results may differ from the reference program's by a relative error of at most 0.02.
Values may be sent and summed in bfloat16 or wider, within the bound.
A program may use at most 128 MiB of HBM per device.

```python
import jax
import jax.numpy as jnp
from jax import lax

D = 768
HEADS = 12
HEAD = 64
FF = 3072
SEQ = 512
MB = 2
NMASK = 77
TAPS = 7
SEQS = 8
N_DP = 2


def draw_inputs(key, part):
    key = jax.random.fold_in(key, 1)
    total_rows = 2 * MB * N_DP
    ramp = jnp.exp(0.5 * jnp.log(3.0) * jnp.arange(SEQ, dtype=jnp.float32) / (SEQ - 1))
    base_key = jax.random.fold_in(key, 0)
    noise = jnp.clip(jax.random.normal(base_key, (total_rows, SEQ, D), jnp.float32), -4.0, 4.0)
    return jnp.clip(noise * ramp[None, :, None], -7.0, 7.0).astype(jnp.bfloat16)


def draw_batch_plan(key, part):
    key = jax.random.fold_in(key, 2)
    count_key = jax.random.fold_in(key, 11)
    pick_key = jax.random.fold_in(key, 12)
    first_key = jax.random.fold_in(key, 13)
    order_key = jax.random.fold_in(key, 14)
    pairs_count = jax.random.randint(count_key, (N_DP,), 0, MB + 1)
    pair_pick = jax.random.randint(pick_key, (), 0, N_DP * (N_DP - 1))
    full_replica = pair_pick // (N_DP - 1)
    short_replica = (full_replica + 1 + pair_pick % (N_DP - 1)) % N_DP
    replica_ids = jnp.arange(N_DP)
    pairs_count = jnp.where(replica_ids == full_replica, MB, pairs_count)
    pairs_count = jnp.where(replica_ids == short_replica, jnp.minimum(pairs_count, MB - 1), pairs_count)
    firsts = jax.vmap(lambda sub_key: jax.random.permutation(sub_key, MB))(jax.random.split(first_key, N_DP))
    orders = jax.vmap(lambda sub_key: jax.random.permutation(sub_key, MB))(jax.random.split(order_key, N_DP))
    rank_of = jnp.argsort(orders, axis=1)
    seconds = jnp.where(rank_of < pairs_count[:, None], MB + rank_of, -1)
    return jnp.stack([firsts, seconds], axis=-1).astype(jnp.int32)


def draw_masked_positions(key, part):
    key = jax.random.fold_in(key, 3)
    row_keys = jax.random.split(key, 2 * MB * N_DP)
    return jax.vmap(lambda row_key: jax.random.permutation(row_key, SEQ)[:NMASK])(row_keys).astype(jnp.int32)


def block_levels(own_key, shape, cuts, smallest, top_value):
    factor_of, own = 1.0, jax.random.fold_in(own_key, 6)
    for axis_at, parts in cuts:
        steps = jnp.exp(jax.random.uniform(jax.random.fold_in(own, axis_at), (parts,), jnp.float32, smallest / len(cuts), top_value / len(cuts)))
        factor_of = factor_of * jnp.repeat(steps, shape[axis_at] // parts).reshape([-1 if axis == axis_at else 1 for axis in range(len(shape))])
    return factor_of


def normal_values(key, dims, deviation, bound, cuts=(), held_as=jnp.bfloat16):
    array = jax.random.normal(key, dims, jnp.float32) * deviation
    if len(cuts) > 0:
        array = block_levels(key, dims, cuts, -0.22, 0.18) * array
    return jnp.clip(array, min=-bound, max=bound).astype(held_as)


def setup_inputs(seed: int = 0) -> dict:
    key_of = jax.random.split(jax.random.key(seed), 15)
    return {
        "inputs": draw_inputs(jax.random.fold_in(key_of[14], 71), 0),
        "attn_qkv": normal_values(key_of[1], (3, D, D), D ** -0.5, 0.21875, ((2, 4),)),
        "attn_out": normal_values(key_of[2], (D, D), (D // 16) ** -0.5, 0.875, ((0, 4),)),
        "conv_in": normal_values(key_of[3], (2, D, D), D ** -0.5, 0.21875, ((2, 4),)),
        "conv_kernel": normal_values(key_of[4], (TAPS, D), 0.6, 3.0, ((1, 4),)),
        "conv_out": normal_values(key_of[5], (D, D), (D // 2) ** -0.5, 0.3125, ((0, 4),)),
        "ffn_up": normal_values(key_of[6], (2, D, FF), D ** -0.5, 0.21875, ((2, 4),)),
        "ffn_down": normal_values(key_of[7], (2, FF, D), (FF // 2) ** -0.5, 0.15625, ((1, 4),)),
        "norm_gain": jnp.clip(1.0 + 0.1 * jax.random.normal(key_of[8], (4, D), jnp.float32), 0.5, 1.5),
        "norm_bias": normal_values(key_of[9], (4, D), 0.3, 1.5, (), jnp.float32),
        "kernel_half": jax.random.randint(key_of[10], (1,), 1, 4).astype(jnp.int32),
        "batch_plan": draw_batch_plan(jax.random.fold_in(key_of[14], 71), 0),
        "masked_positions": draw_masked_positions(jax.random.fold_in(key_of[14], 71), 0),
        "out_grad": normal_values(key_of[13], (SEQS, NMASK, D), 1.0, 6.0, ((0, 2),)),
    }


@jax.custom_vjp
def low(v):
    return lax.optimization_barrier(v.astype(jnp.bfloat16)).astype(jnp.float32)

@jax.custom_vjp
def low_back(v):
    return v

def low_keep(v):
    return (low(v), None)

def low_pass(kept, grad):
    return (grad,)

def back_keep(v):
    return (v, None)

def back_low(kept, grad):
    return (low(grad),)
low.defvjp(low_keep, low_pass)
low_back.defvjp(back_keep, back_low)
EPSILON = 1e-05
HIGHEST = lax.Precision.HIGHEST

def matmul(left, right):
    return jnp.dot(left, right, precision=HIGHEST)

def layer_norm(summed, gain_row, shift_term):
    centre = summed - lax.optimization_barrier(jnp.mean(summed, axis=-1, keepdims=True))
    variance = lax.optimization_barrier(jnp.mean(centre * centre, axis=-1, keepdims=True))
    return centre * lax.rsqrt(variance + EPSILON) * gain_row + shift_term

def attention(hidden, qkv_weight, out_weight):
    length = hidden.shape[0]
    queries = low(low_back(matmul(hidden, qkv_weight[0]))).reshape(length, HEADS, HEAD)
    key_rows = low(low_back(matmul(hidden, qkv_weight[1]))).reshape(length, HEADS, HEAD)
    value_rows = low(low_back(matmul(hidden, qkv_weight[2]))).reshape(length, HEADS, HEAD)
    scores = low_back(jnp.einsum('qhe,khe->hqk', queries, key_rows, precision=HIGHEST) * HEAD ** (-0.5))
    weights = low(jax.nn.softmax(scores, axis=-1))
    mixture = jnp.einsum('hqk,khe->qhe', weights, value_rows, precision=HIGHEST).reshape(length, HEADS * HEAD)
    mixture = low(low_back(mixture))
    return matmul(mixture, out_weight)

def feed_forward(hidden, up_weight, down_weight):
    before = low_back(matmul(hidden, up_weight))
    active = low(jax.nn.gelu(before, approximate=False))
    return matmul(active, down_weight)

def convolution(hidden, in_weight, kernel, out_weight, tap_mask):
    length = hidden.shape[0]
    value_rows = low_back(matmul(hidden, in_weight[0]))
    gate_rows = low_back(matmul(hidden, in_weight[1]))
    gated = value_rows * jax.nn.sigmoid(gate_rows)
    margin = TAPS // 2
    padded = jnp.pad(gated, ((margin, margin), (0, 0)))
    mixture = jnp.zeros_like(gated)
    for offset in range(TAPS):
        mixture = mixture + (tap_mask[offset] * kernel[offset])[None, :] * padded[offset:offset + length]
    return matmul(low(mixture), out_weight)

def one_sequence(params, tap_mask, inputs_row):
    qkv_weight, out_weight, conv_in, conv_kernel, conv_out, ffn_up, ffn_down, norm_gain, norm_bias = params
    branches = (lambda hidden: attention(hidden, qkv_weight, out_weight), lambda hidden: feed_forward(hidden, ffn_up[0], ffn_down[0]), lambda hidden: convolution(hidden, conv_in, conv_kernel, conv_out, tap_mask), lambda hidden: feed_forward(hidden, ffn_up[1], ffn_down[1]))
    hidden = inputs_row
    stream_sums = []
    branch_sums = []
    for branch_id in range(4):
        branch_out = low_back(branches[branch_id](hidden))
        normed = layer_norm(hidden + branch_out, norm_gain[branch_id], norm_bias[branch_id])
        stream_sums.append(jnp.sum(hidden * hidden))
        branch_sums.append(jnp.sum(branch_out * branch_out))
        hidden = low(normed) if branch_id < 3 else normed
    return (hidden, jnp.stack(stream_sums + branch_sums))

def reference(inputs, attn_qkv, attn_out, conv_in, conv_kernel, conv_out, ffn_up, ffn_down, norm_gain, norm_bias, kernel_half, batch_plan, masked_positions, out_grad):
    params = tuple((item.astype(jnp.float32) for item in (attn_qkv, attn_out, conv_in, conv_kernel, conv_out, ffn_up, ffn_down, norm_gain, norm_bias)))
    tap_mask = (jnp.abs(jnp.arange(TAPS) - TAPS // 2) <= kernel_half[0]).astype(jnp.float32)
    replicas = batch_plan.shape[0]
    slot_count = 2 * MB
    slot_ids = jnp.arange(slot_count)
    paired = jnp.any(batch_plan[:, :, 1][:, :, None] == slot_ids[None, None, :], axis=1)
    used = ((slot_ids[None, :] < MB) | paired).astype(jnp.float32)
    used_rows = used.reshape(replicas * slot_count)
    seq_index = jnp.arange(replicas * slot_count)[:, None]
    cotangent = jnp.zeros((replicas * slot_count, SEQ, D), jnp.float32).at[seq_index, masked_positions].add(out_grad.astype(jnp.float32))
    cotangent = cotangent * used_rows[:, None, None]

    def forward(weights_all, inputs_all):
        return lax.map(jax.checkpoint(lambda inputs_row: one_sequence(weights_all, tap_mask, inputs_row)), inputs_all)
    (layer_values, sums), pullback = jax.vjp(forward, params, inputs.astype(jnp.float32))
    grad_list, input_grad = pullback((cotangent, jnp.zeros_like(sums)))
    layer_out = (layer_values * used_rows[:, None, None]).astype(jnp.bfloat16)
    input_grad = input_grad * used_rows[:, None, None]
    totals = lax.optimization_barrier(jnp.sum((sums * used_rows[:, None]).reshape(replicas, slot_count, 8), axis=1))
    counts = lax.optimization_barrier(jnp.sum(used, axis=1)) * (SEQ * D)
    stream_rms = jnp.sqrt(totals / counts[:, None])
    return (layer_out, input_grad, grad_list[0], grad_list[1], grad_list[2], grad_list[3], grad_list[4], grad_list[5], grad_list[6], grad_list[7], grad_list[8], stream_rms)
```

```python
import functools
import math

import jax
import jax.numpy as jnp
from jax import lax
from jax.experimental import pallas as pl
from jax.experimental.pallas import tpu as pltpu
from jax.sharding import PartitionSpec as P

HEAD = 64
TAPS = 7
MARGIN = TAPS // 2
EPSILON = 1e-05
SECTIONS = 4
GROUP = 4
PAD = 8
TILE = 32
LANES = 256

F32 = jnp.float32
BF16 = jnp.bfloat16
MESH = pl.DeviceIdType.MESH


def dot(left, right):
    return jnp.dot(left, right, preferred_element_type=F32)


def dot_lanes(left, right):
    return lax.dot_general(left, right, (((1,), (1,)), ((), ())), preferred_element_type=F32)


def dot_rows(left, right):
    return lax.dot_general(left, right, (((0,), (0,)), ((), ())), preferred_element_type=F32)


def round_up(value, step):
    return (value + step - 1) // step * step


def normalise(summed):
    centre = summed - jnp.mean(summed, axis=-1, keepdims=True)
    variance = jnp.mean(centre * centre, axis=-1, keepdims=True)
    inverse = lax.rsqrt(variance + EPSILON)
    return centre * inverse, inverse


def norm_pull(grad_out, normed, inverse, gain_row):
    scaled = grad_out * gain_row
    first = jnp.mean(scaled, axis=-1, keepdims=True)
    second = jnp.mean(scaled * normed, axis=-1, keepdims=True)
    return inverse * (scaled - first - normed * second)


def gelu_parts(before):
    cdf = 0.5 * (1.0 + lax.erf(before * math.sqrt(0.5)))
    slope = cdf + before * jnp.exp(-0.5 * before * before) * (1.0 / math.sqrt(2.0 * math.pi))
    return before * cdf, slope


def two_terms(values):
    high = values.astype(BF16)
    return high, (values - high.astype(F32)).astype(BF16)


def fold(rows):
    count, width = rows.shape
    return jnp.sum(rows.reshape(count // 8, 8, width), axis=0)


def whole_sum(values):
    return jnp.sum(values, axis=(0, 1), keepdims=True)


class Layout:
    def __init__(self, dp, seq, width, heads_width, hidden, marked):
        self.dp, self.seq, self.width = dp, seq, width
        self.heads_width, self.hidden = heads_width, hidden
        self.marked = marked
        self.part = seq // GROUP
        self.chunk = 2 * self.part
        unit = 16 * dp
        conv_rows = round_up(3 * heads_width + 16, max(unit, 128))
        self.conv_at, at = 0, conv_rows
        self.up_at, at = at, at + width
        self.down_at, at = at, at + hidden
        self.attn_at, at = at, at + 4 * heads_width
        self.rows = at
        self.kernel_at = self.conv_at + 3 * heads_width
        self.pieces = {
            "conv": self.cut(self.conv_at, conv_rows, 1),
            "up": self.cut(self.up_at, width, 2),
            "down": self.cut(self.down_at, hidden, 2),
            "attn": self.cut(self.attn_at, 4 * heads_width, 2),
        }
        self.bits = dp.bit_length() - 1
        assert dp == 1 << self.bits and dp <= 8
        self.misc_rows = 16
        self.sets = 3 if dp <= 2 else 2

    def cut(self, start, rows, count):
        step = rows // count
        assert step * count == rows and step % (16 * self.dp) == 0
        return [(start + i * step, step) for i in range(count)]


def main_kernel(
    lay,
    x_in,
    qkv_in,
    ao_in,
    cin_in,
    co_in,
    up_in,
    down_in,
    gain,
    bias,
    tap_weight,
    tap_on,
    where,
    cotangent,
    used,
    final,
    up1_grad,
    down1_grad,
    layer_rows,
    input_rows,
    misc_out,
    wqkv,
    wao,
    wcin,
    wco,
    wup,
    wdown,
    hid,
    dfull,
    normed,
    inverse,
    qkv,
    probs,
    mix,
    dmix,
    dqkv,
    dkv,
    units,
    slope,
    dbefore,
    value,
    sig,
    gated,
    conv,
    dconv,
    dgates,
    hits,
    mh,
    mnorm,
    mslope,
    munits,
    mdz,
    partial,
    cs,
    cr,
    ys,
    yr,
    ms,
    mr,
    mys,
    myr,
    grads,
    xr,
    za,
    zb,
    factors,
    misc,
    misc_in,
    load_sem,
    send_sem,
    recv_sem,
):
    section, replica, member = (
        lax.axis_index("section"),
        lax.axis_index("dp"),
        lax.axis_index("mp"),
    )
    low = lax.rem(member, 2)
    high = lax.div(member, 2)
    part, chunk, width = lay.part, lay.chunk, lay.width
    hw, marked = lay.heads_width, lay.marked
    local_heads = hw // HEAD
    scale = HEAD ** (-0.5)
    side = (section, replica, member + 1 - 2 * low)
    across = (section, replica, lax.rem(member + 2, GROUP))
    is_end = (section == 0) | (section == SECTIONS - 1)
    is_inner = jnp.logical_not(is_end)
    inner_of = jnp.where(section == 0, 1, SECTIONS - 2)
    end_of = jnp.where(section == 1, 0, SECTIONS - 1)
    other_inner = SECTIONS - 1 - section
    counter = [0]
    closing = []
    leaving = {}

    def section_peer(by):
        return (lax.rem(section + by, SECTIONS), replica, member)

    def replica_peer(by):
        return (section, lax.rem(replica + by, lay.dp), member)

    def replica_bit(bit):
        on = lax.rem(lax.div(replica, 1 << bit), 2)
        return (section, replica + (1 - 2 * on) * (1 << bit), member), on

    def slots(count=1):
        at = counter[0]
        counter[0] += count
        return at

    def remote(src, dst, target, slot):
        return pltpu.make_async_remote_copy(
            src_ref=src,
            dst_ref=dst,
            send_sem=send_sem.at[slot],
            recv_sem=recv_sem.at[slot],
            device_id=target,
            device_id_type=MESH,
        )

    def send(src, dst, target, slot=None):
        copy = remote(src, dst, target, slots() if slot is None else slot)
        copy.start()
        closing.append(copy.wait_send)
        return copy

    def send_slot(name, ref, e, t, dst, target, slot=None):
        copy = remote(ref.at[e % lay.sets, t], dst.at[e % lay.sets, t], target, slots() if slot is None else slot)
        copy.start()
        leaving[name, e % lay.sets, t] = copy.wait_send
        return copy

    def reuse(name, e, t):
        wait = leaving.pop((name, e % lay.sets, t), None)
        if wait is not None:
            wait()

    barrier = pltpu.get_barrier_semaphore()
    peers = (
        [side, across]
        + [section_peer(by) for by in range(1, SECTIONS)]
        + [replica_peer(by) for by in range(1, lay.dp)]
    )
    for peer in peers:
        pl.semaphore_signal(barrier, inc=1, device_id=peer, device_id_type=MESH)

    loads = {}
    for at, (name, src, dst) in enumerate(
        [
            ("x", x_in.at[section], hid.at[0, pl.ds(pl.multiple_of(member * part, part), part)]),
            ("qkv", qkv_in, wqkv),
            ("ao", ao_in, wao),
            ("up", up_in, wup),
            ("down", down_in, wdown),
            ("cin", cin_in, wcin),
            ("co", co_in, wco),
        ]
    ):
        copy = pltpu.make_async_copy(src, dst, load_sem.at[at])
        copy.start()
        loads[name] = copy

    misc[...] = jnp.zeros_like(misc)
    lane = lax.broadcasted_iota(jnp.int32, (1, hw), 1)
    head_lanes = [(lane >= HEAD * i) & (lane < HEAD * (i + 1)) for i in range(local_heads)]
    head_low = [jnp.where(on, 1.0, 0.0).astype(BF16) for on in head_lanes]

    def block(at, size):
        return pl.ds(pl.multiple_of(at, size), size)

    def own_rows(t):
        return block(chunk * t + part * low, part)

    def other_rows(t):
        return block(chunk * t + part * (1 - low), part)

    def tiles(count, body, init=0):
        return lax.fori_loop(0, count, body, init)

    def exchange_send(e, t):
        reuse("cs", e, t)
        reuse("ys", e, t)
        at = e % lay.sets

        def body(i, carry):
            rows = block(i * TILE, TILE)
            cs[at, t, rows] = partial[block(part * (1 - low) + i * TILE, TILE)].astype(BF16)
            return carry

        tiles(part // TILE, body)
        copy = send_slot("cs", cs, e, t, cr, side)

        def body(i, carry):
            rows = block(i * TILE, TILE)
            ys[at, t, rows] = partial[block(part * low + i * TILE, TILE)].astype(BF16)
            return carry

        tiles(part // TILE, body)
        return copy

    def sums_across(e, t, core_copy, start=True):
        core_copy.wait_recv()
        at = e % lay.sets

        def body(i, carry):
            rows = block(i * TILE, TILE)
            ys[at, t, rows] = (ys[at, t, rows].astype(F32) + cr[at, t, rows].astype(F32)).astype(BF16)
            return carry

        tiles(part // TILE, body)
        if start:
            return send_slot("ys", ys, e, t, yr, across)

    def total_tile(e, t, rows):
        return ys[e % lay.sets, t, rows].astype(F32) + yr[e % lay.sets, t, rows].astype(F32)

    def send_half(e):
        slot = slots()
        at = e % lay.sets
        out = remote(ys.at[at, 1 - high], yr.at[at, 1 - high], across, slot)
        out.start()
        leaving["ys", at, 0] = out.wait_send
        return remote(ys.at[at, high], yr.at[at, high], across, slot)

    def add_stat(column, amount):
        cell = (lax.broadcasted_iota(jnp.int32, (8, width), 0) == replica) & (
            lax.broadcasted_iota(jnp.int32, (8, width), 1) == column
        )
        misc[8:16] += jnp.where(cell, amount, 0.0)

    def run_exchange(e, work, finish, during=None):
        core, y = [None, None], [None, None]
        for t in range(2):
            work(t)
            core[t] = exchange_send(e, t)
            if t == 1:
                y[0] = sums_across(e, 0, core[0])
        y[1] = sums_across(e, 1, core[1])
        if during is not None:
            during()
        last = []
        for t in range(2):
            y[t].wait_recv()
            last.append(finish(t))
        return last

    def forward_finish(e, k, keep_normed):
        def finish(t):
            at = chunk * t + part * low

            def body(i, carry):
                rows = block(i * TILE, TILE)
                place = block(at + i * TILE, TILE)
                stream = hid[k, place].astype(F32)
                branch = total_tile(e, t, rows)
                norm, inv = normalise(stream + branch)
                if keep_normed:
                    normed[k, t, rows] = norm
                    inverse[k, t, rows] = inv
                hid[k + 1, place] = (norm * gain[k : k + 1] + bias[k : k + 1]).astype(BF16)
                return (carry[0] + fold(stream * stream), carry[1] + fold(branch * branch))

            zero = jnp.zeros((8, width), F32)
            squares = tiles(part // TILE, body, (zero, zero))

            @pl.when(high == t)
            def _():
                add_stat(k, whole_sum(squares[0]) * used[0:1, 0:1])
                add_stat(4 + k, whole_sum(squares[1]) * used[0:1, 0:1])

            rows = own_rows(t)
            return send(hid.at[k + 1, rows], hid.at[k + 1, rows], side)

        return finish

    def norm_back_rows(k, t, grad_tile):
        at = chunk * t + part * low

        def body(i, carry):
            rows = block(i * TILE, TILE)
            dy = grad_tile(rows, block(at + i * TILE, TILE))
            norm = normed[k, t, rows]
            result = norm_pull(dy, norm, inverse[k, t, rows], gain[k : k + 1])
            normed[k, t, rows] = result
            dfull[k, block(at + i * TILE, TILE)] = result.astype(BF16)
            return (carry[0] + fold(dy * norm), carry[1] + fold(dy))

        zero = jnp.zeros((8, width), F32)
        terms = tiles(part // TILE, body, (zero, zero))

        @pl.when(high == t)
        def _():
            misc[k : k + 1] += jnp.sum(terms[0], axis=0, keepdims=True)
            misc[4 + k : 5 + k] += jnp.sum(terms[1], axis=0, keepdims=True)

        rows = own_rows(t)
        return send(dfull.at[k, rows], dfull.at[k, rows], side)

    def marked_total(e, values):
        ms[e] = values.astype(BF16)
        core = send(ms.at[e], mr.at[e], side)
        core.wait_recv()
        mys[e] = (ms[e].astype(F32) + mr[e].astype(F32)).astype(BF16)
        y = send(mys.at[e], myr.at[e], across)
        y.wait_recv()
        return mys[e].astype(F32) + myr[e].astype(F32)

    def reduce_piece(start, rows):
        xr_at, z_at = reduce_piece.xr_at, reduce_piece.z_at
        reduce_piece.xr_at += rows - rows // lay.dp
        reduce_piece.z_at += rows // lay.dp
        first, size = start, rows
        steps = []
        for bit in reversed(range(lay.bits)):
            half = size // 2
            peer, on = replica_bit(bit)
            keep = first + on * half
            give = first + (1 - on) * half
            copy = send(
                grads.at[pl.ds(pl.multiple_of(give, 16), half)],
                xr.at[pl.ds(xr_at, half)],
                peer,
            )
            yield
            copy.wait_recv()
            step = math.gcd(half, 64)

            def body(i, carry, keep=keep, xr_at=xr_at, step=step):
                here = pl.ds(pl.multiple_of(keep + i * step, 16), step)
                there = pl.ds(pl.multiple_of(xr_at + i * step, 16), step)
                grads[here] = (grads[here].astype(F32) + xr[there].astype(F32)).astype(BF16)
                return carry

            tiles(half // step, body)
            xr_at += half
            steps.append((first, size, keep, give, half, peer))
            first, size = keep, half
        mine = pl.ds(pl.multiple_of(first, 16), size)
        z_rows = pl.ds(z_at, size)
        step = math.gcd(size, 64)
        slot_a, slot_b, slot_c = slots(), slots(), slots()

        def z_copy(kind):
            if kind == "a":
                return remote(
                    grads.at[mine], za.at[z_rows], (inner_of, replica, member), slot_a
                )
            if kind == "b":
                return remote(
                    grads.at[mine], zb.at[z_rows], (other_inner, replica, member), slot_b
                )
            return remote(final.at[mine], final.at[mine], (end_of, replica, member), slot_c)

        @pl.when(is_end)
        def _():
            z_copy("a").start()

        yield

        @pl.when(is_inner)
        def _():
            z_copy("a").wait_recv()

            def body(i, carry):
                here = pl.ds(pl.multiple_of(first + i * step, 16), step)
                there = pl.ds(pl.multiple_of(z_at + i * step, 16), step)
                grads[here] = (grads[here].astype(F32) + za[there].astype(F32)).astype(BF16)
                return carry

            tiles(size // step, body)
            z_copy("b").start()

        yield

        @pl.when(is_inner)
        def _():
            z_copy("b").wait_recv()

            def body(i, carry):
                here = pl.ds(pl.multiple_of(first + i * step, 16), step)
                there = pl.ds(pl.multiple_of(z_at + i * step, 16), step)
                final[here] = (grads[here].astype(F32) + zb[there].astype(F32)).astype(BF16)
                return carry

            tiles(size // step, body)
            z_copy("c").start()

        yield

        @pl.when(is_end)
        def _():
            z_copy("c").wait_recv()

        for first, size, keep, give, half, peer in reversed(steps):
            here = pl.ds(pl.multiple_of(keep, 16), half)
            there = pl.ds(pl.multiple_of(give, 16), half)
            slot = slots()
            out = remote(final.at[here], final.at[here], peer, slot)
            out.start()
            closing.append(out.wait_send)
            yield
            remote(final.at[there], final.at[there], peer, slot).wait_recv()

        def close():
            @pl.when(is_end)
            def _():
                z_copy("a").wait_send()

            @pl.when(is_inner)
            def _():
                z_copy("b").wait_send()
                z_copy("c").wait_send()

        closing.append(close)

    reduce_piece.xr_at = 0
    reduce_piece.z_at = 0
    running = []

    def launch(name):
        for start, rows in lay.pieces[name]:
            piece = reduce_piece(start, rows)
            next(piece)
            running.append(piece)

    def pump(count=1):
        for _ in range(count):
            for piece in list(running):
                try:
                    next(piece)
                except StopIteration:
                    running.remove(piece)

    pl.semaphore_wait(barrier, len(peers))
    loads["x"].wait()
    mine = block(member * part, part)
    to_side = send(hid.at[0, mine], hid.at[0, mine], side)
    to_across = send(hid.at[0, mine], hid.at[0, mine], across)
    hits[...] = jnp.where(
        lax.broadcasted_iota(jnp.int32, hits.shape, 0) == where[0:1, 0 : hits.shape[1]], 1.0, 0.0
    ).astype(BF16)
    loads["qkv"].wait()

    def project(at):
        rows = block(at, part)
        for j in range(3):
            qkv[j, rows] = dot(hid[0, rows], wqkv[j]).astype(BF16)

    project(member * part)
    to_side.wait_recv()
    project(side[2] * part)
    to_across.wait_recv()
    theirs = block(across[2] * part, part)
    onward = send(hid.at[0, theirs], hid.at[0, theirs], side)
    project(across[2] * part)
    onward.wait_recv()
    project(lax.rem(side[2] + 2, GROUP) * part)
    loads["ao"].wait()

    def attention_work(t):
        rows = pl.ds(chunk * t, chunk)
        mixture = jnp.zeros((chunk, hw), F32)
        for i in range(local_heads):
            scores = dot_lanes(qkv[0, rows] * head_low[i], qkv[1]) * scale
            top = jnp.max(scores, axis=-1, keepdims=True)
            powers = jnp.exp(scores - top)
            chances = powers * (1.0 / jnp.sum(powers, axis=-1, keepdims=True))
            probs[i, rows] = chances
            mixture = mixture + jnp.where(head_lanes[i], dot(chances.astype(BF16), qkv[2]), 0.0)
        mix[rows] = mixture.astype(BF16)
        partial[...] = dot(mix[rows], wao[...])

    gathered = run_exchange(0, attention_work, forward_finish(0, 0, True))

    loads["up"].wait()
    loads["down"].wait()

    def ffn_forward(layer, src, rows, keep):
        def body(i, carry):
            lanes = block(i * LANES, LANES)
            unit, slope_here = gelu_parts(dot(src[rows], wup[layer, :, lanes]))
            units[rows, lanes] = unit.astype(BF16)
            if keep:
                slope[rows, lanes] = slope_here
            return carry

        tiles(lay.hidden // LANES, body)
        partial[...] = dot(units[rows], wdown[layer])

    def ffn0_work(t):
        gathered[t].wait_recv()
        ffn_forward(0, hid.at[1], pl.ds(chunk * t, chunk), True)

    gathered = run_exchange(1, ffn0_work, forward_finish(1, 1, True))

    loads["cin"].wait()
    loads["co"].wait()
    edge = jnp.zeros((PAD, hw), F32)
    for buffer in (gated, dconv):
        buffer[0:PAD] = edge
        buffer[PAD + lay.seq : 2 * PAD + lay.seq] = edge
    for t in range(2):
        gathered[t].wait_recv()
        rows = pl.ds(chunk * t, chunk)
        value_here = dot(hid[2, rows], wcin[0])
        sig_here = jax.nn.sigmoid(dot(hid[2, rows], wcin[1]))
        value[rows] = value_here
        sig[rows] = sig_here
        gated[pl.ds(PAD + chunk * t, chunk)] = value_here * sig_here
    tap_tile = 64

    def taps(i, carry):
        total = jnp.zeros((tap_tile, hw), F32)
        window = gated[pl.ds(pl.multiple_of(i * tap_tile, 8), tap_tile + 2 * PAD)]
        for j in range(TAPS):
            at = PAD - MARGIN + j
            total = total + tap_weight[j : j + 1] * window[at : at + tap_tile]
        conv[block(i * tap_tile, tap_tile)] = total.astype(BF16)
        return carry

    tiles(lay.seq // tap_tile, taps)

    spots = hits[...]
    conv_marked = dot_rows(spots, conv[...]).astype(BF16)
    stream = dot_rows(spots, hid[2])
    branch = marked_total(0, dot(conv_marked, wco[...]))
    norm2, inv2 = normalise(stream + branch)
    mnorm[0] = norm2
    mh[...] = (norm2 * gain[2:3] + bias[2:3]).astype(BF16)

    def marked_up(i, carry):
        lanes = block(i * LANES, LANES)
        unit, slope_here = gelu_parts(dot(mh[...], wup[1, :, lanes]))
        munits[:, lanes] = unit.astype(BF16)
        mslope[:, lanes] = slope_here
        return carry

    tiles(lay.hidden // LANES, marked_up)
    branch = marked_total(1, dot(munits[...], wdown[1]))
    norm3, inv3 = normalise(mh[...].astype(F32) + branch)
    once = jnp.where(member == 0, 1.0, 0.0).astype(F32)
    dy = cotangent[...].astype(F32)
    misc[3:4] += once * jnp.sum(dy * norm3, axis=0, keepdims=True)
    misc[7:8] += once * jnp.sum(dy, axis=0, keepdims=True)
    dz3 = norm_pull(dy, norm3, inv3, gain[3:4])
    mdz[0] = dz3
    df3 = dz3.astype(BF16)

    per_section = lay.dp * marked
    here = pl.ds(pl.multiple_of(section * per_section + replica * marked, 16), marked)
    factors[0, here] = mh[...]
    factors[1, here] = df3
    factor_copies = [
        send(factors.at[low, here], factors.at[low, here], replica_peer(by))
        for by in range(1, lay.dp)
    ]

    def marked_down(i, carry):
        lanes = block(i * LANES, LANES)
        grad_units = dot_lanes(factors[1, here], wdown[1, lanes])
        munits[:, lanes] = (grad_units * mslope[:, lanes]).astype(BF16)
        return carry

    tiles(lay.hidden // LANES, marked_down)
    dy = mdz[0] + marked_total(2, dot_lanes(munits[...], wup[1]))
    for copy in factor_copies:
        copy.wait_recv()
    ours = pl.ds(pl.multiple_of(section * per_section, 16), per_section)
    factor_copies = [
        send(factors.at[low, ours], factors.at[low, ours], section_peer(by))
        for by in range(1, SECTIONS)
    ]
    norm2 = mnorm[0]
    misc[2:3] += once * jnp.sum(dy * norm2, axis=0, keepdims=True)
    misc[6:7] += once * jnp.sum(dy, axis=0, keepdims=True)
    dz2 = norm_pull(dy, norm2, inv2, gain[2:3])
    dz2_terms = two_terms(dz2)
    mdz[1] = dz2
    df2 = dz2.astype(BF16)

    def spread(rows, terms):
        where_rows = hits[rows]
        return dot(where_rows, terms[0]) + dot(where_rows, terms[1])

    dconv_terms = two_terms(dot_lanes(df2, wco[...]))
    dconv[pl.ds(PAD, lay.seq)] = spread(pl.ds(0, lay.seq), dconv_terms)

    def taps_back(i, carry):
        total = jnp.zeros((tap_tile, hw), F32)
        place = pl.ds(pl.multiple_of(i * tap_tile, 8), tap_tile + 2 * PAD)
        window = dconv[place]
        around = gated[place]
        middle = window[PAD : PAD + tap_tile]
        sums = []
        for j in range(TAPS):
            at = PAD + MARGIN - j
            total = total + tap_weight[j : j + 1] * window[at : at + tap_tile]
            at = PAD - MARGIN + j
            sums.append(jnp.sum(around[at : at + tap_tile] * middle, axis=0, keepdims=True))
        rows = block(i * tap_tile, tap_tile)
        s = sig[rows]
        by_value = total * s
        dgates[0, rows] = by_value.astype(BF16)
        dgates[1, rows] = (by_value * value[rows] * (1.0 - s)).astype(BF16)
        sums.append(jnp.zeros((1, hw), F32))
        return carry + jnp.concatenate(sums, axis=0)

    kernel_rows = tiles(lay.seq // tap_tile, taps_back, jnp.zeros((8, hw), F32)) * tap_on[...]
    grads[pl.ds(lay.kernel_at, lay.up_at - lay.kernel_at)] = jnp.zeros(
        (lay.up_at - lay.kernel_at, width), BF16
    )
    grads[pl.ds(lay.kernel_at, 16), 0:hw] = jnp.concatenate(
        [kernel_rows, jnp.zeros((8, hw), F32)], axis=0
    ).astype(BF16)
    for j in range(2):
        grads[pl.ds(lay.conv_at + j * hw, hw)] = dot_rows(dgates[j], hid[2]).astype(BF16)
    grads[pl.ds(lay.conv_at + 2 * hw, hw)] = dot_rows(conv_marked, df2).astype(BF16)
    launch("conv")

    def conv_back_work(t):
        rows = pl.ds(chunk * t, chunk)
        partial[...] = dot_lanes(dgates[0, rows], wcin[0]) + dot_lanes(dgates[1, rows], wcin[1])

    def conv_back_finish(t):
        def grad_tile(rows, place):
            return total_tile(2, t, rows) + spread(place, dz2_terms)

        return norm_back_rows(1, t, grad_tile)

    gathered = run_exchange(2, conv_back_work, conv_back_finish)

    def ffn0_back_work(t):
        gathered[t].wait_recv()
        rows = pl.ds(chunk * t, chunk)

        def body(i, carry):
            lanes = block(i * LANES, LANES)
            grad_units = dot_lanes(dfull[1, rows], wdown[0, lanes])
            dbefore[rows, lanes] = (grad_units * slope[rows, lanes]).astype(BF16)
            return carry

        tiles(lay.hidden // LANES, body)
        partial[...] = dot_lanes(dbefore[rows], wup[0])

    def ffn0_back_finish(t):
        return norm_back_rows(
            0, t, lambda rows, place: normed[1, t, rows] + total_tile(3, t, rows)
        )

    def weight_rows(start, left, right, count):
        def body(i, carry):
            lanes = block(i * LANES, LANES)
            grads[pl.ds(pl.multiple_of(start + i * LANES, 16), LANES)] = dot_rows(
                left[:, lanes], right[...]
            ).astype(BF16)
            return carry

        tiles(count // LANES, body)

    def ffn0_weights():
        pump()
        weight_rows(lay.up_at, hid.at[1], dbefore, width)
        launch("up")
        pump()
        weight_rows(lay.down_at, units0, dfull.at[1], lay.hidden)
        launch("down")

    units0 = units
    gathered = run_exchange(3, ffn0_back_work, ffn0_back_finish, ffn0_weights)

    dkv[...] = jnp.zeros_like(dkv)
    for t in range(2):
        gathered[t].wait_recv()
        rows = pl.ds(chunk * t, chunk)
        dmix[rows] = dot_lanes(dfull[0, rows], wao[...]).astype(BF16)
        grad_queries = jnp.zeros((chunk, hw), F32)
        for i in range(local_heads):
            chances = probs[i, rows]
            grad_chances = dot_lanes(dmix[rows] * head_low[i], qkv[2])
            grad_scores = chances * (
                grad_chances - jnp.sum(grad_chances * chances, axis=-1, keepdims=True)
            )
            grad_scores = grad_scores.astype(BF16)
            on = head_lanes[i]
            grad_queries = grad_queries + jnp.where(on, dot(grad_scores, qkv[1]), 0.0)
            dkv[0] += jnp.where(on, dot_rows(grad_scores, qkv[0, rows]), 0.0)
            dkv[1] += jnp.where(on, dot_rows(chances.astype(BF16), dmix[rows]), 0.0)
        dqkv[0, rows] = (grad_queries * scale).astype(BF16)
        pump()
    dqkv[1] = (dkv[0] * scale).astype(BF16)
    dqkv[2] = dkv[1].astype(BF16)

    def attention_back_work(t):
        rows = pl.ds(chunk * t, chunk)
        partial[...] = (
            dot_lanes(dqkv[0, rows], wqkv[0])
            + dot_lanes(dqkv[1, rows], wqkv[1])
            + dot_lanes(dqkv[2, rows], wqkv[2])
        )

    core = []
    for t in range(2):
        attention_back_work(t)
        core.append(exchange_send(4, t))
    for t in range(2):
        sums_across(4, t, core[t], start=False)
    last = send_half(4)
    for j in range(3):
        grads[pl.ds(lay.attn_at + j * hw, hw)] = dot_rows(dqkv[j], hid[0]).astype(BF16)
    grads[pl.ds(lay.attn_at + 3 * hw, hw)] = dot_rows(mix[...], dfull[0]).astype(BF16)
    launch("attn")
    pump()
    last.wait_recv()

    def input_body(i, carry):
        rows = block(i * TILE, TILE)
        total = total_tile(4, high, rows)
        input_rows[section, rows] = (normed[0, high, rows] + total).astype(BF16)
        return carry

    tiles(part // TILE, input_body)
    end_copies = [
        send(input_rows.at[section], input_rows.at[section], section_peer(by))
        for by in range(1, SECTIONS)
    ]
    pump()

    def conv_work(t):
        partial[...] = dot(conv[pl.ds(chunk * t, chunk)], wco[...])

    gathered = run_exchange(5, conv_work, forward_finish(5, 2, False), pump)
    core = []
    for t in range(2):
        gathered[t].wait_recv()
        ffn_forward(1, hid.at[3], pl.ds(chunk * t, chunk), False)
        core.append(exchange_send(6, t))
        pump()
    for t in range(2):
        sums_across(6, t, core[t], start=False)
    last = send_half(6)
    pump()

    for copy in factor_copies:
        copy.wait_recv()
    shared = slots()
    send(factors.at[low], factors.at[low], side, shared)
    remote(factors.at[1 - low], factors.at[1 - low], side, shared).wait_recv()
    group_rows = GROUP * marked
    for group in range(SECTIONS * per_section // group_rows):
        rows = pl.ds(group * group_rows, group_rows)

        def recompute(j, carry):
            lanes = block(j * LANES, LANES)
            unit, slope_here = gelu_parts(dot(factors[0, rows], wup[1, :, lanes]))
            units[0:group_rows, lanes] = unit.astype(BF16)
            grad_units = dot_lanes(factors[1, rows], wdown[1, lanes])
            dbefore[0:group_rows, lanes] = (grad_units * slope_here).astype(BF16)
            return carry

        tiles(lay.hidden // LANES, recompute)

        def last_weights(i, carry):
            lanes = block(i * LANES, LANES)
            by_up = dot_rows(factors[0, rows, lanes], dbefore[0:group_rows])
            by_down = dot_rows(units[0:group_rows, lanes], factors[1, rows])
            if group == 0:
                up1_grad[lanes] = by_up
                down1_grad[lanes] = by_down
            else:
                up1_grad[lanes] += by_up
                down1_grad[lanes] += by_down
            return carry

        tiles(width // LANES, last_weights)
        pump()
    last.wait_recv()

    def layer_body(i, carry):
        rows = block(i * TILE, TILE)
        stream = hid[3, block(member * part + i * TILE, TILE)].astype(F32)
        branch = total_tile(6, high, rows)
        norm, _ = normalise(stream + branch)
        result = (norm * gain[3:4] + bias[3:4]) * used[0:1, 0:1]
        layer_rows[section, rows] = result.astype(BF16)
        return (carry[0] + fold(stream * stream), carry[1] + fold(branch * branch))

    zero = jnp.zeros((8, width), F32)
    squares = tiles(part // TILE, layer_body, (zero, zero))
    add_stat(3, whole_sum(squares[0]) * used[0:1, 0:1])
    add_stat(7, whole_sum(squares[1]) * used[0:1, 0:1])
    end_copies += [
        send(layer_rows.at[section], layer_rows.at[section], section_peer(by))
        for by in range(1, SECTIONS)
    ]

    hops = [side, across] + [replica_bit(bit)[0] for bit in range(lay.bits)]
    for at, peer in enumerate(hops):
        misc_in[2 * at] = misc[...]
        copy = send(misc_in.at[2 * at], misc_in.at[2 * at + 1], peer)
        pump()
        copy.wait_recv()
        misc[...] = misc_in[2 * at] + misc_in[2 * at + 1]
    at = 2 * len(hops)
    slot_a, slot_b, slot_c = slots(), slots(), slots()
    to_inner = remote(misc_in.at[at], misc_in.at[at + 1], (inner_of, replica, member), slot_a)
    to_other = remote(misc_in.at[at + 2], misc_in.at[at + 3], (other_inner, replica, member), slot_b)
    to_end = remote(misc_out, misc_out, (end_of, replica, member), slot_c)

    @pl.when(is_end)
    def _():
        misc_in[at] = misc[...]
        to_inner.start()

    pump()

    @pl.when(is_inner)
    def _():
        to_inner.wait_recv()
        misc_in[at + 2] = misc[...] + misc_in[at + 1]
        to_other.start()

    pump()

    @pl.when(is_inner)
    def _():
        to_other.wait_recv()
        misc_out[...] = misc_in[at + 2] + misc_in[at + 3]
        to_end.start()

    pump(8)

    @pl.when(is_end)
    def _():
        to_end.wait_recv()
        to_inner.wait_send()

    @pl.when(is_inner)
    def _():
        to_other.wait_send()
        to_end.wait_send()

    for copy in end_copies:
        copy.wait_recv()
    for wait in closing + list(leaving.values()):
        wait()


def on_device(
    inputs,
    attn_qkv,
    attn_out,
    conv_in,
    conv_kernel,
    conv_out,
    ffn_up,
    ffn_down,
    norm_gain,
    norm_bias,
    kernel_half,
    batch_plan,
    masked_positions,
    out_grad,
):
    section = lax.axis_index("section")
    replica = lax.axis_index("dp")
    dp = lax.axis_size("dp")
    slot_count, part, width = inputs.shape
    micro_count = batch_plan.shape[1]
    count = masked_positions.shape[1]
    marked = round_up(count, 16)
    assert slot_count == SECTIONS == lax.axis_size("section") and lax.axis_size("mp") == GROUP
    hw = attn_out.shape[0]
    hidden = ffn_up.shape[2]
    lay = Layout(dp, part * GROUP, width, hw, hidden, marked)
    assert hidden == width and width % LANES == 0 and hw % HEAD == 0

    slot_ids = jnp.arange(slot_count)
    paired = jnp.any(batch_plan[:, :, 1][:, :, None] == slot_ids[None, None, :], axis=1)
    used_all = ((slot_ids[None, :] < micro_count) | paired).astype(F32)
    used = used_all[replica, section]
    tap_mask = (jnp.abs(jnp.arange(8) - MARGIN) <= kernel_half[0]) & (jnp.arange(8) < TAPS)
    tap_on = jnp.broadcast_to(tap_mask.astype(F32)[:, None], (8, hw))
    tap_weight = jnp.pad(conv_kernel.astype(F32), ((0, 1), (0, 0))) * tap_on
    where = lax.dynamic_index_in_dim(masked_positions, section, 0, keepdims=True)
    where = jnp.pad(where, ((0, 7), (0, 128 - count)), constant_values=-1)
    cotangent = lax.dynamic_index_in_dim(out_grad, section, 0, keepdims=False)
    cotangent = jnp.pad(cotangent, ((0, marked - count), (0, 0))) * used.astype(BF16)
    used_rows = jnp.full((8, 128), used, F32)

    seq, chunk = lay.seq, lay.chunk
    any_spec = pl.BlockSpec(memory_space=pl.ANY)
    vmem_spec = pl.BlockSpec(memory_space=pltpu.VMEM)
    hops = 2 + lay.bits
    all_marked = SECTIONS * dp * marked
    z_rows = lay.rows // dp
    scratch = [
        pltpu.VMEM(attn_qkv.shape, BF16),
        pltpu.VMEM(attn_out.shape, BF16),
        pltpu.VMEM(conv_in.shape, BF16),
        pltpu.VMEM(conv_out.shape, BF16),
        pltpu.VMEM(ffn_up.shape, BF16),
        pltpu.VMEM(ffn_down.shape, BF16),
        pltpu.VMEM((4, seq, width), BF16),
        pltpu.VMEM((2, seq, width), BF16),
        pltpu.VMEM((2, 2, part, width), F32),
        pltpu.VMEM((2, 2, part, 1), F32),
        pltpu.VMEM((3, seq, hw), BF16),
        pltpu.VMEM((hw // HEAD, seq, seq), F32),
        pltpu.VMEM((seq, hw), BF16),
        pltpu.VMEM((seq, hw), BF16),
        pltpu.VMEM((3, seq, hw), BF16),
        pltpu.VMEM((2, seq, hw), F32),
        pltpu.VMEM((seq, hidden), BF16),
        pltpu.VMEM((seq, hidden), F32),
        pltpu.VMEM((seq, hidden), BF16),
        pltpu.VMEM((seq, hw), F32),
        pltpu.VMEM((seq, hw), F32),
        pltpu.VMEM((seq + 2 * PAD, hw), F32),
        pltpu.VMEM((seq, hw), BF16),
        pltpu.VMEM((seq + 2 * PAD, hw), F32),
        pltpu.VMEM((2, seq, hw), BF16),
        pltpu.VMEM((seq, marked), BF16),
        pltpu.VMEM((marked, width), BF16),
        pltpu.VMEM((1, marked, width), F32),
        pltpu.VMEM((marked, hidden), F32),
        pltpu.VMEM((marked, hidden), BF16),
        pltpu.VMEM((2, marked, width), F32),
        pltpu.VMEM((chunk, width), F32),
        pltpu.VMEM((lay.sets, 2, part, width), BF16),
        pltpu.VMEM((lay.sets, 2, part, width), BF16),
        pltpu.VMEM((lay.sets, 2, part, width), BF16),
        pltpu.VMEM((lay.sets, 2, part, width), BF16),
        pltpu.VMEM((3, marked, width), BF16),
        pltpu.VMEM((3, marked, width), BF16),
        pltpu.VMEM((3, marked, width), BF16),
        pltpu.VMEM((3, marked, width), BF16),
        pltpu.VMEM((lay.rows, width), BF16),
        pltpu.VMEM((max(lay.rows - z_rows, 16), width), BF16),
        pltpu.VMEM((z_rows, width), BF16),
        pltpu.VMEM((z_rows, width), BF16),
        pltpu.VMEM((2, all_marked, width), BF16),
        pltpu.VMEM((lay.misc_rows, width), F32),
        pltpu.VMEM((2 * hops + 4, lay.misc_rows, width), F32),
        pltpu.SemaphoreType.DMA((8,)),
        pltpu.SemaphoreType.DMA((160,)),
        pltpu.SemaphoreType.DMA((160,)),
    ]
    final, up1_grad, down1_grad, layer_rows, input_rows, misc = pl.pallas_call(
        functools.partial(main_kernel, lay),
        out_shape=(
            jax.ShapeDtypeStruct((lay.rows, width), BF16),
            jax.ShapeDtypeStruct((width, hidden), F32),
            jax.ShapeDtypeStruct((hidden, width), F32),
            jax.ShapeDtypeStruct((slot_count, part, width), BF16),
            jax.ShapeDtypeStruct((slot_count, part, width), BF16),
            jax.ShapeDtypeStruct((lay.misc_rows, width), F32),
        ),
        in_specs=[any_spec] * 7 + [vmem_spec] * 7,
        out_specs=(vmem_spec,) * 6,
        scratch_shapes=scratch,
        compiler_params=pltpu.CompilerParams(
            collective_id=0, has_side_effects=True, vmem_limit_bytes=62 * 2**20
        ),
        name="layers",
    )(
        inputs,
        attn_qkv,
        attn_out,
        conv_in,
        conv_out,
        ffn_up,
        ffn_down,
        norm_gain,
        norm_bias,
        tap_weight,
        tap_on,
        where,
        cotangent,
        used_rows,
    )
    conv_grads = final[lay.conv_at : lay.conv_at + 3 * hw].astype(F32)
    attn_grads = final[lay.attn_at : lay.attn_at + 4 * hw].astype(F32)
    grad_qkv = attn_grads[: 3 * hw].reshape(3, hw, width).transpose(0, 2, 1)
    grad_cin = conv_grads[: 2 * hw].reshape(2, hw, width).transpose(0, 2, 1)
    grad_kernel = final[lay.kernel_at : lay.kernel_at + TAPS, :hw].astype(F32)
    grad_up = jnp.stack([final[lay.up_at : lay.up_at + width].astype(F32), up1_grad])
    grad_down = jnp.stack([final[lay.down_at : lay.down_at + hidden].astype(F32), down1_grad])
    counts = jnp.sum(used_all, axis=1) * (seq * width)
    stream_rms = jnp.sqrt(misc[8 : 8 + dp, 0:8] / counts[:, None])
    return (
        layer_rows,
        input_rows.astype(F32),
        grad_qkv,
        attn_grads[3 * hw :],
        grad_cin,
        grad_kernel,
        conv_grads[2 * hw :],
        grad_up,
        grad_down,
        misc[0:4],
        misc[4:8],
        stream_rms,
    )


def solution(mesh):
    return jax.shard_map(
        on_device,
        mesh=mesh,
        in_specs=(
            P("dp", "mp", None),
            P(None, None, "mp"),
            P("mp", None),
            P(None, None, "mp"),
            P(None, "mp"),
            P("mp", None),
            P(None, None, "mp"),
            P(None, "mp", None),
            P(),
            P(),
            P(),
            P(),
            P("dp", None),
            P("dp", None, None),
        ),
        out_specs=(
            P("dp", "mp", None),
            P("dp", "mp", None),
            P(None, None, "mp"),
            P("mp", None),
            P(None, None, "mp"),
            P(None, "mp"),
            P("mp", None),
            P(None, None, "mp"),
            P(None, "mp", None),
            P(),
            P(),
            P(),
        ),
        check_vma=False,
    )
```

```python
import functools
import math

import jax
import jax.numpy as jnp
from jax import lax
from jax.experimental import pallas as pl
from jax.experimental.pallas import tpu as pltpu
from jax.sharding import PartitionSpec as P

HEAD = 64
TAPS = 7
MARGIN = TAPS // 2
EPSILON = 1e-05
SECTIONS = 4
GROUP = 4
PAD = 8
TILE = 32
LANES = 256

F32 = jnp.float32
BF16 = jnp.bfloat16
MESH = pl.DeviceIdType.MESH


def dot(left, right):
    return jnp.dot(left, right, preferred_element_type=F32)


def dot_lanes(left, right):
    return lax.dot_general(left, right, (((1,), (1,)), ((), ())), preferred_element_type=F32)


def dot_rows(left, right):
    return lax.dot_general(left, right, (((0,), (0,)), ((), ())), preferred_element_type=F32)


def round_up(value, step):
    return (value + step - 1) // step * step


def normalise(summed):
    centre = summed - jnp.mean(summed, axis=-1, keepdims=True)
    variance = jnp.mean(centre * centre, axis=-1, keepdims=True)
    inverse = lax.rsqrt(variance + EPSILON)
    return centre * inverse, inverse


def norm_pull(grad_out, normed, inverse, gain_row):
    scaled = grad_out * gain_row
    first = jnp.mean(scaled, axis=-1, keepdims=True)
    second = jnp.mean(scaled * normed, axis=-1, keepdims=True)
    return inverse * (scaled - first - normed * second)


def gelu_parts(before):
    cdf = 0.5 * (1.0 + lax.erf(before * math.sqrt(0.5)))
    slope = cdf + before * jnp.exp(-0.5 * before * before) * (1.0 / math.sqrt(2.0 * math.pi))
    return before * cdf, slope


def two_terms(values):
    high = values.astype(BF16)
    return high, (values - high.astype(F32)).astype(BF16)


def fold(rows):
    count, width = rows.shape
    return jnp.sum(rows.reshape(count // 8, 8, width), axis=0)


def whole_sum(values):
    return jnp.sum(values, axis=(0, 1), keepdims=True)


class Layout:
    def __init__(self, dp, micro, seq, width, heads_width, hidden, marked):
        self.dp, self.micro, self.seq, self.width = dp, micro, seq, width
        self.heads_width, self.hidden = heads_width, hidden
        self.marked = marked
        self.part = seq // GROUP
        self.chunk = 2 * self.part
        unit = 16 * dp
        conv_rows = round_up(3 * heads_width + 16, max(unit, 128))
        self.conv_at, at = 0, conv_rows
        self.up_at, at = at, at + width
        self.down_at, at = at, at + hidden
        self.attn_at, at = at, at + 4 * heads_width
        self.rows = at
        self.up1_at, at = at, at + width
        self.down1_at, at = at, at + hidden
        self.all_rows = at
        self.kernel_at = self.conv_at + 3 * heads_width
        self.pieces = {
            "conv": self.cut(self.conv_at, conv_rows, 1),
            "up": self.cut(self.up_at, width, 2),
            "down": self.cut(self.down_at, hidden, 2),
            "attn": self.cut(self.attn_at, 4 * heads_width, 2),
        }
        self.stores = [
            (self.conv_at, self.up_at),
            (self.up_at, width + hidden),
            (self.attn_at, 4 * heads_width),
            (self.up1_at, width + hidden),
        ]
        self.bits = dp.bit_length() - 1
        assert dp == 1 << self.bits and dp <= 8
        self.misc_rows = 16
        self.sets = 3 if dp <= 2 else 2

    def cut(self, start, rows, count):
        step = rows // count
        assert step * count == rows and step % (16 * self.dp) == 0
        return [(start + i * step, step) for i in range(count)]


def main_kernel(
    lay,
    x_in,
    qkv_in,
    ao_in,
    cin_in,
    co_in,
    up_in,
    down_in,
    gain,
    bias,
    taps_in,
    positions,
    cotangent,
    half_size,
    plan,
    final_out,
    layer_rows,
    input_rows,
    misc_out,
    final,
    tap_weight,
    tap_on,
    where,
    wqkv,
    wao,
    wcin,
    wco,
    wup,
    wdown,
    hid,
    dfull,
    normed,
    inverse,
    qkv,
    probs,
    mix,
    dmix,
    dqkv,
    dkv,
    units,
    slope,
    dbefore,
    value,
    sig,
    gated,
    conv,
    dconv,
    dgates,
    hits,
    mh,
    mnorm,
    mslope,
    munits,
    mdz,
    partial,
    cs,
    cr,
    ys,
    yr,
    ms,
    mr,
    mys,
    myr,
    grads,
    xr,
    za,
    zb,
    factors,
    sums,
    misc,
    misc_in,
    load_sem,
    store_sem,
    send_sem,
    recv_sem,
):
    section, replica, member = (
        lax.axis_index("section"),
        lax.axis_index("dp"),
        lax.axis_index("mp"),
    )
    low = lax.rem(member, 2)
    high = lax.div(member, 2)
    part, chunk, width = lay.part, lay.chunk, lay.width
    hw, marked = lay.heads_width, lay.marked
    local_heads = hw // HEAD
    scale = HEAD ** (-0.5)
    side = (section, replica, member + 1 - 2 * low)
    across = (section, replica, lax.rem(member + 2, GROUP))
    is_end = (section == 0) | (section == SECTIONS - 1)
    is_inner = jnp.logical_not(is_end)
    inner_of = jnp.where(section == 0, 1, SECTIONS - 2)
    end_of = jnp.where(section == 1, 0, SECTIONS - 1)
    other_inner = SECTIONS - 1 - section
    counter = [0]
    closing = []
    leaving = {}

    def section_peer(by):
        return (lax.rem(section + by, SECTIONS), replica, member)

    def replica_peer(by):
        return (section, lax.rem(replica + by, lay.dp), member)

    def replica_bit(bit):
        on = lax.rem(lax.div(replica, 1 << bit), 2)
        return (section, replica + (1 - 2 * on) * (1 << bit), member), on

    def slots(count=1):
        at = counter[0]
        counter[0] += count
        return at

    def remote(src, dst, target, slot):
        return pltpu.make_async_remote_copy(
            src_ref=src,
            dst_ref=dst,
            send_sem=send_sem.at[slot],
            recv_sem=recv_sem.at[slot],
            device_id=target,
            device_id_type=MESH,
        )

    def send(src, dst, target, slot=None):
        copy = remote(src, dst, target, slots() if slot is None else slot)
        copy.start()
        closing.append(copy.wait_send)
        return copy

    def send_slot(name, ref, e, t, dst, target, slot=None):
        copy = remote(ref.at[e % lay.sets, t], dst.at[e % lay.sets, t], target, slots() if slot is None else slot)
        copy.start()
        leaving[name, e % lay.sets, t] = copy.wait_send
        return copy

    def reuse(name, e, t):
        wait = leaving.pop((name, e % lay.sets, t), None)
        if wait is not None:
            wait()

    barrier = pltpu.get_barrier_semaphore()
    peers = (
        [side, across]
        + [section_peer(by) for by in range(1, SECTIONS)]
        + [replica_peer(by) for by in range(1, lay.dp)]
    )
    for peer in peers:
        pl.semaphore_signal(barrier, inc=1, device_id=peer, device_id_type=MESH)

    loads = {}
    for at, (name, src, dst) in enumerate(
        [
            ("x", x_in.at[section], hid.at[0, pl.ds(pl.multiple_of(member * part, part), part)]),
            ("qkv", qkv_in, wqkv),
            ("ao", ao_in, wao),
            ("up", up_in, wup),
            ("down", down_in, wdown),
            ("cin", cin_in, wcin),
            ("co", co_in, wco),
        ]
    ):
        copy = pltpu.make_async_copy(src, dst, load_sem.at[at])
        copy.start()
        loads[name] = copy

    misc[...] = jnp.zeros_like(misc)
    holds = section < lay.micro
    for i in range(lay.micro):
        holds = holds | (plan[replica, i, 1] == section)
    used = jnp.where(holds, 1.0, 0.0).astype(F32)
    tap_row = lax.broadcasted_iota(jnp.int32, (TAPS, hw), 0)
    tap_mask = jnp.where(jnp.abs(tap_row - MARGIN) <= half_size[0], 1.0, 0.0)
    tap_on[...] = jnp.zeros_like(tap_on)
    tap_on[0:TAPS] = tap_mask
    tap_weight[0:TAPS] = taps_in[...].astype(F32) * tap_mask
    where[...] = jnp.full(where.shape, -1, jnp.int32)
    where[0:1, 0 : positions.shape[1]] = positions[pl.ds(section, 1)]
    lane = lax.broadcasted_iota(jnp.int32, (1, hw), 1)
    head_lanes = [(lane >= HEAD * i) & (lane < HEAD * (i + 1)) for i in range(local_heads)]
    head_low = [jnp.where(on, 1.0, 0.0).astype(BF16) for on in head_lanes]

    def block(at, size):
        return pl.ds(pl.multiple_of(at, size), size)

    def own_rows(t):
        return block(chunk * t + part * low, part)

    def other_rows(t):
        return block(chunk * t + part * (1 - low), part)

    def tiles(count, body, init=0):
        return lax.fori_loop(0, count, body, init)

    def exchange_send(e, t):
        reuse("cs", e, t)
        reuse("ys", e, t)
        at = e % lay.sets

        def body(i, carry):
            rows = block(i * TILE, TILE)
            cs[at, t, rows] = partial[block(part * (1 - low) + i * TILE, TILE)].astype(BF16)
            return carry

        tiles(part // TILE, body)
        copy = send_slot("cs", cs, e, t, cr, side)

        def body(i, carry):
            rows = block(i * TILE, TILE)
            ys[at, t, rows] = partial[block(part * low + i * TILE, TILE)].astype(BF16)
            return carry

        tiles(part // TILE, body)
        return copy

    def sums_across(e, t, core_copy, start=True):
        core_copy.wait_recv()
        at = e % lay.sets

        def body(i, carry):
            rows = block(i * TILE, TILE)
            ys[at, t, rows] = (ys[at, t, rows].astype(F32) + cr[at, t, rows].astype(F32)).astype(BF16)
            return carry

        tiles(part // TILE, body)
        if start:
            return send_slot("ys", ys, e, t, yr, across)

    def total_tile(e, t, rows):
        return ys[e % lay.sets, t, rows].astype(F32) + yr[e % lay.sets, t, rows].astype(F32)

    def send_half(e):
        slot = slots()
        at = e % lay.sets
        out = remote(ys.at[at, 1 - high], yr.at[at, 1 - high], across, slot)
        out.start()
        leaving["ys", at, 0] = out.wait_send
        return remote(ys.at[at, high], yr.at[at, high], across, slot)

    def add_stat(column, amount):
        cell = (lax.broadcasted_iota(jnp.int32, (8, width), 0) == replica) & (
            lax.broadcasted_iota(jnp.int32, (8, width), 1) == column
        )
        misc[8:16] += jnp.where(cell, amount, 0.0)

    def run_exchange(e, work, finish, during=None):
        core, y = [None, None], [None, None]
        for t in range(2):
            work(t)
            core[t] = exchange_send(e, t)
            if t == 1:
                y[0] = sums_across(e, 0, core[0])
        y[1] = sums_across(e, 1, core[1])
        if during is not None:
            during()
        last = []
        for t in range(2):
            y[t].wait_recv()
            last.append(finish(t))
        return last

    def forward_finish(e, k, keep_normed):
        def finish(t):
            at = chunk * t + part * low

            def body(i, carry):
                rows = block(i * TILE, TILE)
                place = block(at + i * TILE, TILE)
                stream = hid[k, place].astype(F32)
                branch = total_tile(e, t, rows)
                norm, inv = normalise(stream + branch)
                if keep_normed:
                    normed[k, t, rows] = norm
                    inverse[k, t, rows] = inv
                hid[k + 1, place] = (norm * gain[k : k + 1] + bias[k : k + 1]).astype(BF16)
                return (carry[0] + fold(stream * stream), carry[1] + fold(branch * branch))

            zero = jnp.zeros((8, width), F32)
            squares = tiles(part // TILE, body, (zero, zero))

            @pl.when(high == t)
            def _():
                add_stat(k, whole_sum(squares[0]) * used)
                add_stat(4 + k, whole_sum(squares[1]) * used)

            rows = own_rows(t)
            return send(hid.at[k + 1, rows], hid.at[k + 1, rows], side)

        return finish

    def norm_back_rows(k, t, grad_tile):
        at = chunk * t + part * low

        def body(i, carry):
            rows = block(i * TILE, TILE)
            dy = grad_tile(rows, block(at + i * TILE, TILE))
            norm = normed[k, t, rows]
            result = norm_pull(dy, norm, inverse[k, t, rows], gain[k : k + 1])
            normed[k, t, rows] = result
            dfull[k, block(at + i * TILE, TILE)] = result.astype(BF16)
            return (carry[0] + fold(dy * norm), carry[1] + fold(dy))

        zero = jnp.zeros((8, width), F32)
        terms = tiles(part // TILE, body, (zero, zero))

        @pl.when(high == t)
        def _():
            misc[k : k + 1] += jnp.sum(terms[0], axis=0, keepdims=True)
            misc[4 + k : 5 + k] += jnp.sum(terms[1], axis=0, keepdims=True)

        rows = own_rows(t)
        return send(dfull.at[k, rows], dfull.at[k, rows], side)

    def marked_total(e, values):
        ms[e] = values.astype(BF16)
        core = send(ms.at[e], mr.at[e], side)
        core.wait_recv()
        mys[e] = (ms[e].astype(F32) + mr[e].astype(F32)).astype(BF16)
        y = send(mys.at[e], myr.at[e], across)
        y.wait_recv()
        return mys[e].astype(F32) + myr[e].astype(F32)

    def reduce_piece(start, rows):
        xr_at, z_at = reduce_piece.xr_at, reduce_piece.z_at
        reduce_piece.xr_at += rows - rows // lay.dp
        reduce_piece.z_at += rows // lay.dp
        first, size = start, rows
        steps = []
        for bit in reversed(range(lay.bits)):
            half = size // 2
            peer, on = replica_bit(bit)
            keep = first + on * half
            give = first + (1 - on) * half
            copy = send(
                grads.at[pl.ds(pl.multiple_of(give, 16), half)],
                xr.at[pl.ds(xr_at, half)],
                peer,
            )
            yield
            copy.wait_recv()
            step = math.gcd(half, 64)

            def body(i, carry, keep=keep, xr_at=xr_at, step=step):
                here = pl.ds(pl.multiple_of(keep + i * step, 16), step)
                there = pl.ds(pl.multiple_of(xr_at + i * step, 16), step)
                grads[here] = (grads[here].astype(F32) + xr[there].astype(F32)).astype(BF16)
                return carry

            tiles(half // step, body)
            xr_at += half
            steps.append((first, size, keep, give, half, peer))
            first, size = keep, half
        mine = pl.ds(pl.multiple_of(first, 16), size)
        z_rows = pl.ds(z_at, size)
        step = math.gcd(size, 64)
        slot_a, slot_b, slot_c = slots(), slots(), slots()

        def z_copy(kind):
            if kind == "a":
                return remote(
                    grads.at[mine], za.at[z_rows], (inner_of, replica, member), slot_a
                )
            if kind == "b":
                return remote(
                    grads.at[mine], zb.at[z_rows], (other_inner, replica, member), slot_b
                )
            return remote(final.at[mine], final.at[mine], (end_of, replica, member), slot_c)

        @pl.when(is_end)
        def _():
            z_copy("a").start()

        yield

        @pl.when(is_inner)
        def _():
            z_copy("a").wait_recv()

            def body(i, carry):
                here = pl.ds(pl.multiple_of(first + i * step, 16), step)
                there = pl.ds(pl.multiple_of(z_at + i * step, 16), step)
                grads[here] = (grads[here].astype(F32) + za[there].astype(F32)).astype(BF16)
                return carry

            tiles(size // step, body)
            z_copy("b").start()

        yield

        @pl.when(is_inner)
        def _():
            z_copy("b").wait_recv()

            def body(i, carry):
                here = pl.ds(pl.multiple_of(first + i * step, 16), step)
                there = pl.ds(pl.multiple_of(z_at + i * step, 16), step)
                final[here] = (grads[here].astype(F32) + zb[there].astype(F32)).astype(BF16)
                return carry

            tiles(size // step, body)
            z_copy("c").start()

        yield

        @pl.when(is_end)
        def _():
            z_copy("c").wait_recv()

        for first, size, keep, give, half, peer in reversed(steps):
            here = pl.ds(pl.multiple_of(keep, 16), half)
            there = pl.ds(pl.multiple_of(give, 16), half)
            slot = slots()
            out = remote(final.at[here], final.at[here], peer, slot)
            out.start()
            closing.append(out.wait_send)
            yield
            remote(final.at[there], final.at[there], peer, slot).wait_recv()

        def close():
            @pl.when(is_end)
            def _():
                z_copy("a").wait_send()

            @pl.when(is_inner)
            def _():
                z_copy("b").wait_send()
                z_copy("c").wait_send()

        closing.append(close)

    reduce_piece.xr_at = 0
    reduce_piece.z_at = 0
    running = []

    def launch(name):
        for start, rows in lay.pieces[name]:
            piece = reduce_piece(start, rows)
            next(piece)
            running.append(piece)

    def pump(count=1):
        for _ in range(count):
            for piece in list(running):
                try:
                    next(piece)
                except StopIteration:
                    running.remove(piece)

    def final_store(at):
        rows = pl.ds(*lay.stores[at])
        return pltpu.make_async_copy(final.at[rows], final_out.at[rows], store_sem.at[at])

    stored = [0]

    def store_final(at):
        final_store(at).start()

    pl.semaphore_wait(barrier, len(peers))
    loads["x"].wait()
    mine = block(member * part, part)
    to_side = send(hid.at[0, mine], hid.at[0, mine], side)
    to_across = send(hid.at[0, mine], hid.at[0, mine], across)
    hits[...] = jnp.where(
        lax.broadcasted_iota(jnp.int32, hits.shape, 0) == where[0:1, 0 : hits.shape[1]], 1.0, 0.0
    ).astype(BF16)
    loads["qkv"].wait()

    def project(at):
        rows = block(at, part)
        for j in range(3):
            qkv[j, rows] = dot_lanes(hid[0, rows], wqkv[j]).astype(BF16)

    project(member * part)
    to_side.wait_recv()
    project(side[2] * part)
    to_across.wait_recv()
    theirs = block(across[2] * part, part)
    onward = send(hid.at[0, theirs], hid.at[0, theirs], side)
    project(across[2] * part)
    onward.wait_recv()
    project(lax.rem(side[2] + 2, GROUP) * part)
    loads["ao"].wait()

    def attention_work(t):
        rows = pl.ds(chunk * t, chunk)
        mixture = jnp.zeros((chunk, hw), F32)
        for i in range(local_heads):
            scores = dot_lanes(qkv[0, rows] * head_low[i], qkv[1]) * scale
            top = jnp.max(scores, axis=-1, keepdims=True)
            powers = jnp.exp(scores - top)
            chances = powers * (1.0 / jnp.sum(powers, axis=-1, keepdims=True))
            probs[i, rows] = chances
            mixture = mixture + jnp.where(head_lanes[i], dot(chances.astype(BF16), qkv[2]), 0.0)
        mix[rows] = mixture.astype(BF16)
        partial[...] = dot(mix[rows], wao[...])

    gathered = run_exchange(0, attention_work, forward_finish(0, 0, True))

    loads["up"].wait()
    loads["down"].wait()

    def ffn_forward(layer, src, rows, keep):
        def body(i, carry):
            lanes = block(i * LANES, LANES)
            unit, slope_here = gelu_parts(dot(src[rows], wup[layer, :, lanes]))
            units[rows, lanes] = unit.astype(BF16)
            if keep:
                slope[rows, lanes] = slope_here
            return carry

        tiles(lay.hidden // LANES, body)
        partial[...] = dot(units[rows], wdown[layer])

    def ffn0_work(t):
        gathered[t].wait_recv()
        ffn_forward(0, hid.at[1], pl.ds(chunk * t, chunk), True)

    gathered = run_exchange(1, ffn0_work, forward_finish(1, 1, True))

    loads["cin"].wait()
    loads["co"].wait()
    edge = jnp.zeros((PAD, hw), F32)
    for buffer in (gated, dconv):
        buffer[0:PAD] = edge
        buffer[PAD + lay.seq : 2 * PAD + lay.seq] = edge
    for t in range(2):
        gathered[t].wait_recv()
        rows = pl.ds(chunk * t, chunk)
        value_here = dot_lanes(hid[2, rows], wcin[0])
        sig_here = jax.nn.sigmoid(dot_lanes(hid[2, rows], wcin[1]))
        value[rows] = value_here
        sig[rows] = sig_here
        gated[pl.ds(PAD + chunk * t, chunk)] = value_here * sig_here
    tap_tile = 64

    def taps(i, carry):
        total = jnp.zeros((tap_tile, hw), F32)
        window = gated[pl.ds(pl.multiple_of(i * tap_tile, 8), tap_tile + 2 * PAD)]
        for j in range(TAPS):
            at = PAD - MARGIN + j
            total = total + tap_weight[j : j + 1] * window[at : at + tap_tile]
        conv[block(i * tap_tile, tap_tile)] = total.astype(BF16)
        return carry

    tiles(lay.seq // tap_tile, taps)

    spots = hits[...]
    conv_marked = dot_rows(spots, conv[...]).astype(BF16)
    stream = dot_rows(spots, hid[2])
    branch = marked_total(0, dot(conv_marked, wco[...]))
    norm2, inv2 = normalise(stream + branch)
    mnorm[0] = norm2
    mh[...] = (norm2 * gain[2:3] + bias[2:3]).astype(BF16)

    def marked_up(i, carry):
        lanes = block(i * LANES, LANES)
        unit, slope_here = gelu_parts(dot(mh[...], wup[1, :, lanes]))
        munits[:, lanes] = unit.astype(BF16)
        mslope[:, lanes] = slope_here
        return carry

    tiles(lay.hidden // LANES, marked_up)
    branch = marked_total(1, dot(munits[...], wdown[1]))
    norm3, inv3 = normalise(mh[...].astype(F32) + branch)
    once = jnp.where(member == 0, 1.0, 0.0).astype(F32)
    dy = cotangent[...].astype(F32) * used
    misc[3:4] += once * jnp.sum(dy * norm3, axis=0, keepdims=True)
    misc[7:8] += once * jnp.sum(dy, axis=0, keepdims=True)
    dz3 = norm_pull(dy, norm3, inv3, gain[3:4])
    mdz[0] = dz3
    df3 = dz3.astype(BF16)

    per_section = lay.dp * marked
    here = pl.ds(pl.multiple_of(section * per_section + replica * marked, 16), marked)
    factors[0, here] = mh[...]
    factors[1, here] = df3
    factor_copies = [
        send(factors.at[low, here], factors.at[low, here], replica_peer(by))
        for by in range(1, lay.dp)
    ]

    def marked_down(i, carry):
        lanes = block(i * LANES, LANES)
        grad_units = dot_lanes(factors[1, here], wdown[1, lanes])
        munits[:, lanes] = (grad_units * mslope[:, lanes]).astype(BF16)
        return carry

    tiles(lay.hidden // LANES, marked_down)
    dy = mdz[0] + marked_total(2, dot_lanes(munits[...], wup[1]))
    for copy in factor_copies:
        copy.wait_recv()
    ours = pl.ds(pl.multiple_of(section * per_section, 16), per_section)
    factor_copies = [
        send(factors.at[low, ours], factors.at[low, ours], section_peer(by))
        for by in range(1, SECTIONS)
    ]
    norm2 = mnorm[0]
    misc[2:3] += once * jnp.sum(dy * norm2, axis=0, keepdims=True)
    misc[6:7] += once * jnp.sum(dy, axis=0, keepdims=True)
    dz2 = norm_pull(dy, norm2, inv2, gain[2:3])
    dz2_terms = two_terms(dz2)
    mdz[1] = dz2
    df2 = dz2.astype(BF16)

    def spread(rows, terms):
        where_rows = hits[rows]
        return dot(where_rows, terms[0]) + dot(where_rows, terms[1])

    dconv_terms = two_terms(dot_lanes(df2, wco[...]))
    dconv[pl.ds(PAD, lay.seq)] = spread(pl.ds(0, lay.seq), dconv_terms)

    def taps_back(i, carry):
        total = jnp.zeros((tap_tile, hw), F32)
        place = pl.ds(pl.multiple_of(i * tap_tile, 8), tap_tile + 2 * PAD)
        window = dconv[place]
        around = gated[place]
        middle = window[PAD : PAD + tap_tile]
        sums = []
        for j in range(TAPS):
            at = PAD + MARGIN - j
            total = total + tap_weight[j : j + 1] * window[at : at + tap_tile]
            at = PAD - MARGIN + j
            sums.append(jnp.sum(around[at : at + tap_tile] * middle, axis=0, keepdims=True))
        rows = block(i * tap_tile, tap_tile)
        s = sig[rows]
        by_value = total * s
        dgates[0, rows] = by_value.astype(BF16)
        dgates[1, rows] = (by_value * value[rows] * (1.0 - s)).astype(BF16)
        sums.append(jnp.zeros((1, hw), F32))
        return carry + jnp.concatenate(sums, axis=0)

    kernel_rows = tiles(lay.seq // tap_tile, taps_back, jnp.zeros((8, hw), F32)) * tap_on[...]
    grads[pl.ds(lay.kernel_at, lay.up_at - lay.kernel_at)] = jnp.zeros(
        (lay.up_at - lay.kernel_at, width), BF16
    )
    grads[pl.ds(lay.kernel_at, 16), 0:hw] = jnp.concatenate(
        [kernel_rows, jnp.zeros((8, hw), F32)], axis=0
    ).astype(BF16)
    for j in range(2):
        grads[pl.ds(lay.conv_at + j * hw, hw)] = dot_rows(dgates[j], hid[2]).astype(BF16)
    grads[pl.ds(lay.conv_at + 2 * hw, hw)] = dot_rows(conv_marked, df2).astype(BF16)
    launch("conv")

    def conv_back_work(t):
        rows = pl.ds(chunk * t, chunk)
        partial[...] = dot(dgates[0, rows], wcin[0]) + dot(dgates[1, rows], wcin[1])

    def conv_back_finish(t):
        def grad_tile(rows, place):
            return total_tile(2, t, rows) + spread(place, dz2_terms)

        return norm_back_rows(1, t, grad_tile)

    gathered = run_exchange(2, conv_back_work, conv_back_finish)

    def ffn0_back_work(t):
        gathered[t].wait_recv()
        rows = pl.ds(chunk * t, chunk)

        def body(i, carry):
            lanes = block(i * LANES, LANES)
            grad_units = dot_lanes(dfull[1, rows], wdown[0, lanes])
            dbefore[rows, lanes] = (grad_units * slope[rows, lanes]).astype(BF16)
            return carry

        tiles(lay.hidden // LANES, body)
        partial[...] = dot_lanes(dbefore[rows], wup[0])

    def ffn0_back_finish(t):
        return norm_back_rows(
            0, t, lambda rows, place: normed[1, t, rows] + total_tile(3, t, rows)
        )

    def weight_rows(start, left, right, count):
        def body(i, carry):
            lanes = block(i * LANES, LANES)
            grads[pl.ds(pl.multiple_of(start + i * LANES, 16), LANES)] = dot_rows(
                left[:, lanes], right[...]
            ).astype(BF16)
            return carry

        tiles(count // LANES, body)

    def ffn0_weights():
        pump()
        weight_rows(lay.up_at, hid.at[1], dbefore, width)
        launch("up")
        pump()
        weight_rows(lay.down_at, units0, dfull.at[1], lay.hidden)
        launch("down")

    units0 = units
    gathered = run_exchange(3, ffn0_back_work, ffn0_back_finish, ffn0_weights)

    dkv[...] = jnp.zeros_like(dkv)
    for t in range(2):
        gathered[t].wait_recv()
        rows = pl.ds(chunk * t, chunk)
        dmix[rows] = dot_lanes(dfull[0, rows], wao[...]).astype(BF16)
        grad_queries = jnp.zeros((chunk, hw), F32)
        for i in range(local_heads):
            chances = probs[i, rows]
            grad_chances = dot_lanes(dmix[rows] * head_low[i], qkv[2])
            grad_scores = chances * (
                grad_chances - jnp.sum(grad_chances * chances, axis=-1, keepdims=True)
            )
            grad_scores = grad_scores.astype(BF16)
            on = head_lanes[i]
            grad_queries = grad_queries + jnp.where(on, dot(grad_scores, qkv[1]), 0.0)
            dkv[0] += jnp.where(on, dot_rows(grad_scores, qkv[0, rows]), 0.0)
            dkv[1] += jnp.where(on, dot_rows(chances.astype(BF16), dmix[rows]), 0.0)
        dqkv[0, rows] = (grad_queries * scale).astype(BF16)
        pump()
    dqkv[1] = (dkv[0] * scale).astype(BF16)
    dqkv[2] = dkv[1].astype(BF16)

    def attention_back_work(t):
        rows = pl.ds(chunk * t, chunk)
        partial[...] = (
            dot(dqkv[0, rows], wqkv[0])
            + dot(dqkv[1, rows], wqkv[1])
            + dot(dqkv[2, rows], wqkv[2])
        )

    core = []
    for t in range(2):
        attention_back_work(t)
        core.append(exchange_send(4, t))
    for t in range(2):
        sums_across(4, t, core[t], start=False)
    last = send_half(4)
    for j in range(3):
        grads[pl.ds(lay.attn_at + j * hw, hw)] = dot_rows(dqkv[j], hid[0]).astype(BF16)
    grads[pl.ds(lay.attn_at + 3 * hw, hw)] = dot_rows(mix[...], dfull[0]).astype(BF16)
    launch("attn")
    pump()
    last.wait_recv()

    def input_body(i, carry):
        rows = block(i * TILE, TILE)
        total = total_tile(4, high, rows)
        input_rows[section, rows] = (normed[0, high, rows] + total).astype(BF16)
        return carry

    tiles(part // TILE, input_body)
    end_copies = [
        send(input_rows.at[section], input_rows.at[section], section_peer(by))
        for by in range(1, SECTIONS)
    ]
    pump()

    def conv_work(t):
        partial[...] = dot(conv[pl.ds(chunk * t, chunk)], wco[...])

    gathered = run_exchange(5, conv_work, forward_finish(5, 2, False), pump)
    core = []
    for t in range(2):
        gathered[t].wait_recv()
        ffn_forward(1, hid.at[3], pl.ds(chunk * t, chunk), False)
        core.append(exchange_send(6, t))
        pump()
    for t in range(2):
        sums_across(6, t, core[t], start=False)
    last = send_half(6)
    pump()

    for copy in factor_copies:
        copy.wait_recv()
    shared = slots()
    send(factors.at[low], factors.at[low], side, shared)
    remote(factors.at[1 - low], factors.at[1 - low], side, shared).wait_recv()
    group_rows = GROUP * marked
    groups = SECTIONS * per_section // group_rows
    for group in range(groups):
        rows = pl.ds(group * group_rows, group_rows)

        def recompute(j, carry):
            lanes = block(j * LANES, LANES)
            unit, slope_here = gelu_parts(dot(factors[0, rows], wup[1, :, lanes]))
            units[0:group_rows, lanes] = unit.astype(BF16)
            grad_units = dot_lanes(factors[1, rows], wdown[1, lanes])
            dbefore[0:group_rows, lanes] = (grad_units * slope_here).astype(BF16)
            return carry

        tiles(lay.hidden // LANES, recompute)

        def last_weights(i, carry):
            lanes = block(i * LANES, LANES)
            by_up = dot_rows(factors[0, rows, lanes], dbefore[0:group_rows])
            by_down = dot_rows(units[0:group_rows, lanes], factors[1, rows])
            if group > 0:
                by_up = by_up + sums[0, lanes]
                by_down = by_down + sums[1, lanes]
            if group < groups - 1:
                sums[0, lanes] = by_up
                sums[1, lanes] = by_down
            else:
                at = pl.multiple_of(i * LANES, LANES)
                final[pl.ds(lay.up1_at + at, LANES)] = by_up.astype(BF16)
                final[pl.ds(lay.down1_at + at, LANES)] = by_down.astype(BF16)
            return carry

        tiles(width // LANES, last_weights)
        pump()
    last.wait_recv()

    def layer_body(i, carry):
        rows = block(i * TILE, TILE)
        stream = hid[3, block(member * part + i * TILE, TILE)].astype(F32)
        branch = total_tile(6, high, rows)
        norm, _ = normalise(stream + branch)
        result = (norm * gain[3:4] + bias[3:4]) * used
        layer_rows[section, rows] = result.astype(BF16)
        return (carry[0] + fold(stream * stream), carry[1] + fold(branch * branch))

    zero = jnp.zeros((8, width), F32)
    squares = tiles(part // TILE, layer_body, (zero, zero))
    add_stat(3, whole_sum(squares[0]) * used)
    add_stat(7, whole_sum(squares[1]) * used)
    end_copies += [
        send(layer_rows.at[section], layer_rows.at[section], section_peer(by))
        for by in range(1, SECTIONS)
    ]

    hops = [side, across] + [replica_bit(bit)[0] for bit in range(lay.bits)]
    for at, peer in enumerate(hops):
        misc_in[2 * at] = misc[...]
        copy = send(misc_in.at[2 * at], misc_in.at[2 * at + 1], peer)
        pump()
        copy.wait_recv()
        misc[...] = misc_in[2 * at] + misc_in[2 * at + 1]
    at = 2 * len(hops)
    slot_a, slot_b, slot_c = slots(), slots(), slots()
    to_inner = remote(misc_in.at[at], misc_in.at[at + 1], (inner_of, replica, member), slot_a)
    to_other = remote(misc_in.at[at + 2], misc_in.at[at + 3], (other_inner, replica, member), slot_b)
    to_end = remote(misc_out, misc_out, (end_of, replica, member), slot_c)

    @pl.when(is_end)
    def _():
        misc_in[at] = misc[...]
        to_inner.start()

    pump()

    @pl.when(is_inner)
    def _():
        to_inner.wait_recv()
        misc_in[at + 2] = misc[...] + misc_in[at + 1]
        to_other.start()

    pump()

    @pl.when(is_inner)
    def _():
        to_other.wait_recv()
        misc_out[...] = misc_in[at + 2] + misc_in[at + 3]
        to_end.start()

    pump(8)

    @pl.when(is_end)
    def _():
        to_end.wait_recv()
        to_inner.wait_send()

    @pl.when(is_inner)
    def _():
        to_other.wait_send()
        to_end.wait_send()

    for at, (start, rows) in enumerate(lay.stores):
        if at >= stored[0]:
            store_final(at)
    for copy in end_copies:
        copy.wait_recv()
    for at in range(len(lay.stores)):
        final_store(at).wait()
    for wait in closing + list(leaving.values()):
        wait()


def widen_kernel(
    lay,
    final,
    input_rows,
    misc,
    plan,
    input_grad,
    qkv,
    out,
    cin,
    cout,
    up,
    down,
    kernel,
    gains,
    biases,
    rms,
    narrow,
    wide,
    narrow_input,
    wide_input,
    load_sem,
    store_sem,
):
    hw, width, hidden = lay.heads_width, lay.width, lay.hidden
    blocks = []

    def cover(start, rows, target, step):
        for at in range(0, rows, step):
            blocks.append((start + at, step, target.at[pl.ds(at, step)]))

    for layer, (up_at, down_at) in enumerate(
        ((lay.up_at, lay.down_at), (lay.up1_at, lay.down1_at))
    ):
        cover(up_at, width, up.at[layer], width // 2)
        cover(down_at, hidden, down.at[layer], hidden // 2)
    for j in range(3):
        cover(lay.attn_at + j * hw, hw, qkv.at[j], hw)
    cover(lay.attn_at + 3 * hw, hw, out, hw)
    for j in range(2):
        cover(lay.conv_at + j * hw, hw, cin.at[j], hw)
    cover(lay.conv_at + 2 * hw, hw, cout, hw)

    def load(at):
        start, rows, _ = blocks[at]
        here = pl.ds(start, rows)
        return pltpu.make_async_copy(final.at[here], narrow.at[here], load_sem.at[at])

    def store(at):
        start, rows, target = blocks[at]
        return pltpu.make_async_copy(wide.at[pl.ds(start, rows)], target, store_sem.at[at])

    extra = len(blocks)
    tap_rows = pltpu.make_async_copy(
        final.at[pl.ds(lay.kernel_at, 16)], narrow.at[pl.ds(lay.kernel_at, 16)], load_sem.at[extra]
    )
    inputs_in = pltpu.make_async_copy(input_rows, narrow_input, load_sem.at[extra + 1])
    inputs_out = pltpu.make_async_copy(wide_input, input_grad, store_sem.at[extra])
    for at in range(len(blocks)):
        load(at).start()
    inputs_in.start()
    tap_rows.start()
    gains[...] = misc[0:4]
    biases[...] = misc[4:8]
    row = lax.broadcasted_iota(jnp.int32, rms.shape, 0)
    counts = jnp.zeros(rms.shape, F32)
    for r in range(rms.shape[0]):
        total = jnp.float32(lay.micro)
        for i in range(lay.micro):
            total = total + jnp.where(plan[r, i, 1] >= 0, 1.0, 0.0).astype(F32)
        counts = jnp.where(row == r, total, counts)
    rms[...] = jnp.sqrt(misc[8 : 8 + rms.shape[0], 0:8] / (counts * (lay.seq * width)))
    for at, (start, rows, _) in enumerate(blocks):
        load(at).wait()

        def body(i, carry, start=start):
            here = pl.ds(pl.multiple_of(start + i * 32, 16), 32)
            wide[here] = narrow[here].astype(F32)
            return carry

        lax.fori_loop(0, rows // 32, body, 0)
        store(at).start()
    inputs_in.wait()
    for slot in range(input_rows.shape[0]):
        wide_input[slot] = narrow_input[slot].astype(F32)
    inputs_out.start()
    tap_rows.wait()
    taps = narrow[pl.ds(lay.kernel_at, 16)].astype(F32)
    kernel[...] = taps[0:TAPS, 0:hw]
    for at in range(len(blocks)):
        store(at).wait()
    inputs_out.wait()


def on_device(
    inputs,
    attn_qkv,
    attn_out,
    conv_in,
    conv_kernel,
    conv_out,
    ffn_up,
    ffn_down,
    norm_gain,
    norm_bias,
    kernel_half,
    batch_plan,
    masked_positions,
    out_grad,
):
    section = lax.axis_index("section")
    replica = lax.axis_index("dp")
    dp = lax.axis_size("dp")
    slot_count, part, width = inputs.shape
    micro_count = batch_plan.shape[1]
    count = masked_positions.shape[1]
    marked = round_up(count, 16)
    assert slot_count == SECTIONS == lax.axis_size("section") and lax.axis_size("mp") == GROUP
    hw = attn_out.shape[0]
    hidden = ffn_up.shape[2]
    lay = Layout(dp, micro_count, part * GROUP, width, hw, hidden, marked)
    assert hidden == width and width % LANES == 0 and hw % HEAD == 0

    cotangent = lax.dynamic_index_in_dim(out_grad, section, 0, keepdims=False)
    cotangent = jnp.pad(cotangent, ((0, marked - count), (0, 0)))

    seq, chunk = lay.seq, lay.chunk
    any_spec = pl.BlockSpec(memory_space=pl.ANY)
    vmem_spec = pl.BlockSpec(memory_space=pltpu.VMEM)
    hops = 2 + lay.bits
    all_marked = SECTIONS * dp * marked
    z_rows = lay.rows // dp
    scratch = [
        pltpu.VMEM((lay.all_rows, width), BF16),
        pltpu.VMEM((8, hw), F32),
        pltpu.VMEM((8, hw), F32),
        pltpu.VMEM((8, marked), jnp.int32),
        pltpu.VMEM((3, hw, width), BF16),
        pltpu.VMEM(attn_out.shape, BF16),
        pltpu.VMEM((2, hw, width), BF16),
        pltpu.VMEM(conv_out.shape, BF16),
        pltpu.VMEM(ffn_up.shape, BF16),
        pltpu.VMEM(ffn_down.shape, BF16),
        pltpu.VMEM((4, seq, width), BF16),
        pltpu.VMEM((2, seq, width), BF16),
        pltpu.VMEM((2, 2, part, width), F32),
        pltpu.VMEM((2, 2, part, 1), F32),
        pltpu.VMEM((3, seq, hw), BF16),
        pltpu.VMEM((hw // HEAD, seq, seq), F32),
        pltpu.VMEM((seq, hw), BF16),
        pltpu.VMEM((seq, hw), BF16),
        pltpu.VMEM((3, seq, hw), BF16),
        pltpu.VMEM((2, seq, hw), F32),
        pltpu.VMEM((seq, hidden), BF16),
        pltpu.VMEM((seq, hidden), F32),
        pltpu.VMEM((seq, hidden), BF16),
        pltpu.VMEM((seq, hw), F32),
        pltpu.VMEM((seq, hw), F32),
        pltpu.VMEM((seq + 2 * PAD, hw), F32),
        pltpu.VMEM((seq, hw), BF16),
        pltpu.VMEM((seq + 2 * PAD, hw), F32),
        pltpu.VMEM((2, seq, hw), BF16),
        pltpu.VMEM((seq, marked), BF16),
        pltpu.VMEM((marked, width), BF16),
        pltpu.VMEM((1, marked, width), F32),
        pltpu.VMEM((marked, hidden), F32),
        pltpu.VMEM((marked, hidden), BF16),
        pltpu.VMEM((2, marked, width), F32),
        pltpu.VMEM((chunk, width), F32),
        pltpu.VMEM((lay.sets, 2, part, width), BF16),
        pltpu.VMEM((lay.sets, 2, part, width), BF16),
        pltpu.VMEM((lay.sets, 2, part, width), BF16),
        pltpu.VMEM((lay.sets, 2, part, width), BF16),
        pltpu.VMEM((3, marked, width), BF16),
        pltpu.VMEM((3, marked, width), BF16),
        pltpu.VMEM((3, marked, width), BF16),
        pltpu.VMEM((3, marked, width), BF16),
        pltpu.VMEM((lay.rows, width), BF16),
        pltpu.VMEM((max(lay.rows - z_rows, 16), width), BF16),
        pltpu.VMEM((z_rows, width), BF16),
        pltpu.VMEM((z_rows, width), BF16),
        pltpu.VMEM((2, all_marked, width), BF16),
        pltpu.VMEM((2, width, hidden), F32),
        pltpu.VMEM((lay.misc_rows, width), F32),
        pltpu.VMEM((2 * hops + 4, lay.misc_rows, width), F32),
        pltpu.SemaphoreType.DMA((8,)),
        pltpu.SemaphoreType.DMA((len(lay.stores),)),
        pltpu.SemaphoreType.DMA((160,)),
        pltpu.SemaphoreType.DMA((160,)),
    ]
    smem_spec = pl.BlockSpec(memory_space=pltpu.SMEM)
    final, layer_rows, input_rows, misc = pl.pallas_call(
        functools.partial(main_kernel, lay),
        out_shape=(
            jax.ShapeDtypeStruct((lay.all_rows, width), BF16),
            jax.ShapeDtypeStruct((slot_count, part, width), BF16),
            jax.ShapeDtypeStruct((slot_count, part, width), BF16),
            jax.ShapeDtypeStruct((lay.misc_rows, width), F32),
        ),
        in_specs=[any_spec] * 7 + [vmem_spec] * 5 + [smem_spec] * 2,
        out_specs=(any_spec,) + (vmem_spec,) * 3,
        scratch_shapes=scratch,
        compiler_params=pltpu.CompilerParams(
            collective_id=0, has_side_effects=True, vmem_limit_bytes=63 * 2**20
        ),
        name="layers",
    )(
        inputs,
        jnp.swapaxes(attn_qkv, 1, 2),
        attn_out,
        jnp.swapaxes(conv_in, 1, 2),
        conv_out,
        ffn_up,
        ffn_down,
        norm_gain,
        norm_bias,
        conv_kernel,
        masked_positions,
        cotangent,
        kernel_half,
        batch_plan,
    )
    shapes = [
        (slot_count, part, width),
        (3, hw, width),
        (hw, width),
        (2, hw, width),
        (hw, width),
        (2, width, hidden),
        (2, hidden, width),
        (TAPS, hw),
        (4, width),
        (4, width),
        (dp, 8),
    ]
    widened = pl.pallas_call(
        functools.partial(widen_kernel, lay),
        out_shape=tuple(jax.ShapeDtypeStruct(shape, F32) for shape in shapes),
        in_specs=[any_spec] * 2 + [vmem_spec] + [smem_spec],
        out_specs=(any_spec,) * 7 + (vmem_spec,) * 4,
        scratch_shapes=[
            pltpu.VMEM((lay.all_rows, width), BF16),
            pltpu.VMEM((lay.all_rows, width), F32),
            pltpu.VMEM((slot_count, part, width), BF16),
            pltpu.VMEM((slot_count, part, width), F32),
            pltpu.SemaphoreType.DMA((32,)),
            pltpu.SemaphoreType.DMA((32,)),
        ],
        compiler_params=pltpu.CompilerParams(vmem_limit_bytes=48 * 2**20),
        name="widen",
    )(final, input_rows, misc, batch_plan)
    (input_grad, qkv, out, cin, cout, up, down, kernel, gains, biases, rms) = widened
    return (
        layer_rows,
        input_grad,
        jnp.swapaxes(qkv, 1, 2),
        out,
        jnp.swapaxes(cin, 1, 2),
        kernel,
        cout,
        up,
        down,
        gains,
        biases,
        rms,
    )


def solution(mesh):
    return jax.shard_map(
        on_device,
        mesh=mesh,
        in_specs=(
            P("dp", "mp", None),
            P(None, None, "mp"),
            P("mp", None),
            P(None, None, "mp"),
            P(None, "mp"),
            P("mp", None),
            P(None, None, "mp"),
            P(None, "mp", None),
            P(),
            P(),
            P(),
            P(),
            P("dp", None),
            P("dp", None, None),
        ),
        out_specs=(
            P("dp", "mp", None),
            P("dp", "mp", None),
            P(None, None, "mp"),
            P("mp", None),
            P(None, None, "mp"),
            P(None, "mp"),
            P("mp", None),
            P(None, None, "mp"),
            P(None, "mp", None),
            P(),
            P(),
            P(),
        ),
        check_vma=False,
    )
```

```python
import functools
import math

import jax
import jax.numpy as jnp
from jax import lax
from jax.experimental import pallas as pl
from jax.experimental.pallas import tpu as pltpu
from jax.sharding import PartitionSpec as P

HEAD = 64
TAPS = 7
MARGIN = TAPS // 2
EPSILON = 1e-05
SECTIONS = 4
GROUP = 4
PAD = 8
TILE = 32
SETS = (0, 1, 0, 1, 2, 2, 3)
LANES = 256

C_CUT, U_CUT, D_CUT, A_CUT = (2, 1, 2), (1, 1, 2, 2), (2, 2, 2), (2, 2, 1, 1)
TAIL = (
    "main", "fa", "lo", "lo", "c0", "fa", "main", "c0", "fa", "fa", "c2", "c1", "lo", "main", "c0",
    "c2", "pw", "pw", "pw", "c0", "c2", "c1", "lo", "main", "main", "ms", "main", "c0", "c2", "c1",
    "ms", "u1", "main", "u2", "c2", "ms", "u1", "lo", "main", "c1", "u3", "u0", "u2", "d0", "ms",
    "u1", "w1", "u3", "a0", "lo", "d1", "u0", "d2", "d0", "ms", "w1", "u2", "a0", "d1", "d2", "ms",
    "w1", "a1", "a3", "u3", "a3", "a2", "a0", "a3", "c1", "u0", "a2", "d0", "u2", "u1", "a1", "ig",
    "d1", "u3", "d2", "u0", "ms", "d0", "a0", "a3", "d1", "d2", "a2", "a1", "a2", "a0", "a3", "a1",
    "ig", "a2", "ig", "a1", "ig",
)

F32 = jnp.float32
BF16 = jnp.bfloat16
MESH = pl.DeviceIdType.MESH


def dot(left, right):
    return jnp.dot(left, right, preferred_element_type=F32)


def dot_lanes(left, right):
    return lax.dot_general(left, right, (((1,), (1,)), ((), ())), preferred_element_type=F32)


def dot_rows(left, right):
    return lax.dot_general(left, right, (((0,), (0,)), ((), ())), preferred_element_type=F32)


def round_up(value, step):
    return (value + step - 1) // step * step


def normalise(summed):
    centre = summed - jnp.mean(summed, axis=-1, keepdims=True)
    variance = jnp.mean(centre * centre, axis=-1, keepdims=True)
    inverse = lax.rsqrt(variance + EPSILON)
    return centre * inverse, inverse


def norm_pull(grad_out, normed, inverse, gain_row):
    scaled = grad_out * gain_row
    first = jnp.mean(scaled, axis=-1, keepdims=True)
    second = jnp.mean(scaled * normed, axis=-1, keepdims=True)
    return inverse * (scaled - first - normed * second)


def gelu_parts(before):
    cdf = 0.5 * (1.0 + lax.erf(before * math.sqrt(0.5)))
    slope = cdf + before * jnp.exp(-0.5 * before * before) * (1.0 / math.sqrt(2.0 * math.pi))
    return before * cdf, slope


def two_terms(values):
    high = values.astype(BF16)
    return high, (values - high.astype(F32)).astype(BF16)


def fold(rows):
    count, width = rows.shape
    return jnp.sum(rows.reshape(count // 8, 8, width), axis=0)


def whole_sum(values):
    return jnp.sum(values, axis=(0, 1), keepdims=True)


class Layout:
    def __init__(self, dp, micro, seq, width, heads_width, hidden, marked):
        self.dp, self.micro, self.seq, self.width = dp, micro, seq, width
        self.heads_width, self.hidden = heads_width, hidden
        self.marked = marked
        self.part = seq // GROUP
        self.chunk = 2 * self.part
        unit = 16 * dp
        conv_rows = round_up(3 * heads_width + 16, max(unit, 128))
        self.conv_at, at = 0, conv_rows
        self.up_at, at = at, at + width
        self.down_at, at = at, at + hidden
        self.attn_at, at = at, at + 4 * heads_width
        self.rows = at
        self.up1_at, at = at, at + width
        self.down1_at, at = at, at + hidden
        self.all_rows = at
        self.kernel_at = self.conv_at + 3 * heads_width
        half, step = width // 2, width // 6
        self.pieces, self.groups = {}, {}

        def cut(name, start, stride, sizes):
            at = start
            self.groups[name] = []
            for i, size in enumerate(sizes):
                size = step * size // 2
                key = name + str(i)
                self.pieces[key] = (at, stride or size, size, stride > 0)
                self.groups[name].append(key)
                at += size if stride else 2 * size

        cut("c", self.conv_at, 0, C_CUT)
        cut("u", self.up_at, half, U_CUT)
        cut("d", self.down_at, half, D_CUT)
        cut("a", self.attn_at, 0, A_CUT)
        self.xr_rows = self.z_rows = 0
        for _, _, size, paired in self.pieces.values():
            least = size // (dp // 2)
            assert least * (dp // 2) == size and least % 16 == 0
            self.xr_rows += size - least + (0 if paired else size)
            self.z_rows += least
        self.stores = [
            (self.conv_at, self.up_at),
            (self.up_at, width + hidden),
            (self.attn_at, 4 * heads_width),
            (self.up1_at, width + hidden),
        ]
        self.bits = dp.bit_length() - 1
        assert dp == 1 << self.bits and dp <= 8
        self.misc_rows = 16


def main_kernel(
    lay,
    x_in,
    qkv_in,
    ao_in,
    cin_in,
    co_in,
    up_in,
    down_in,
    gain,
    bias,
    taps_in,
    positions,
    cotangent,
    half_size,
    plan,
    final_out,
    layer_rows,
    input_rows,
    misc_out,
    final,
    tap_weight,
    tap_on,
    where,
    wqkv,
    wao,
    wcin,
    wco,
    wup,
    wdown,
    hid,
    dfull,
    normed,
    inverse,
    qkv,
    probs,
    mix,
    dmix,
    dqkv,
    dkv,
    units,
    slope,
    dbefore,
    last_units,
    value,
    sig,
    gated,
    conv,
    dconv,
    dgates,
    hits,
    mh,
    mnorm,
    mslope,
    munits,
    mdz,
    partial,
    cs,
    cr,
    ys,
    yr,
    ms,
    mr,
    mys,
    myr,
    grads,
    xr,
    za,
    zb,
    factors,
    pair,
    punits,
    pslope,
    pdbefore,
    misc,
    misc_in,
    load_sem,
    store_sem,
    send_sem,
    recv_sem,
):
    section, replica, member = (
        lax.axis_index("section"),
        lax.axis_index("dp"),
        lax.axis_index("mp"),
    )
    low = lax.rem(member, 2)
    high = lax.div(member, 2)
    part, chunk, width = lay.part, lay.chunk, lay.width
    hw, marked = lay.heads_width, lay.marked
    local_heads = hw // HEAD
    scale = HEAD ** (-0.5)
    side = (section, replica, member + 1 - 2 * low)
    across = (section, replica, lax.rem(member + 2, GROUP))
    is_end = (section == 0) | (section == SECTIONS - 1)
    is_inner = jnp.logical_not(is_end)
    inner_of = jnp.where(section == 0, 1, SECTIONS - 2)
    end_of = jnp.where(section == 1, 0, SECTIONS - 1)
    other_inner = SECTIONS - 1 - section
    counter = [0]
    closing = []
    leaving = {}

    def section_peer(by):
        return (lax.rem(section + by, SECTIONS), replica, member)

    def replica_peer(by):
        return (section, lax.rem(replica + by, lay.dp), member)

    def replica_bit(bit):
        on = lax.rem(lax.div(replica, 1 << bit), 2)
        return (section, replica + (1 - 2 * on) * (1 << bit), member), on

    def slots(count=1):
        at = counter[0]
        counter[0] += count
        return at

    def remote(src, dst, target, slot):
        return pltpu.make_async_remote_copy(
            src_ref=src,
            dst_ref=dst,
            send_sem=send_sem.at[slot],
            recv_sem=recv_sem.at[slot],
            device_id=target,
            device_id_type=MESH,
        )

    def send(src, dst, target, slot=None):
        copy = remote(src, dst, target, slots() if slot is None else slot)
        copy.start()
        closing.append(copy.wait_send)
        return copy

    def send_slot(name, ref, e, t, dst, target, slot=None):
        copy = remote(ref.at[SETS[e], t], dst.at[SETS[e], t], target, slots() if slot is None else slot)
        copy.start()
        leaving[name, SETS[e], t] = copy.wait_send
        return copy

    def reuse(name, e, t):
        wait = leaving.pop((name, SETS[e], t), None)
        if wait is not None:
            wait()

    barrier = pltpu.get_barrier_semaphore()
    peers = (
        [side, across]
        + [section_peer(by) for by in range(1, SECTIONS)]
        + [replica_peer(by) for by in range(1, lay.dp)]
    )
    for peer in peers:
        pl.semaphore_signal(barrier, inc=1, device_id=peer, device_id_type=MESH)

    loads = {}
    for at, (name, src, dst) in enumerate(
        [
            ("x", x_in.at[section], hid.at[0, pl.ds(pl.multiple_of(member * part, part), part)]),
            ("qkv", qkv_in, wqkv),
            ("ao", ao_in, wao),
            ("up", up_in, wup),
            ("down", down_in, wdown),
            ("cin", cin_in, wcin),
            ("co", co_in, wco),
        ]
    ):
        copy = pltpu.make_async_copy(src, dst, load_sem.at[at])
        copy.start()
        loads[name] = copy

    misc[...] = jnp.zeros_like(misc)
    holds = section < lay.micro
    for i in range(lay.micro):
        holds = holds | (plan[replica, i, 1] == section)
    used = jnp.where(holds, 1.0, 0.0).astype(F32)
    tap_row = lax.broadcasted_iota(jnp.int32, (TAPS, hw), 0)
    tap_mask = jnp.where(jnp.abs(tap_row - MARGIN) <= half_size[0], 1.0, 0.0)
    tap_on[...] = jnp.zeros_like(tap_on)
    tap_on[0:TAPS] = tap_mask
    tap_weight[0:TAPS] = taps_in[...].astype(F32) * tap_mask
    where[...] = jnp.full(where.shape, -1, jnp.int32)
    where[0:1, 0 : positions.shape[1]] = positions[pl.ds(section, 1)]
    lane = lax.broadcasted_iota(jnp.int32, (1, hw), 1)
    head_lanes = [(lane >= HEAD * i) & (lane < HEAD * (i + 1)) for i in range(local_heads)]
    head_low = [jnp.where(on, 1.0, 0.0).astype(BF16) for on in head_lanes]

    def block(at, size):
        return pl.ds(pl.multiple_of(at, size), size)

    def own_rows(t):
        return block(chunk * t + part * low, part)

    def other_rows(t):
        return block(chunk * t + part * (1 - low), part)

    def tiles(count, body, init=0):
        return lax.fori_loop(0, count, body, init)

    def exchange_send(e, t):
        reuse("cs", e, t)
        reuse("ys", e, t)
        at = SETS[e]

        def body(i, carry):
            rows = block(i * TILE, TILE)
            cs[at, t, rows] = partial[block(part * (1 - low) + i * TILE, TILE)].astype(BF16)
            return carry

        tiles(part // TILE, body)
        copy = send_slot("cs", cs, e, t, cr, side)

        def body(i, carry):
            rows = block(i * TILE, TILE)
            ys[at, t, rows] = partial[block(part * low + i * TILE, TILE)].astype(BF16)
            return carry

        tiles(part // TILE, body)
        return copy

    def sums_across(e, t, core_copy, start=True):
        core_copy.wait_recv()
        at = SETS[e]

        def body(i, carry):
            rows = block(i * TILE, TILE)
            ys[at, t, rows] = (ys[at, t, rows].astype(F32) + cr[at, t, rows].astype(F32)).astype(BF16)
            return carry

        tiles(part // TILE, body)
        if start:
            return send_slot("ys", ys, e, t, yr, across)

    def total_tile(e, t, rows):
        return ys[SETS[e], t, rows].astype(F32) + yr[SETS[e], t, rows].astype(F32)

    def send_half(e):
        slot = slots()
        at = SETS[e]
        out = remote(ys.at[at, 1 - high], yr.at[at, 1 - high], across, slot)
        out.start()
        leaving["ys", at, 0] = out.wait_send
        return remote(ys.at[at, high], yr.at[at, high], across, slot)

    def add_stat(column, amount):
        cell = (lax.broadcasted_iota(jnp.int32, (8, width), 0) == replica) & (
            lax.broadcasted_iota(jnp.int32, (8, width), 1) == column
        )
        misc[8:16] += jnp.where(cell, amount, 0.0)

    core_copies, y_copies, gathered = {}, {}, {}

    def begin(e, t, work):
        work(t)
        core_copies[e, t] = exchange_send(e, t)

    def cross(e, t):
        y_copies[e, t] = sums_across(e, t, core_copies[e, t])

    def end(e, t, finish):
        y_copies[e, t].wait_recv()
        gathered[e, t] = finish(t)

    pair_peer, pair_on = replica_bit(lay.bits - 1)
    pair_copies = {}
    halfway = lay.hidden // 2
    half_lanes = pl.ds(pl.multiple_of(pair_on * halfway, 128), halfway)

    def to_pair(which, t, src):
        rows = own_rows(t)
        pair_copies[which, t] = send(src.at[rows], pair.at[which, rows], pair_peer)

    def pass_on(which):
        for t in range(2):
            pair_copies[which, t].wait_recv()
            rows = own_rows(t)
            pair_copies[which, t] = send(pair.at[which, rows], pair.at[which, rows], side)

    def forward_finish(e, k, keep_normed):
        def finish(t):
            at = chunk * t + part * low

            def body(i, carry):
                rows = block(i * TILE, TILE)
                place = block(at + i * TILE, TILE)
                stream = hid[k, place].astype(F32)
                branch = total_tile(e, t, rows)
                norm, inv = normalise(stream + branch)
                if keep_normed:
                    normed[k, t, rows] = norm
                    inverse[k, t, rows] = inv
                hid[k + 1, place] = (norm * gain[k : k + 1] + bias[k : k + 1]).astype(BF16)
                return (carry[0] + fold(stream * stream), carry[1] + fold(branch * branch))

            zero = jnp.zeros((8, width), F32)
            squares = tiles(part // TILE, body, (zero, zero))

            @pl.when(high == t)
            def _():
                add_stat(k, whole_sum(squares[0]) * used)
                add_stat(4 + k, whole_sum(squares[1]) * used)

            rows = own_rows(t)
            copy = send(hid.at[k + 1, rows], hid.at[k + 1, rows], side)
            if k == 0:
                to_pair(0, t, hid.at[1])
            return copy

        return finish

    def norm_back_rows(k, t, grad_tile):
        at = chunk * t + part * low

        def body(i, carry):
            rows = block(i * TILE, TILE)
            dy = grad_tile(rows, block(at + i * TILE, TILE))
            norm = normed[k, t, rows]
            result = norm_pull(dy, norm, inverse[k, t, rows], gain[k : k + 1])
            normed[k, t, rows] = result
            dfull[k, block(at + i * TILE, TILE)] = result.astype(BF16)
            return (carry[0] + fold(dy * norm), carry[1] + fold(dy))

        zero = jnp.zeros((8, width), F32)
        terms = tiles(part // TILE, body, (zero, zero))

        @pl.when(high == t)
        def _():
            misc[k : k + 1] += jnp.sum(terms[0], axis=0, keepdims=True)
            misc[4 + k : 5 + k] += jnp.sum(terms[1], axis=0, keepdims=True)

        rows = own_rows(t)
        copy = send(dfull.at[k, rows], dfull.at[k, rows], side)
        if k == 1:
            to_pair(1, t, dfull.at[1])
        return copy

    def marked_total(e, values, during=None):
        ms[e] = values.astype(BF16)
        core = send(ms.at[e], mr.at[e], side)
        core.wait_recv()
        mys[e] = (ms[e].astype(F32) + mr[e].astype(F32)).astype(BF16)
        y = send(mys.at[e], myr.at[e], across)
        if during is not None:
            during()
        y.wait_recv()
        return mys[e].astype(F32) + myr[e].astype(F32)

    def reduce_piece(base, stride, size, paired):
        steps = []
        first, bit = base, lay.bits - 1
        while bit >= 0:
            peer, on = replica_bit(bit)
            keep = first + on * stride
            give = first + (1 - on) * stride
            if not paired:
                xr_at = reduce_piece.xr_at
                reduce_piece.xr_at += size
                copy = send(
                    grads.at[pl.ds(pl.multiple_of(give, 16), size)],
                    xr.at[pl.ds(xr_at, size)],
                    peer,
                )
                yield
                copy.wait_recv()
                step = math.gcd(size, 64)

                def body(i, carry, keep=keep, xr_at=xr_at, step=step):
                    here = pl.ds(pl.multiple_of(keep + i * step, 16), step)
                    there = pl.ds(pl.multiple_of(xr_at + i * step, 16), step)
                    grads[here] = (grads[here].astype(F32) + xr[there].astype(F32)).astype(BF16)
                    return carry

                tiles(size // step, body)
            steps.append((keep, give, size, peer))
            paired = False
            first, bit = keep, bit - 1
            if bit >= 0:
                size = size // 2
                stride = size
        z_at = reduce_piece.z_at
        reduce_piece.z_at += size
        mine = pl.ds(pl.multiple_of(first, 16), size)
        z_rows = pl.ds(z_at, size)
        step = math.gcd(size, 64)
        slot_a, slot_b, slot_c = slots(), slots(), slots()

        def z_copy(kind):
            if kind == "a":
                return remote(
                    grads.at[mine], za.at[z_rows], (inner_of, replica, member), slot_a
                )
            if kind == "b":
                return remote(
                    grads.at[mine], zb.at[z_rows], (other_inner, replica, member), slot_b
                )
            return remote(final.at[mine], final.at[mine], (end_of, replica, member), slot_c)

        steps.reverse()
        gather_slots = [slots() for _ in steps]

        def gather(at, arriving=False):
            keep, give, half, peer = steps[at]
            rows = pl.ds(pl.multiple_of(give if arriving else keep, 16), half)
            return remote(final.at[rows], final.at[rows], peer, gather_slots[at])

        @pl.when(is_end)
        def _():
            z_copy("a").start()

        yield

        @pl.when(is_inner)
        def _():
            z_copy("a").wait_recv()

            def body(i, carry):
                here = pl.ds(pl.multiple_of(first + i * step, 16), step)
                there = pl.ds(pl.multiple_of(z_at + i * step, 16), step)
                grads[here] = (grads[here].astype(F32) + za[there].astype(F32)).astype(BF16)
                return carry

            tiles(size // step, body)
            z_copy("b").start()

        yield

        @pl.when(is_inner)
        def _():
            z_copy("b").wait_recv()

            def body(i, carry):
                here = pl.ds(pl.multiple_of(first + i * step, 16), step)
                there = pl.ds(pl.multiple_of(z_at + i * step, 16), step)
                final[here] = (grads[here].astype(F32) + zb[there].astype(F32)).astype(BF16)
                return carry

            tiles(size // step, body)
            z_copy("c").start()
            gather(0).start()

        yield

        @pl.when(is_end)
        def _():
            z_copy("c").wait_recv()
            gather(0).start()

        yield
        for at in range(len(steps)):
            if at > 0:
                gather(at).start()
                yield
            gather(at, True).wait_recv()
            closing.append(gather(at).wait_send)

        def close():
            @pl.when(is_end)
            def _():
                z_copy("a").wait_send()

            @pl.when(is_inner)
            def _():
                z_copy("b").wait_send()
                z_copy("c").wait_send()

        closing.append(close)

    reduce_piece.xr_at = 0
    reduce_piece.z_at = 0
    running = {}
    summed = set()

    def launch(*names):
        for name in names:
            spec = lay.pieces.get(name)
            running[name] = reduce_piece(*spec)
            next(running[name])

    def start(name, task):
        running[name] = task
        next(task)

    def pump(*names):
        for name in names:
            if name in running:
                try:
                    next(running[name])
                except StopIteration:
                    del running[name]

    def line_gather(view):
        right, left = [slots() for _ in range(3)], [slots() for _ in range(3)]

        def hop(k, to_right, at):
            origin = at - k if to_right else at + k
            target = (section + (1 if to_right else -1), replica, member)
            return remote(view(origin), view(origin), target, (right if to_right else left)[k])

        def sends(k, action):
            @pl.when((section >= k) & (section < SECTIONS - 1))
            def _():
                getattr(hop(k, True, section), action)()

            @pl.when((section + k < SECTIONS) & (section > 0))
            def _():
                getattr(hop(k, False, section), action)()

        def arrivals(k):
            @pl.when(section > k)
            def _():
                hop(k, True, section - 1).wait_recv()

            @pl.when(section + k < SECTIONS - 1)
            def _():
                hop(k, False, section + 1).wait_recv()

        for k in range(SECTIONS - 1):
            sends(k, "start")
            closing.append(functools.partial(sends, k, "wait_send"))
            yield
            arrivals(k)

    def final_store(at):
        rows = pl.ds(*lay.stores[at])
        return pltpu.make_async_copy(final.at[rows], final_out.at[rows], store_sem.at[at])

    def store_final(at):
        final_store(at).start()

    pl.semaphore_wait(barrier, len(peers))
    loads["x"].wait()
    mine = block(member * part, part)
    to_side = send(hid.at[0, mine], hid.at[0, mine], side)
    to_across = send(hid.at[0, mine], hid.at[0, mine], across)
    hits[...] = jnp.where(
        lax.broadcasted_iota(jnp.int32, hits.shape, 0) == where[0:1, 0 : hits.shape[1]], 1.0, 0.0
    ).astype(BF16)
    loads["qkv"].wait()

    def project(at):
        rows = block(at, part)
        for j in range(3):
            qkv[j, rows] = dot_lanes(hid[0, rows], wqkv[j]).astype(BF16)

    project(member * part)
    to_side.wait_recv()
    project(side[2] * part)
    to_across.wait_recv()
    theirs = block(across[2] * part, part)
    onward = send(hid.at[0, theirs], hid.at[0, theirs], side)
    project(across[2] * part)
    onward.wait_recv()
    project(lax.rem(side[2] + 2, GROUP) * part)
    loads["ao"].wait()

    def attention_work(t):
        rows = pl.ds(chunk * t, chunk)
        mixture = jnp.zeros((chunk, hw), F32)
        for i in range(local_heads):
            if t == 1 and i == 1:
                cross(0, 0)
            scores = dot_lanes(qkv[0, rows] * head_low[i], qkv[1]) * scale
            top = jnp.max(scores, axis=-1, keepdims=True)
            powers = jnp.exp(scores - top)
            chances = powers * (1.0 / jnp.sum(powers, axis=-1, keepdims=True))
            probs[i, rows] = chances
            mixture = mixture + jnp.where(head_lanes[i], dot(chances.astype(BF16), qkv[2]), 0.0)
        mix[rows] = mixture.astype(BF16)
        partial[...] = dot(mix[rows], wao[...])

    begin(0, 0, attention_work)
    begin(0, 1, attention_work)
    cross(0, 1)
    loads["up"].wait()
    loads["down"].wait()

    def ffn_forward(layer, src, rows, units_here, slope_here=None):
        def body(i, carry):
            lanes = block(i * LANES, LANES)
            unit, steep = gelu_parts(dot(src[rows], wup[layer, :, lanes]))
            units_here[:, lanes] = unit.astype(BF16)
            if slope_here is not None:
                slope_here[:, lanes] = steep
            return carry

        tiles(lay.hidden // LANES, body)
        partial[...] = dot(units_here[...], wdown[layer])

    def ffn0_work(t):
        gathered[0, t].wait_recv()
        rows = pl.ds(chunk * t, chunk)
        ffn_forward(0, hid.at[1], rows, units.at[rows], slope.at[rows])

    attention_finish = forward_finish(0, 0, True)
    end(0, 0, attention_finish)
    begin(1, 0, ffn0_work)
    end(0, 1, attention_finish)
    cross(1, 0)
    begin(1, 1, ffn0_work)
    cross(1, 1)

    loads["cin"].wait()
    loads["co"].wait()
    edge = jnp.zeros((PAD, hw), F32)
    for buffer in (gated, dconv):
        buffer[0:PAD] = edge
        buffer[PAD + lay.seq : 2 * PAD + lay.seq] = edge

    def conv_gates(t):
        gathered[1, t].wait_recv()
        rows = pl.ds(chunk * t, chunk)
        value_here = dot_lanes(hid[2, rows], wcin[0])
        sig_here = jax.nn.sigmoid(dot_lanes(hid[2, rows], wcin[1]))
        value[rows] = value_here
        sig[rows] = sig_here
        gated[pl.ds(PAD + chunk * t, chunk)] = value_here * sig_here

    ffn0_finish = forward_finish(1, 1, True)
    pass_on(0)
    end(1, 0, ffn0_finish)
    conv_gates(0)
    end(1, 1, ffn0_finish)
    conv_gates(1)
    tap_tile = 64

    def taps(i, carry):
        total = jnp.zeros((tap_tile, hw), F32)
        window = gated[pl.ds(pl.multiple_of(i * tap_tile, 8), tap_tile + 2 * PAD)]
        for j in range(TAPS):
            at = PAD - MARGIN + j
            total = total + tap_weight[j : j + 1] * window[at : at + tap_tile]
        conv[block(i * tap_tile, tap_tile)] = total.astype(BF16)
        return carry

    tiles(lay.seq // tap_tile, taps)

    spots = hits[...]
    conv_marked = dot_rows(spots, conv[...]).astype(BF16)
    stream = dot_rows(spots, hid[2])

    def pair_up(t):
        pair_copies[0, t].wait_recv()
        rows = pl.ds(chunk * t, chunk)
        unit, slope_here = gelu_parts(dot(pair[0, rows], wup[0, :, half_lanes]))
        punits[rows] = unit.astype(BF16)
        pslope[rows] = slope_here


    def conv_work(t):
        partial[...] = dot(conv[pl.ds(chunk * t, chunk)], wco[...])

    def ffn1_work(t):
        gathered[5, t].wait_recv()
        ffn_forward(1, hid.at[3], pl.ds(chunk * t, chunk), last_units)

    def layer_output():
        last_finish = forward_finish(5, 2, False)
        begin(5, 0, conv_work)
        begin(5, 1, conv_work)
        cross(5, 0)
        yield
        cross(5, 1)
        yield
        end(5, 0, last_finish)
        yield
        end(5, 1, last_finish)
        yield
        begin(6, 0, ffn1_work)
        yield
        begin(6, 1, ffn1_work)
        for t in range(2):
            sums_across(6, t, core_copies[6, t], start=False)
        last = send_half(6)
        yield
        last.wait_recv()

        def layer_body(i, carry):
            rows = block(i * TILE, TILE)
            stream = hid[3, block(member * part + i * TILE, TILE)].astype(F32)
            branch = total_tile(6, high, rows)
            norm, _ = normalise(stream + branch)
            result = (norm * gain[3:4] + bias[3:4]) * used
            layer_rows[section, rows] = result.astype(BF16)
            return (carry[0] + fold(stream * stream), carry[1] + fold(branch * branch))

        zero = jnp.zeros((8, width), F32)
        squares = tiles(part // TILE, layer_body, (zero, zero))
        add_stat(3, whole_sum(squares[0]) * used)
        add_stat(7, whole_sum(squares[1]) * used)
        summed.add("rows")
        yield from line_gather(lambda at: layer_rows.at[at])

    branch = marked_total(
        0, dot(conv_marked, wco[...]), lambda: start("lo", layer_output())
    )
    norm2, inv2 = normalise(stream + branch)
    mnorm[0] = norm2
    mh[...] = (norm2 * gain[2:3] + bias[2:3]).astype(BF16)

    def marked_up(i, carry):
        lanes = block(i * LANES, LANES)
        unit, slope_here = gelu_parts(dot(mh[...], wup[1, :, lanes]))
        munits[:, lanes] = unit.astype(BF16)
        mslope[:, lanes] = slope_here
        return carry

    tiles(lay.hidden // LANES, marked_up)

    def beside_units():
        pump("lo")
        pair_up(0)

    branch = marked_total(1, dot(munits[...], wdown[1]), beside_units)
    norm3, inv3 = normalise(mh[...].astype(F32) + branch)
    once = jnp.where(member == 0, 1.0, 0.0).astype(F32)
    dy = cotangent[...].astype(F32) * used
    misc[3:4] += once * jnp.sum(dy * norm3, axis=0, keepdims=True)
    misc[7:8] += once * jnp.sum(dy, axis=0, keepdims=True)
    dz3 = norm_pull(dy, norm3, inv3, gain[3:4])
    mdz[0] = dz3
    df3 = dz3.astype(BF16)

    per_section = lay.dp * marked
    here = pl.ds(pl.multiple_of(section * per_section + replica * marked, 16), marked)
    factors[0, here] = mh[...]
    factors[1, here] = df3

    def spread_factors():
        copies = [
            send(factors.at[low, here], factors.at[low, here], replica_peer(by))
            for by in range(1, lay.dp)
        ]
        yield
        for copy in copies:
            copy.wait_recv()
        yield from line_gather(
            lambda at: factors.at[low, pl.ds(pl.multiple_of(at * per_section, 16), per_section)]
        )
        slot = slots()
        send(factors.at[low], factors.at[low], side, slot)
        yield
        remote(factors.at[1 - low], factors.at[1 - low], side, slot).wait_recv()

    start("fa", spread_factors())

    def marked_down(i, carry):
        lanes = block(i * LANES, LANES)
        grad_units = dot_lanes(factors[1, here], wdown[1, lanes])
        munits[:, lanes] = (grad_units * mslope[:, lanes]).astype(BF16)
        return carry

    tiles(lay.hidden // LANES, marked_down)
    def beside_down():
        pump("lo")
        pump("lo")
        pair_up(1)

    dy = mdz[0] + marked_total(2, dot_lanes(munits[...], wup[1]), beside_down)
    pump("fa")
    norm2 = mnorm[0]
    misc[2:3] += once * jnp.sum(dy * norm2, axis=0, keepdims=True)
    misc[6:7] += once * jnp.sum(dy, axis=0, keepdims=True)
    dz2 = norm_pull(dy, norm2, inv2, gain[2:3])
    dz2_terms = two_terms(dz2)
    df2 = dz2.astype(BF16)

    def spread(rows, terms):
        where_rows = hits[rows]
        return dot(where_rows, terms[0]) + dot(where_rows, terms[1])

    dconv_terms = two_terms(dot_lanes(df2, wco[...]))
    dconv[pl.ds(PAD, lay.seq)] = spread(pl.ds(0, lay.seq), dconv_terms)

    def taps_back(i, carry):
        total = jnp.zeros((tap_tile, hw), F32)
        place = pl.ds(pl.multiple_of(i * tap_tile, 8), tap_tile + 2 * PAD)
        window = dconv[place]
        around = gated[place]
        middle = window[PAD : PAD + tap_tile]
        sums = []
        for j in range(TAPS):
            at = PAD + MARGIN - j
            total = total + tap_weight[j : j + 1] * window[at : at + tap_tile]
            at = PAD - MARGIN + j
            sums.append(jnp.sum(around[at : at + tap_tile] * middle, axis=0, keepdims=True))
        rows = block(i * tap_tile, tap_tile)
        s = sig[rows]
        by_value = total * s
        dgates[0, rows] = by_value.astype(BF16)
        dgates[1, rows] = (by_value * value[rows] * (1.0 - s)).astype(BF16)
        sums.append(jnp.zeros((1, hw), F32))
        return carry + jnp.concatenate(sums, axis=0)

    kernel_rows = tiles(lay.seq // tap_tile, taps_back, jnp.zeros((8, hw), F32)) * tap_on[...]
    grads[pl.ds(lay.kernel_at, lay.up_at - lay.kernel_at)] = jnp.zeros(
        (lay.up_at - lay.kernel_at, width), BF16
    )
    grads[pl.ds(lay.kernel_at, 16), 0:hw] = jnp.concatenate(
        [kernel_rows, jnp.zeros((8, hw), F32)], axis=0
    ).astype(BF16)

    def conv_back_work(t):
        rows = pl.ds(chunk * t, chunk)
        partial[...] = dot(dgates[0, rows], wcin[0]) + dot(dgates[1, rows], wcin[1])

    def conv_back_finish(t):
        def grad_tile(rows, place):
            return total_tile(2, t, rows) + spread(place, dz2_terms)

        return norm_back_rows(1, t, grad_tile)

    def ffn0_back_work(t):
        gathered[2, t].wait_recv()
        rows = pl.ds(chunk * t, chunk)

        def body(i, carry):
            lanes = block(i * LANES, LANES)
            grad_units = dot_lanes(dfull[1, rows], wdown[0, lanes])
            dbefore[rows, lanes] = (grad_units * slope[rows, lanes]).astype(BF16)
            return carry

        tiles(lay.hidden // LANES, body)
        partial[...] = dot_lanes(dbefore[rows], wup[0])

    def ffn0_back_finish(t):
        return norm_back_rows(
            0, t, lambda rows, place: normed[1, t, rows] + total_tile(3, t, rows)
        )

    up_rows = pl.ds(pl.multiple_of(lay.up_at + pair_on * halfway, 16), halfway)
    down_rows = pl.ds(pl.multiple_of(lay.down_at + pair_on * halfway, 16), halfway)

    def own_weights():
        left = dbefore[:, half_lanes]
        for q in range(2):
            lanes = pl.ds(q * halfway, halfway)
            grads[up_rows, lanes] = dot_rows(hid[1, :, lanes], left).astype(BF16)
        grads[down_rows] = dot_rows(units[:, half_lanes], dfull[1]).astype(BF16)

    def pair_weights():
        for t in range(2):
            pair_copies[1, t].wait_recv()
            rows = pl.ds(chunk * t, chunk)
            grad_units = dot_lanes(pair[1, rows], wdown[0, half_lanes])
            pdbefore[rows] = (grad_units * pslope[rows]).astype(BF16)
        left = pdbefore[...]
        for q in range(2):
            lanes = pl.ds(q * halfway, halfway)
            total = grads[up_rows, lanes].astype(F32) + dot_rows(pair[0, :, lanes], left)
            grads[up_rows, lanes] = total.astype(BF16)
        launch(*lay.groups["u"])
        total = grads[down_rows].astype(F32) + dot_rows(punits[...], pair[1])
        grads[down_rows] = total.astype(BF16)
        launch(*lay.groups["d"])

    def attention_back_work(t):
        rows = pl.ds(chunk * t, chunk)
        partial[...] = (
            dot(dqkv[0, rows], wqkv[0])
            + dot(dqkv[1, rows], wqkv[1])
            + dot(dqkv[2, rows], wqkv[2])
        )

    def attention_back_rows(t):
        gathered[3, t].wait_recv()
        rows = pl.ds(chunk * t, chunk)
        dmix[rows] = dot_lanes(dfull[0, rows], wao[...]).astype(BF16)
        grad_queries = jnp.zeros((chunk, hw), F32)
        for i in range(local_heads):
            chances = probs[i, rows]
            grad_chances = dot_lanes(dmix[rows] * head_low[i], qkv[2])
            grad_scores = chances * (
                grad_chances - jnp.sum(grad_chances * chances, axis=-1, keepdims=True)
            )
            grad_scores = grad_scores.astype(BF16)
            on = head_lanes[i]
            grad_queries = grad_queries + jnp.where(on, dot(grad_scores, qkv[1]), 0.0)
            dkv[0] += jnp.where(on, dot_rows(grad_scores, qkv[0, rows]), 0.0)
            dkv[1] += jnp.where(on, dot_rows(chances.astype(BF16), dmix[rows]), 0.0)
        dqkv[0, rows] = (grad_queries * scale).astype(BF16)

    waits = {}

    def backward():
        begin(2, 0, conv_back_work)
        begin(2, 1, conv_back_work)
        cross(2, 0)
        cross(2, 1)
        for j in range(2):
            grads[pl.ds(lay.conv_at + j * hw, hw)] = dot_rows(dgates[j], hid[2]).astype(BF16)
        grads[pl.ds(lay.conv_at + 2 * hw, hw)] = dot_rows(conv_marked, df2).astype(BF16)
        launch(*lay.groups["c"])
        yield
        end(2, 0, conv_back_finish)
        begin(3, 0, ffn0_back_work)
        yield
        end(2, 1, conv_back_finish)
        cross(3, 0)
        begin(3, 1, ffn0_back_work)
        cross(3, 1)
        yield
        end(3, 0, ffn0_back_finish)
        yield
        end(3, 1, ffn0_back_finish)
        summed.add("norms")
        yield
        dkv[...] = jnp.zeros_like(dkv)
        attention_back_rows(0)
        yield
        attention_back_rows(1)
        dqkv[1] = (dkv[0] * scale).astype(BF16)
        dqkv[2] = dkv[1].astype(BF16)
        for t in range(2):
            begin(4, t, attention_back_work)
        for t in range(2):
            sums_across(4, t, core_copies[4, t], start=False)
        waits["input"] = send_half(4)
        yield
        for j in range(3):
            grads[pl.ds(lay.attn_at + j * hw, hw)] = dot_rows(dqkv[j], hid[0]).astype(BF16)
        grads[pl.ds(lay.attn_at + 3 * hw, hw)] = dot_rows(mix[...], dfull[0]).astype(BF16)
        launch(*lay.groups["a"])

    def feed_forward_weights():
        own_weights()
        yield
        pass_on(1)
        yield
        pair_weights()

    def input_body(i, carry):
        rows = block(i * TILE, TILE)
        total = total_tile(4, high, rows)
        input_rows[section, rows] = (normed[0, high, rows] + total).astype(BF16)
        return carry

    def input_gradient():
        waits["input"].wait_recv()
        tiles(part // TILE, input_body)
        yield from line_gather(lambda at: input_rows.at[at])

    group_rows = GROUP * marked
    groups = SECTIONS * per_section // group_rows

    def last_block():
        assert not {"main", "pw", "fa"} & set(running)
        for group in range(groups):
            rows = pl.ds(group * group_rows, group_rows)

            def recompute(j, carry, rows=rows):
                lanes = block(j * LANES, LANES)
                unit, slope_here = gelu_parts(dot(factors[0, rows], wup[1, :, lanes]))
                units[0:group_rows, lanes] = unit.astype(BF16)
                grad_units = dot_lanes(factors[1, rows], wdown[1, lanes])
                dbefore[0:group_rows, lanes] = (grad_units * slope_here).astype(BF16)
                return carry

            tiles(lay.hidden // LANES, recompute)

            def last_weights(i, carry, rows=rows, group=group):
                lanes = block(i * LANES, LANES)
                by_up = dot_rows(factors[0, rows, lanes], dbefore[0:group_rows])
                by_down = dot_rows(units[0:group_rows, lanes], factors[1, rows])
                wide, rest = probs.shape[2], width - probs.shape[2]
                held = [
                    (
                        probs.at[i, pl.ds(j * LANES, LANES)],
                        slope.at[pl.ds(j * LANES, LANES), block(i * rest, rest)],
                    )
                    for j in range(2)
                ]
                if group > 0:
                    by_up = by_up + jnp.concatenate([held[0][0][...], held[0][1][...]], axis=1)
                    by_down = by_down + jnp.concatenate([held[1][0][...], held[1][1][...]], axis=1)
                if group < groups - 1:
                    for (left, right), total in zip(held, (by_up, by_down)):
                        left[...] = total[:, :wide]
                        right[...] = total[:, wide:]
                else:
                    at = pl.multiple_of(i * LANES, LANES)
                    final[pl.ds(lay.up1_at + at, LANES)] = by_up.astype(BF16)
                    final[pl.ds(lay.down1_at + at, LANES)] = by_down.astype(BF16)
                return carry

            tiles(width // LANES, last_weights)
            yield
        store_final(3)

    def small_sums():
        assert summed >= {"norms", "rows"}
        hops = [side, across] + [replica_bit(bit)[0] for bit in range(lay.bits)]
        for at, peer in enumerate(hops):
            misc_in[2 * at] = misc[...]
            copy = send(misc_in.at[2 * at], misc_in.at[2 * at + 1], peer)
            yield
            copy.wait_recv()
            misc[...] = misc_in[2 * at] + misc_in[2 * at + 1]
        at = 2 * len(hops)
        slot_a, slot_b, slot_c = slots(), slots(), slots()
        to_inner = remote(misc_in.at[at], misc_in.at[at + 1], (inner_of, replica, member), slot_a)
        to_other = remote(
            misc_in.at[at + 2], misc_in.at[at + 3], (other_inner, replica, member), slot_b
        )
        to_end = remote(misc_out, misc_out, (end_of, replica, member), slot_c)

        @pl.when(is_end)
        def _():
            misc_in[at] = misc[...]
            to_inner.start()

        yield

        @pl.when(is_inner)
        def _():
            to_inner.wait_recv()
            misc_in[at + 2] = misc[...] + misc_in[at + 1]
            to_other.start()

        yield

        @pl.when(is_inner)
        def _():
            to_other.wait_recv()
            misc_out[...] = misc_in[at + 2] + misc_in[at + 3]
            to_end.start()

        yield

        @pl.when(is_end)
        def _():
            to_end.wait_recv()
            to_inner.wait_send()

        @pl.when(is_inner)
        def _():
            to_other.wait_send()
            to_end.wait_send()

    later = {
        "main": backward,
        "pw": feed_forward_weights,
        "ig": input_gradient,
        "w1": last_block,
        "ms": small_sums,
    }
    for name in TAIL:
        if name in later:
            start(name, later.pop(name)())
        elif name.startswith("s"):
            store_final(int(name[1]))
        else:
            pump(name)
    assert not later
    while running:
        pump(*list(running))
    for at in range(3):
        store_final(at)
    for at in range(len(lay.stores)):
        final_store(at).wait()
    for wait in closing + list(leaving.values()):
        wait()


def widen_kernel(
    lay,
    final,
    input_rows,
    misc,
    plan,
    input_grad,
    qkv,
    out,
    cin,
    cout,
    up,
    down,
    kernel,
    gains,
    biases,
    rms,
    narrow,
    wide,
    narrow_input,
    wide_input,
    load_sem,
    store_sem,
):
    hw, width, hidden = lay.heads_width, lay.width, lay.hidden
    blocks = []

    def cover(start, rows, target, step):
        for at in range(0, rows, step):
            blocks.append((start + at, step, target.at[pl.ds(at, step)]))

    for layer, (up_at, down_at) in enumerate(
        ((lay.up_at, lay.down_at), (lay.up1_at, lay.down1_at))
    ):
        cover(up_at, width, up.at[layer], width // 2)
        cover(down_at, hidden, down.at[layer], hidden // 2)
    for j in range(3):
        cover(lay.attn_at + j * hw, hw, qkv.at[j], hw)
    cover(lay.attn_at + 3 * hw, hw, out, hw)
    for j in range(2):
        cover(lay.conv_at + j * hw, hw, cin.at[j], hw)
    cover(lay.conv_at + 2 * hw, hw, cout, hw)

    def load(at):
        start, rows, _ = blocks[at]
        here = pl.ds(start, rows)
        return pltpu.make_async_copy(final.at[here], narrow.at[here], load_sem.at[at])

    def store(at):
        start, rows, target = blocks[at]
        return pltpu.make_async_copy(wide.at[pl.ds(start, rows)], target, store_sem.at[at])

    extra = len(blocks)
    tap_rows = pltpu.make_async_copy(
        final.at[pl.ds(lay.kernel_at, 16)], narrow.at[pl.ds(lay.kernel_at, 16)], load_sem.at[extra]
    )
    inputs_in = pltpu.make_async_copy(input_rows, narrow_input, load_sem.at[extra + 1])
    inputs_out = pltpu.make_async_copy(wide_input, input_grad, store_sem.at[extra])
    for at in range(len(blocks)):
        load(at).start()
    inputs_in.start()
    tap_rows.start()
    gains[...] = misc[0:4]
    biases[...] = misc[4:8]
    row = lax.broadcasted_iota(jnp.int32, rms.shape, 0)
    counts = jnp.zeros(rms.shape, F32)
    for r in range(rms.shape[0]):
        total = jnp.float32(lay.micro)
        for i in range(lay.micro):
            total = total + jnp.where(plan[r, i, 1] >= 0, 1.0, 0.0).astype(F32)
        counts = jnp.where(row == r, total, counts)
    rms[...] = jnp.sqrt(misc[8 : 8 + rms.shape[0], 0:8] / (counts * (lay.seq * width)))
    half = width // 2
    for at in range(2):
        load(at).wait()
    for at, (start, rows, _) in enumerate(blocks):
        if at >= 2:
            load(at).wait()

        def body(i, carry, start=start, at=at):
            here = pl.ds(pl.multiple_of(start + i * 32, 16), 32)
            if at >= 2:
                wide[here] = narrow[here].astype(F32)
            else:
                for q in range(2):
                    there = pl.ds(pl.multiple_of(lay.up_at + q * half + i * 32, 16), 32)
                    wide[here, q * half : (q + 1) * half] = narrow[
                        there, at * half : (at + 1) * half
                    ].astype(F32)
            return carry

        lax.fori_loop(0, rows // 32, body, 0)
        store(at).start()
    inputs_in.wait()
    for slot in range(input_rows.shape[0]):
        wide_input[slot] = narrow_input[slot].astype(F32)
    inputs_out.start()
    tap_rows.wait()
    taps = narrow[pl.ds(lay.kernel_at, 16)].astype(F32)
    kernel[...] = taps[0:TAPS, 0:hw]
    for at in range(len(blocks)):
        store(at).wait()
    inputs_out.wait()


def on_device(
    inputs,
    attn_qkv,
    attn_out,
    conv_in,
    conv_kernel,
    conv_out,
    ffn_up,
    ffn_down,
    norm_gain,
    norm_bias,
    kernel_half,
    batch_plan,
    masked_positions,
    out_grad,
):
    section = lax.axis_index("section")
    replica = lax.axis_index("dp")
    dp = lax.axis_size("dp")
    slot_count, part, width = inputs.shape
    micro_count = batch_plan.shape[1]
    count = masked_positions.shape[1]
    marked = round_up(count, 16)
    assert slot_count == SECTIONS == lax.axis_size("section") and lax.axis_size("mp") == GROUP
    hw = attn_out.shape[0]
    hidden = ffn_up.shape[2]
    lay = Layout(dp, micro_count, part * GROUP, width, hw, hidden, marked)
    assert hidden == width and width % LANES == 0 and hw % HEAD == 0

    cotangent = lax.dynamic_index_in_dim(out_grad, section, 0, keepdims=False)
    cotangent = jnp.pad(cotangent, ((0, marked - count), (0, 0)))

    seq, chunk = lay.seq, lay.chunk
    any_spec = pl.BlockSpec(memory_space=pl.ANY)
    vmem_spec = pl.BlockSpec(memory_space=pltpu.VMEM)
    hops = 2 + lay.bits
    all_marked = SECTIONS * dp * marked
    scratch = [
        pltpu.VMEM((lay.all_rows, width), BF16),
        pltpu.VMEM((8, hw), F32),
        pltpu.VMEM((8, hw), F32),
        pltpu.VMEM((8, marked), jnp.int32),
        pltpu.VMEM((3, hw, width), BF16),
        pltpu.VMEM(attn_out.shape, BF16),
        pltpu.VMEM((2, hw, width), BF16),
        pltpu.VMEM(conv_out.shape, BF16),
        pltpu.VMEM(ffn_up.shape, BF16),
        pltpu.VMEM(ffn_down.shape, BF16),
        pltpu.VMEM((4, seq, width), BF16),
        pltpu.VMEM((2, seq, width), BF16),
        pltpu.VMEM((2, 2, part, width), F32),
        pltpu.VMEM((2, 2, part, 1), F32),
        pltpu.VMEM((3, seq, hw), BF16),
        pltpu.VMEM((hw // HEAD, seq, seq), F32),
        pltpu.VMEM((seq, hw), BF16),
        pltpu.VMEM((seq, hw), BF16),
        pltpu.VMEM((3, seq, hw), BF16),
        pltpu.VMEM((2, seq, hw), F32),
        pltpu.VMEM((seq, hidden), BF16),
        pltpu.VMEM((seq, hidden), F32),
        pltpu.VMEM((seq, hidden), BF16),
        pltpu.VMEM((chunk, hidden), BF16),
        pltpu.VMEM((seq, hw), F32),
        pltpu.VMEM((seq, hw), F32),
        pltpu.VMEM((seq + 2 * PAD, hw), F32),
        pltpu.VMEM((seq, hw), BF16),
        pltpu.VMEM((seq + 2 * PAD, hw), F32),
        pltpu.VMEM((2, seq, hw), BF16),
        pltpu.VMEM((seq, marked), BF16),
        pltpu.VMEM((marked, width), BF16),
        pltpu.VMEM((1, marked, width), F32),
        pltpu.VMEM((marked, hidden), F32),
        pltpu.VMEM((marked, hidden), BF16),
        pltpu.VMEM((1, marked, width), F32),
        pltpu.VMEM((chunk, width), F32),
        pltpu.VMEM((4, 2, part, width), BF16),
        pltpu.VMEM((4, 2, part, width), BF16),
        pltpu.VMEM((4, 2, part, width), BF16),
        pltpu.VMEM((4, 2, part, width), BF16),
        pltpu.VMEM((3, marked, width), BF16),
        pltpu.VMEM((3, marked, width), BF16),
        pltpu.VMEM((3, marked, width), BF16),
        pltpu.VMEM((3, marked, width), BF16),
        pltpu.VMEM((lay.rows, width), BF16),
        pltpu.VMEM((lay.xr_rows, width), BF16),
        pltpu.VMEM((lay.z_rows, width), BF16),
        pltpu.VMEM((lay.z_rows, width), BF16),
        pltpu.VMEM((2, all_marked, width), BF16),
        pltpu.VMEM((2, seq, width), BF16),
        pltpu.VMEM((seq, hidden // 2), BF16),
        pltpu.VMEM((seq, hidden // 2), F32),
        pltpu.VMEM((seq, hidden // 2), BF16),
        pltpu.VMEM((lay.misc_rows, width), F32),
        pltpu.VMEM((2 * hops + 4, lay.misc_rows, width), F32),
        pltpu.SemaphoreType.DMA((8,)),
        pltpu.SemaphoreType.DMA((len(lay.stores),)),
        pltpu.SemaphoreType.DMA((160,)),
        pltpu.SemaphoreType.DMA((160,)),
    ]
    smem_spec = pl.BlockSpec(memory_space=pltpu.SMEM)
    final, layer_rows, input_rows, misc = pl.pallas_call(
        functools.partial(main_kernel, lay),
        out_shape=(
            jax.ShapeDtypeStruct((lay.all_rows, width), BF16),
            jax.ShapeDtypeStruct((slot_count, part, width), BF16),
            jax.ShapeDtypeStruct((slot_count, part, width), BF16),
            jax.ShapeDtypeStruct((lay.misc_rows, width), F32),
        ),
        in_specs=[any_spec] * 7 + [vmem_spec] * 5 + [smem_spec] * 2,
        out_specs=(any_spec,) + (vmem_spec,) * 3,
        scratch_shapes=scratch,
        compiler_params=pltpu.CompilerParams(
            collective_id=0, has_side_effects=True, vmem_limit_bytes=63 * 2**20
        ),
        name="layers",
    )(
        inputs,
        jnp.swapaxes(attn_qkv, 1, 2),
        attn_out,
        jnp.swapaxes(conv_in, 1, 2),
        conv_out,
        ffn_up,
        ffn_down,
        norm_gain,
        norm_bias,
        conv_kernel,
        masked_positions,
        cotangent,
        kernel_half,
        batch_plan,
    )
    shapes = [
        (slot_count, part, width),
        (3, hw, width),
        (hw, width),
        (2, hw, width),
        (hw, width),
        (2, width, hidden),
        (2, hidden, width),
        (TAPS, hw),
        (4, width),
        (4, width),
        (dp, 8),
    ]
    widened = pl.pallas_call(
        functools.partial(widen_kernel, lay),
        out_shape=tuple(jax.ShapeDtypeStruct(shape, F32) for shape in shapes),
        in_specs=[any_spec] * 2 + [vmem_spec] + [smem_spec],
        out_specs=(any_spec,) * 7 + (vmem_spec,) * 4,
        scratch_shapes=[
            pltpu.VMEM((lay.all_rows, width), BF16),
            pltpu.VMEM((lay.all_rows, width), F32),
            pltpu.VMEM((slot_count, part, width), BF16),
            pltpu.VMEM((slot_count, part, width), F32),
            pltpu.SemaphoreType.DMA((32,)),
            pltpu.SemaphoreType.DMA((32,)),
        ],
        compiler_params=pltpu.CompilerParams(vmem_limit_bytes=48 * 2**20),
        name="widen",
    )(final, input_rows, misc, batch_plan)
    (input_grad, qkv, out, cin, cout, up, down, kernel, gains, biases, rms) = widened
    return (
        layer_rows,
        input_grad,
        jnp.swapaxes(qkv, 1, 2),
        out,
        jnp.swapaxes(cin, 1, 2),
        kernel,
        cout,
        up,
        down,
        gains,
        biases,
        rms,
    )


def solution(mesh):
    return jax.shard_map(
        on_device,
        mesh=mesh,
        in_specs=(
            P("dp", "mp", None),
            P(None, None, "mp"),
            P("mp", None),
            P(None, None, "mp"),
            P(None, "mp"),
            P("mp", None),
            P(None, None, "mp"),
            P(None, "mp", None),
            P(),
            P(),
            P(),
            P(),
            P("dp", None),
            P("dp", None, None),
        ),
        out_specs=(
            P("dp", "mp", None),
            P("dp", "mp", None),
            P(None, None, "mp"),
            P("mp", None),
            P(None, None, "mp"),
            P(None, "mp"),
            P("mp", None),
            P(None, None, "mp"),
            P(None, "mp", None),
            P(),
            P(),
            P(),
        ),
        check_vma=False,
    )
```

```python
import functools
import math

import jax
import jax.numpy as jnp
from jax import lax
from jax.experimental import pallas as pl
from jax.experimental.pallas import tpu as pltpu
from jax.sharding import PartitionSpec as P

HEAD = 64
TAPS = 7
MARGIN = TAPS // 2
EPSILON = 1e-05
SECTIONS = 4
GROUP = 4
PAD = 8
TILE = 32
VMEM_BYTES = 55 * 2**20 + 2**17
SETS = (0, 1, 0, 1, 2, 2, 3)
LANES = 256

KEEP = 12
C_CUT, U_CUT, D_CUT, A_CUT = (2, 1, 2), (1, 1, 2, 2), (2, 2, 2), (2, 2, 1, 1)
TAIL = (
    "main", "fa", "lo", "lo", "c0", "fa", "main", "c1", "lo", "c0", "main", "fa", "fa", "c1", "lo",
    "c2", "pw", "main", "c0", "pw", "pw", "c1", "c2", "main", "ms", "u0", "main", "u1", "lo", "ms",
    "c0", "main", "u2", "c1", "ms", "u0", "c2", "u1", "u3", "u2", "d0", "main", "d1", "u3", "c0",
    "lo", "d0", "d2", "d1", "ig", "c1", "a0", "ms", "u0", "c2", "a0", "d2", "ms", "u1", "a1", "a2",
    "u2", "a3", "a1", "a2", "a0", "a3", "ms", "w1", "u3", "a1", "a2", "a3", "u0", "w1", "d0", "u1",
    "d1", "u2", "c2", "ig", "u3", "w1", "d2", "d0", "a0", "d1", "ms", "a1", "a2", "a3", "d2", "a0",
    "ig", "ig", "a1", "a2", "a3",
)

F32 = jnp.float32
BF16 = jnp.bfloat16
MESH = pl.DeviceIdType.MESH


def dot(left, right):
    return jnp.dot(left, right, preferred_element_type=F32)


def dot_lanes(left, right):
    return lax.dot_general(left, right, (((1,), (1,)), ((), ())), preferred_element_type=F32)


def dot_rows(left, right):
    return lax.dot_general(left, right, (((0,), (0,)), ((), ())), preferred_element_type=F32)


def round_up(value, step):
    return (value + step - 1) // step * step


def normalise(summed):
    centre = summed - jnp.mean(summed, axis=-1, keepdims=True)
    variance = jnp.mean(centre * centre, axis=-1, keepdims=True)
    inverse = lax.rsqrt(variance + EPSILON)
    return centre * inverse, inverse


def norm_pull(grad_out, normed, inverse, gain_row):
    scaled = grad_out * gain_row
    first = jnp.mean(scaled, axis=-1, keepdims=True)
    second = jnp.mean(scaled * normed, axis=-1, keepdims=True)
    return inverse * (scaled - first - normed * second)


def gelu_parts(before):
    cdf = 0.5 * (1.0 + lax.erf(before * math.sqrt(0.5)))
    slope = cdf + before * jnp.exp(-0.5 * before * before) * (1.0 / math.sqrt(2.0 * math.pi))
    return before * cdf, slope


def two_terms(values):
    high = values.astype(BF16)
    return high, (values - high.astype(F32)).astype(BF16)


def fold(rows):
    count, width = rows.shape
    return jnp.sum(rows.reshape(count // 8, 8, width), axis=0)


def whole_sum(values):
    return jnp.sum(values, axis=(0, 1), keepdims=True)


class Layout:
    def __init__(self, dp, micro, seq, width, heads_width, hidden, marked):
        self.dp, self.micro, self.seq, self.width = dp, micro, seq, width
        self.heads_width, self.hidden = heads_width, hidden
        self.marked = marked
        self.part = seq // GROUP
        self.chunk = 2 * self.part
        unit = 16 * dp
        conv_rows = round_up(3 * heads_width + 16, max(unit, 128))
        self.conv_at, at = 0, conv_rows
        self.up_at, at = at, at + width
        self.down_at, at = at, at + hidden
        self.attn_at, at = at, at + 4 * heads_width
        self.rows = at
        self.up1_at, at = at, at + width
        self.down1_at, at = at, at + hidden
        self.all_rows = at
        self.kernel_at = self.conv_at + 3 * heads_width
        half, step = width // 2, width // 6
        self.pieces, self.groups = {}, {}

        def cut(name, start, stride, sizes):
            at = start
            self.groups[name] = []
            for i, size in enumerate(sizes):
                size = step * size // 2
                key = name + str(i)
                self.pieces[key] = (at, stride or size, size, stride > 0)
                self.groups[name].append(key)
                at += size if stride else 2 * size

        cut("c", self.conv_at, 0, C_CUT)
        cut("u", self.up_at, half, U_CUT)
        cut("d", self.down_at, half, D_CUT)
        cut("a", self.attn_at, 0, A_CUT)
        self.xr_rows = self.z_rows = 0
        for _, _, size, paired in self.pieces.values():
            least = size // (dp // 2)
            assert least * (dp // 2) == size and least % 16 == 0
            self.xr_rows += size - least + (0 if paired else size)
            self.z_rows += least
        self.bits = dp.bit_length() - 1
        assert dp == 1 << self.bits and dp <= 8
        self.misc_rows = 16
        self.arrivals = 127 + (2 * len(self.pieces) + 1) * (self.bits - 1) + dp - 2
        self.departures = self.arrivals * 4 // 7


def main_kernel(
    lay,
    x_in,
    qkv_in,
    ao_in,
    cin_in,
    co_in,
    up_in,
    down_in,
    gain_in,
    bias_in,
    taps_in,
    positions,
    out_grads_in,
    half_size,
    plan,
    final,
    layer_rows,
    input_rows,
    misc_out,
    tap_weight,
    tap_on,
    where,
    gain,
    bias,
    cotangent,
    out_grads,
    wqkv,
    wao,
    wcin,
    wco,
    wup,
    wdown,
    hid,
    dfull,
    normed,
    inverse,
    qkv,
    probs,
    mix,
    dmix,
    dqkv,
    dkv,
    units,
    slope,
    dbefore,
    last_units,
    value,
    sig,
    gated,
    conv,
    dconv,
    dgates,
    hits,
    mh,
    mnorm,
    mslope,
    munits,
    partial,
    cs,
    cr,
    ys,
    yr,
    ms,
    mr,
    mys,
    myr,
    grads,
    xr,
    za,
    zb,
    factors,
    pair,
    punits,
    pslope,
    pdbefore,
    misc,
    misc_in,
    load_sem,
    send_sem,
    recv_sem,
):
    section, replica, member = (
        lax.axis_index("section"),
        lax.axis_index("dp"),
        lax.axis_index("mp"),
    )
    low = lax.rem(member, 2)
    high = lax.div(member, 2)
    part, chunk, width = lay.part, lay.chunk, lay.width
    hw, marked = lay.heads_width, lay.marked
    local_heads = hw // HEAD
    scale = HEAD ** (-0.5)
    side = (section, replica, member + 1 - 2 * low)
    across = (section, replica, lax.rem(member + 2, GROUP))
    is_end = (section == 0) | (section == SECTIONS - 1)
    is_inner = jnp.logical_not(is_end)
    inner_of = jnp.where(section == 0, 1, SECTIONS - 2)
    end_of = jnp.where(section == 1, 0, SECTIONS - 1)
    other_inner = SECTIONS - 1 - section
    counter = [0, 0]
    closing = []
    leaving = {}

    def section_peer(by):
        return (lax.rem(section + by, SECTIONS), replica, member)

    def replica_peer(by):
        return (section, lax.rem(replica + by, lay.dp), member)

    def replica_bit(bit):
        on = lax.rem(lax.div(replica, 1 << bit), 2)
        return (section, replica + (1 - 2 * on) * (1 << bit), member), on

    free, departures = [], {}

    def slots():
        at = counter[0]
        counter[0] += 1
        if not free:
            free.append(counter[1])
            counter[1] += 1
        departures[at] = free.pop()
        return at

    def settle(keep=0):
        while len(closing) > keep:
            wait, done = closing.pop(0)
            wait()
            free.extend(departures[slot] for slot in done)

    def remote(src, dst, target, slot):
        return pltpu.make_async_remote_copy(
            src_ref=src,
            dst_ref=dst,
            send_sem=send_sem.at[departures[slot]],
            recv_sem=recv_sem.at[slot],
            device_id=target,
            device_id_type=MESH,
        )

    def send(src, dst, target, slot=None):
        slot = slots() if slot is None else slot
        copy = remote(src, dst, target, slot)
        copy.start()
        closing.append((copy.wait_send, (slot,)))
        return copy

    def send_slot(name, ref, e, t, dst, target):
        slot = slots()
        copy = remote(ref.at[SETS[e], t], dst.at[SETS[e], t], target, slot)
        copy.start()
        leaving[name, SETS[e], t] = copy.wait_send, (slot,)
        return copy

    def reuse(name, e, t):
        entry = leaving.pop((name, SETS[e], t), None)
        if entry is not None:
            closing.insert(0, entry)
            settle(len(closing) - 1)

    barrier = pltpu.get_barrier_semaphore()
    peers = (
        [side, across]
        + [section_peer(by) for by in range(1, SECTIONS)]
        + [replica_peer(by) for by in range(1, lay.dp)]
    )
    for peer in peers:
        pl.semaphore_signal(barrier, inc=1, device_id=peer, device_id_type=MESH)

    loads = {}
    for at, (name, src, dst) in enumerate(
        [
            ("x", x_in.at[section], hid.at[0, pl.ds(pl.multiple_of(member * part, part), part)]),
            ("qkv", qkv_in, wqkv),
            ("ao", ao_in, wao),
            ("gain", gain_in, gain),
            ("out_grads", out_grads_in, out_grads),
            ("bias", bias_in, bias),
            ("up", up_in, wup),
            ("down", down_in, wdown),
            ("cin", cin_in, wcin),
            ("co", co_in, wco),
        ]
    ):
        copy = pltpu.make_async_copy(src, dst, load_sem.at[at])
        copy.start()
        loads[name] = copy

    misc[...] = jnp.zeros_like(misc)
    holds = section < lay.micro
    for i in range(lay.micro):
        holds = holds | (plan[replica, i, 1] == section)
    used = jnp.where(holds, 1.0, 0.0).astype(F32)
    tap_row = lax.broadcasted_iota(jnp.int32, (TAPS, hw), 0)
    tap_mask = jnp.where(jnp.abs(tap_row - MARGIN) <= half_size[0], 1.0, 0.0)
    tap_on[...] = jnp.zeros_like(tap_on)
    tap_on[0:TAPS] = tap_mask
    tap_weight[0:TAPS] = taps_in[...].astype(F32) * tap_mask
    where[...] = jnp.full(where.shape, -1, jnp.int32)
    where[0:1, 0 : positions.shape[1]] = positions[pl.ds(section, 1)]
    lane = lax.broadcasted_iota(jnp.int32, (1, hw), 1)
    head_lanes = [(lane >= HEAD * i) & (lane < HEAD * (i + 1)) for i in range(local_heads)]
    head_low = [jnp.where(on, 1.0, 0.0).astype(BF16) for on in head_lanes]

    def block(at, size):
        return pl.ds(pl.multiple_of(at, size), size)

    def own_rows(t):
        return block(chunk * t + part * low, part)

    def other_rows(t):
        return block(chunk * t + part * (1 - low), part)

    def tiles(count, body, init=0):
        return lax.fori_loop(0, count, body, init)

    def exchange_send(e, t):
        reuse("cs", e, t)
        reuse("ys", e, t)
        at = SETS[e]

        def body(i, carry):
            rows = block(i * TILE, TILE)
            cs[at, t, rows] = partial[block(part * (1 - low) + i * TILE, TILE)].astype(BF16)
            return carry

        tiles(part // TILE, body)
        copy = send_slot("cs", cs, e, t, cr, side)

        def body(i, carry):
            rows = block(i * TILE, TILE)
            ys[at, t, rows] = partial[block(part * low + i * TILE, TILE)].astype(BF16)
            return carry

        tiles(part // TILE, body)
        return copy

    def sums_across(e, t, core_copy, start=True):
        core_copy.wait_recv()
        at = SETS[e]

        def body(i, carry):
            rows = block(i * TILE, TILE)
            ys[at, t, rows] = (ys[at, t, rows].astype(F32) + cr[at, t, rows].astype(F32)).astype(BF16)
            return carry

        tiles(part // TILE, body)
        if start:
            return send_slot("ys", ys, e, t, yr, across)

    def total_tile(e, t, rows):
        return ys[SETS[e], t, rows].astype(F32) + yr[SETS[e], t, rows].astype(F32)

    def send_half(e):
        slot = slots()
        at = SETS[e]
        out = remote(ys.at[at, 1 - high], yr.at[at, 1 - high], across, slot)
        out.start()
        leaving["ys", at, 0] = out.wait_send, (slot,)
        return remote(ys.at[at, high], yr.at[at, high], across, slot)

    def add_stat(column, amount):
        cell = (lax.broadcasted_iota(jnp.int32, (8, width), 0) == replica) & (
            lax.broadcasted_iota(jnp.int32, (8, width), 1) == column
        )
        misc[8:16] += jnp.where(cell, amount, 0.0)

    core_copies, y_copies, gathered = {}, {}, {}

    def begin(e, t, work):
        work(t)
        core_copies[e, t] = exchange_send(e, t)

    def cross(e, t):
        y_copies[e, t] = sums_across(e, t, core_copies[e, t])

    def end(e, t, finish):
        y_copies[e, t].wait_recv()
        gathered[e, t] = finish(t)

    pair_peer, pair_on = replica_bit(lay.bits - 1)
    pair_copies = {}
    halfway = lay.hidden // 2
    half_lanes = pl.ds(pl.multiple_of(pair_on * halfway, 128), halfway)

    def to_pair(which, t, src):
        rows = own_rows(t)
        pair_copies[which, t] = send(src.at[rows], pair.at[which, rows], pair_peer)

    def pass_on(which):
        for t in range(2):
            pair_copies[which, t].wait_recv()
            rows = own_rows(t)
            pair_copies[which, t] = send(pair.at[which, rows], pair.at[which, rows], side)

    def forward_finish(e, k, keep_normed):
        def finish(t):
            at = chunk * t + part * low

            def body(i, carry):
                rows = block(i * TILE, TILE)
                place = block(at + i * TILE, TILE)
                stream = hid[k, place].astype(F32)
                branch = total_tile(e, t, rows)
                norm, inv = normalise(stream + branch)
                if keep_normed:
                    normed[k, t, rows] = norm
                    inverse[k, t, rows] = inv
                hid[k + 1, place] = (norm * gain[k : k + 1] + bias[k : k + 1]).astype(BF16)
                return (carry[0] + fold(stream * stream), carry[1] + fold(branch * branch))

            zero = jnp.zeros((8, width), F32)
            squares = tiles(part // TILE, body, (zero, zero))

            @pl.when(high == t)
            def _():
                add_stat(k, whole_sum(squares[0]) * used)
                add_stat(4 + k, whole_sum(squares[1]) * used)

            rows = own_rows(t)
            copy = send(hid.at[k + 1, rows], hid.at[k + 1, rows], side)
            if k == 0:
                to_pair(0, t, hid.at[1])
            return copy

        return finish

    def norm_back_rows(k, t, grad_tile):
        at = chunk * t + part * low

        def body(i, carry):
            rows = block(i * TILE, TILE)
            dy = grad_tile(rows, block(at + i * TILE, TILE))
            norm = normed[k, t, rows]
            result = norm_pull(dy, norm, inverse[k, t, rows], gain[k : k + 1])
            normed[k, t, rows] = result
            dfull[k, block(at + i * TILE, TILE)] = result.astype(BF16)
            return (carry[0] + fold(dy * norm), carry[1] + fold(dy))

        zero = jnp.zeros((8, width), F32)
        terms = tiles(part // TILE, body, (zero, zero))

        @pl.when(high == t)
        def _():
            misc[k : k + 1] += jnp.sum(terms[0], axis=0, keepdims=True)
            misc[4 + k : 5 + k] += jnp.sum(terms[1], axis=0, keepdims=True)

        rows = own_rows(t)
        copy = send(dfull.at[k, rows], dfull.at[k, rows], side)
        if k == 1:
            to_pair(1, t, dfull.at[1])
        return copy

    def marked_total(e, values, during=None):
        ms[e] = values.astype(BF16)
        core = send(ms.at[e], mr.at[e], side)
        core.wait_recv()
        mys[e] = (ms[e].astype(F32) + mr[e].astype(F32)).astype(BF16)
        y = send(mys.at[e], myr.at[e], across)
        if during is not None:
            during()
        y.wait_recv()
        return mys[e].astype(F32) + myr[e].astype(F32)

    def reduce_piece(base, stride, size, paired):
        steps = []
        first, bit = base, lay.bits - 1
        while bit >= 0:
            peer, on = replica_bit(bit)
            keep = first + on * stride
            give = first + (1 - on) * stride
            if not paired:
                xr_at = reduce_piece.xr_at
                reduce_piece.xr_at += size
                copy = send(
                    grads.at[pl.ds(pl.multiple_of(give, 16), size)],
                    xr.at[pl.ds(xr_at, size)],
                    peer,
                )
                yield
                copy.wait_recv()
                step = math.gcd(size, 64)

                def body(i, carry, keep=keep, xr_at=xr_at, step=step):
                    here = pl.ds(pl.multiple_of(keep + i * step, 16), step)
                    there = pl.ds(pl.multiple_of(xr_at + i * step, 16), step)
                    grads[here] = (grads[here].astype(F32) + xr[there].astype(F32)).astype(BF16)
                    return carry

                tiles(size // step, body)
            steps.append((keep, give, size, peer))
            paired = False
            first, bit = keep, bit - 1
            if bit >= 0:
                size = size // 2
                stride = size
        z_at = reduce_piece.z_at
        reduce_piece.z_at += size
        mine = pl.ds(pl.multiple_of(first, 16), size)
        z_rows = pl.ds(z_at, size)
        step = math.gcd(size, 64)
        slot_a, slot_b = slots(), slots()

        def z_copy(kind):
            if kind == "a":
                return remote(
                    grads.at[mine], za.at[z_rows], (inner_of, replica, member), slot_a
                )
            if kind == "b":
                return remote(
                    grads.at[mine], zb.at[z_rows], (other_inner, replica, member), slot_b
                )
            return remote(final.at[mine], final.at[mine], (end_of, replica, member), slot_a)

        steps.reverse()
        gather_slots = [slots() for _ in steps]

        def gather(at, arriving=False):
            keep, give, half, peer = steps[at]
            rows = pl.ds(pl.multiple_of(give if arriving else keep, 16), half)
            return remote(final.at[rows], final.at[rows], peer, gather_slots[at])

        @pl.when(is_end)
        def _():
            z_copy("a").start()

        yield

        @pl.when(is_inner)
        def _():
            z_copy("a").wait_recv()

            def body(i, carry):
                here = pl.ds(pl.multiple_of(first + i * step, 16), step)
                there = pl.ds(pl.multiple_of(z_at + i * step, 16), step)
                grads[here] = (grads[here].astype(F32) + za[there].astype(F32)).astype(BF16)
                return carry

            tiles(size // step, body)
            z_copy("b").start()

        yield

        @pl.when(is_inner)
        def _():
            z_copy("b").wait_recv()

            def body(i, carry):
                here = pl.ds(pl.multiple_of(first + i * step, 16), step)
                there = pl.ds(pl.multiple_of(z_at + i * step, 16), step)
                final[here] = (grads[here].astype(F32) + zb[there].astype(F32)).astype(BF16)
                return carry

            tiles(size // step, body)
            z_copy("c").start()
            gather(0).start()

        yield

        @pl.when(is_end)
        def _():
            z_copy("c").wait_recv()
            gather(0).start()

        yield
        for at in range(len(steps)):
            if at > 0:
                gather(at).start()
                yield
            gather(at, True).wait_recv()
            closing.append((gather(at).wait_send, (gather_slots[at],)))

        def close():
            @pl.when(is_end)
            def _():
                z_copy("a").wait_send()

            @pl.when(is_inner)
            def _():
                z_copy("b").wait_send()
                z_copy("c").wait_send()

        closing.append((close, (slot_a, slot_b)))

    reduce_piece.xr_at = 0
    reduce_piece.z_at = 0
    running = {}
    summed = set()

    def launch(*names):
        for name in names:
            spec = lay.pieces.get(name)
            running[name] = reduce_piece(*spec)
            next(running[name])

    def start(name, task):
        running[name] = task
        next(task)

    def pump(*names):
        settle(KEEP)
        for name in names:
            if name in running:
                try:
                    next(running[name])
                except StopIteration:
                    del running[name]

    def line_gather(view):
        right, left = [slots() for _ in range(3)], [slots() for _ in range(3)]

        def hop(k, to_right, at):
            origin = at - k if to_right else at + k
            target = (section + (1 if to_right else -1), replica, member)
            return remote(view(origin), view(origin), target, (right if to_right else left)[k])

        def sends(k, action):
            @pl.when((section >= k) & (section < SECTIONS - 1))
            def _():
                getattr(hop(k, True, section), action)()

            @pl.when((section + k < SECTIONS) & (section > 0))
            def _():
                getattr(hop(k, False, section), action)()

        def arrivals(k):
            @pl.when(section > k)
            def _():
                hop(k, True, section - 1).wait_recv()

            @pl.when(section + k < SECTIONS - 1)
            def _():
                hop(k, False, section + 1).wait_recv()

        for k in range(SECTIONS - 1):
            sends(k, "start")
            closing.append((functools.partial(sends, k, "wait_send"), (right[k], left[k])))
            yield
            arrivals(k)

    pl.semaphore_wait(barrier, len(peers))
    mine = block(member * part, part)
    to_across = send(x_in.at[section], hid.at[0, mine], across)
    to_side = send(x_in.at[section], hid.at[0, mine], side)
    loads["x"].wait()
    hits[...] = jnp.where(
        lax.broadcasted_iota(jnp.int32, hits.shape, 0) == where[0:1, 0 : hits.shape[1]], 1.0, 0.0
    ).astype(BF16)
    loads["qkv"].wait()

    def project(at):
        rows = block(at, part)
        for j in range(3):
            qkv[j, rows] = dot_lanes(hid[0, rows], wqkv[j]).astype(BF16)

    project(member * part)
    to_side.wait_recv()
    project(side[2] * part)
    to_across.wait_recv()
    theirs = block(across[2] * part, part)
    onward = send(hid.at[0, theirs], hid.at[0, theirs], side)
    project(across[2] * part)
    onward.wait_recv()
    project(lax.rem(side[2] + 2, GROUP) * part)
    loads["ao"].wait()

    def attention_work(t):
        rows = pl.ds(chunk * t, chunk)
        mixture = jnp.zeros((chunk, hw), F32)
        for i in range(local_heads):
            if t == 1 and i == 1:
                cross(0, 0)
            scores = dot_lanes(qkv[0, rows] * head_low[i], qkv[1]) * scale
            top = jnp.max(scores, axis=-1, keepdims=True)
            powers = jnp.exp(scores - top)
            chances = powers * (1.0 / jnp.sum(powers, axis=-1, keepdims=True))
            probs[i, rows] = chances
            mixture = mixture + jnp.where(head_lanes[i], dot(chances.astype(BF16), qkv[2]), 0.0)
        mix[rows] = mixture.astype(BF16)
        partial[...] = dot(mix[rows], wao[...])

    begin(0, 0, attention_work)
    begin(0, 1, attention_work)
    cross(0, 1)
    loads["up"].wait()
    loads["down"].wait()

    def ffn_forward(layer, src, rows, units_here, slope_here=None):
        def body(i, carry):
            lanes = block(i * LANES, LANES)
            unit, steep = gelu_parts(dot(src[rows], wup[layer, :, lanes]))
            units_here[:, lanes] = unit.astype(BF16)
            if slope_here is not None:
                slope_here[:, lanes] = steep
            return carry

        tiles(lay.hidden // LANES, body)
        partial[...] = dot(units_here[...], wdown[layer])

    def ffn0_work(t):
        gathered[0, t].wait_recv()
        rows = pl.ds(chunk * t, chunk)
        ffn_forward(0, hid.at[1], rows, units.at[rows], slope.at[rows])

    for name in ("gain", "bias"):
        loads[name].wait()
    attention_finish = forward_finish(0, 0, True)
    end(0, 0, attention_finish)
    begin(1, 0, ffn0_work)
    end(0, 1, attention_finish)
    cross(1, 0)
    begin(1, 1, ffn0_work)
    cross(1, 1)

    loads["cin"].wait()
    loads["co"].wait()
    edge = jnp.zeros((PAD, hw), F32)
    for buffer in (gated, dconv):
        buffer[0:PAD] = edge
        buffer[PAD + lay.seq : 2 * PAD + lay.seq] = edge

    def conv_gates(t):
        gathered[1, t].wait_recv()
        rows = pl.ds(chunk * t, chunk)
        value_here = dot_lanes(hid[2, rows], wcin[0])
        sig_here = jax.nn.sigmoid(dot_lanes(hid[2, rows], wcin[1]))
        value[rows] = value_here
        sig[rows] = sig_here
        gated[pl.ds(PAD + chunk * t, chunk)] = value_here * sig_here

    ffn0_finish = forward_finish(1, 1, True)
    pass_on(0)
    end(1, 0, ffn0_finish)
    conv_gates(0)
    end(1, 1, ffn0_finish)
    conv_gates(1)
    tap_tile = 64

    def taps(i, carry):
        total = jnp.zeros((tap_tile, hw), F32)
        window = gated[pl.ds(pl.multiple_of(i * tap_tile, 8), tap_tile + 2 * PAD)]
        for j in range(TAPS):
            at = PAD - MARGIN + j
            total = total + tap_weight[j : j + 1] * window[at : at + tap_tile]
        conv[block(i * tap_tile, tap_tile)] = total.astype(BF16)
        return carry

    tiles(lay.seq // tap_tile, taps)

    spots = hits[...]
    conv_marked = dot_rows(spots, conv[...]).astype(BF16)
    stream = dot_rows(spots, hid[2])

    def pair_up(t):
        pair_copies[0, t].wait_recv()
        rows = pl.ds(chunk * t, chunk)
        unit, slope_here = gelu_parts(dot(pair[0, rows], wup[0, :, half_lanes]))
        punits[rows] = unit.astype(BF16)
        pslope[rows] = slope_here


    def conv_work(t):
        partial[...] = dot(conv[pl.ds(chunk * t, chunk)], wco[...])

    def ffn1_work(t):
        gathered[5, t].wait_recv()
        ffn_forward(1, hid.at[3], pl.ds(chunk * t, chunk), last_units)

    def layer_output():
        last_finish = forward_finish(5, 2, False)
        begin(5, 0, conv_work)
        begin(5, 1, conv_work)
        cross(5, 0)
        yield
        cross(5, 1)
        yield
        end(5, 0, last_finish)
        yield
        end(5, 1, last_finish)
        yield
        begin(6, 0, ffn1_work)
        yield
        begin(6, 1, ffn1_work)
        for t in range(2):
            sums_across(6, t, core_copies[6, t], start=False)
        last = send_half(6)
        yield
        last.wait_recv()

        def layer_body(i, carry):
            rows = block(i * TILE, TILE)
            stream = hid[3, block(member * part + i * TILE, TILE)].astype(F32)
            branch = total_tile(6, high, rows)
            norm, _ = normalise(stream + branch)
            result = (norm * gain[3:4] + bias[3:4]) * used
            layer_rows[section, rows] = result.astype(BF16)
            return (carry[0] + fold(stream * stream), carry[1] + fold(branch * branch))

        zero = jnp.zeros((8, width), F32)
        squares = tiles(part // TILE, layer_body, (zero, zero))
        add_stat(3, whole_sum(squares[0]) * used)
        add_stat(7, whole_sum(squares[1]) * used)
        summed.add("rows")
        yield from line_gather(lambda at: layer_rows.at[at])

    branch = marked_total(
        0, dot(conv_marked, wco[...]), lambda: start("lo", layer_output())
    )
    norm2, inv2 = normalise(stream + branch)
    mnorm[0] = norm2
    mh[...] = (norm2 * gain[2:3] + bias[2:3]).astype(BF16)

    def pick_cotangent():
        loads["out_grads"].wait()
        count = out_grads.shape[0]
        slot = lax.broadcasted_iota(jnp.int32, (1, out_grads.shape[1], 1), 1)
        mine = jnp.where(slot == section, used, 0.0)
        cotangent[...] = jnp.zeros_like(cotangent)
        cotangent[0:count] = jnp.sum(out_grads[...].astype(F32) * mine, axis=1)

    def marked_up(i, carry):
        lanes = block(i * LANES, LANES)
        unit, slope_here = gelu_parts(dot(mh[...], wup[1, :, lanes]))
        munits[:, lanes] = unit.astype(BF16)
        mslope[:, lanes] = slope_here
        return carry

    tiles(lay.hidden // LANES, marked_up)

    def beside_units():
        pump("lo")
        pick_cotangent()
        pair_up(0)

    branch = marked_total(1, dot(munits[...], wdown[1]), beside_units)
    norm3, inv3 = normalise(mh[...].astype(F32) + branch)
    once = jnp.where(member == 0, 1.0, 0.0).astype(F32)
    dy = cotangent[...]
    misc[3:4] += once * jnp.sum(dy * norm3, axis=0, keepdims=True)
    misc[7:8] += once * jnp.sum(dy, axis=0, keepdims=True)
    dz3 = norm_pull(dy, norm3, inv3, gain[3:4])
    cotangent[...] = dz3
    df3 = dz3.astype(BF16)

    per_section = lay.dp * marked
    here = pl.ds(pl.multiple_of(section * per_section + replica * marked, 16), marked)
    factors[0, here] = mh[...]
    factors[1, here] = df3

    def spread_factors():
        copies = [
            send(factors.at[low, here], factors.at[low, here], replica_peer(by))
            for by in range(1, lay.dp)
        ]
        yield
        for copy in copies:
            copy.wait_recv()
        def of_section(at):
            return factors.at[low, pl.ds(pl.multiple_of(at * per_section, 16), per_section)]

        yield from line_gather(of_section)
        slot = slots()
        send(factors.at[low], factors.at[low], side, slot)
        yield
        remote(factors.at[1 - low], factors.at[1 - low], side, slot).wait_recv()

    start("fa", spread_factors())

    def marked_down(i, carry):
        lanes = block(i * LANES, LANES)
        grad_units = dot_lanes(factors[1, here], wdown[1, lanes])
        munits[:, lanes] = (grad_units * mslope[:, lanes]).astype(BF16)
        return carry

    tiles(lay.hidden // LANES, marked_down)
    def beside_down():
        pump("lo")
        pump("lo")
        pair_up(1)

    dy = cotangent[...] + marked_total(2, dot_lanes(munits[...], wup[1]), beside_down)
    pump("fa")
    norm2 = mnorm[0]
    misc[2:3] += once * jnp.sum(dy * norm2, axis=0, keepdims=True)
    misc[6:7] += once * jnp.sum(dy, axis=0, keepdims=True)
    dz2 = norm_pull(dy, norm2, inv2, gain[2:3])
    dz2_terms = two_terms(dz2)
    df2 = dz2.astype(BF16)

    def spread(rows, terms):
        where_rows = hits[rows]
        return dot(where_rows, terms[0]) + dot(where_rows, terms[1])

    dconv_terms = two_terms(dot_lanes(df2, wco[...]))
    dconv[pl.ds(PAD, lay.seq)] = spread(pl.ds(0, lay.seq), dconv_terms)

    def taps_back(i, carry):
        total = jnp.zeros((tap_tile, hw), F32)
        place = pl.ds(pl.multiple_of(i * tap_tile, 8), tap_tile + 2 * PAD)
        window = dconv[place]
        around = gated[place]
        middle = window[PAD : PAD + tap_tile]
        sums = []
        for j in range(TAPS):
            at = PAD + MARGIN - j
            total = total + tap_weight[j : j + 1] * window[at : at + tap_tile]
            at = PAD - MARGIN + j
            sums.append(jnp.sum(around[at : at + tap_tile] * middle, axis=0, keepdims=True))
        rows = block(i * tap_tile, tap_tile)
        s = sig[rows]
        by_value = total * s
        dgates[0, rows] = by_value.astype(BF16)
        dgates[1, rows] = (by_value * value[rows] * (1.0 - s)).astype(BF16)
        sums.append(jnp.zeros((1, hw), F32))
        return carry + jnp.concatenate(sums, axis=0)

    def conv_back_work(t):
        rows = pl.ds(chunk * t, chunk)
        partial[...] = dot(dgates[0, rows], wcin[0]) + dot(dgates[1, rows], wcin[1])

    half_tiles = chunk // tap_tile
    kernel_rows = lax.fori_loop(0, half_tiles, taps_back, jnp.zeros((8, hw), F32))
    begin(2, 0, conv_back_work)
    kernel_rows = lax.fori_loop(half_tiles, 2 * half_tiles, taps_back, kernel_rows)
    cross(2, 0)
    begin(2, 1, conv_back_work)
    kernel_rows = kernel_rows * tap_on[...]
    grads[pl.ds(lay.kernel_at, lay.up_at - lay.kernel_at)] = jnp.zeros(
        (lay.up_at - lay.kernel_at, width), BF16
    )
    grads[pl.ds(lay.kernel_at, 16), 0:hw] = jnp.concatenate(
        [kernel_rows, jnp.zeros((8, hw), F32)], axis=0
    ).astype(BF16)

    def conv_back_finish(t):
        def grad_tile(rows, place):
            return total_tile(2, t, rows) + spread(place, dz2_terms)

        return norm_back_rows(1, t, grad_tile)

    def ffn0_back_work(t):
        gathered[2, t].wait_recv()
        rows = pl.ds(chunk * t, chunk)

        def body(i, carry):
            lanes = block(i * LANES, LANES)
            grad_units = dot_lanes(dfull[1, rows], wdown[0, lanes])
            dbefore[rows, lanes] = (grad_units * slope[rows, lanes]).astype(BF16)
            return carry

        tiles(lay.hidden // LANES, body)
        partial[...] = dot_lanes(dbefore[rows], wup[0])

    def ffn0_back_finish(t):
        return norm_back_rows(
            0, t, lambda rows, place: normed[1, t, rows] + total_tile(3, t, rows)
        )

    up_rows = pl.ds(pl.multiple_of(lay.up_at + pair_on * halfway, 16), halfway)
    down_rows = pl.ds(pl.multiple_of(lay.down_at + pair_on * halfway, 16), halfway)

    def own_weights():
        left = dbefore[:, half_lanes]
        for q in range(2):
            lanes = pl.ds(q * halfway, halfway)
            grads[up_rows, lanes] = dot_rows(hid[1, :, lanes], left).astype(BF16)
        grads[down_rows] = dot_rows(units[:, half_lanes], dfull[1]).astype(BF16)

    def pair_weights():
        for t in range(2):
            pair_copies[1, t].wait_recv()
            rows = pl.ds(chunk * t, chunk)
            grad_units = dot_lanes(pair[1, rows], wdown[0, half_lanes])
            pdbefore[rows] = (grad_units * pslope[rows]).astype(BF16)
        left = pdbefore[...]
        for q in range(2):
            lanes = pl.ds(q * halfway, halfway)
            total = grads[up_rows, lanes].astype(F32) + dot_rows(pair[0, :, lanes], left)
            grads[up_rows, lanes] = total.astype(BF16)
        launch(*lay.groups["u"])
        total = grads[down_rows].astype(F32) + dot_rows(punits[...], pair[1])
        grads[down_rows] = total.astype(BF16)
        launch(*lay.groups["d"])

    def attention_back_work(t):
        rows = pl.ds(chunk * t, chunk)
        partial[...] = (
            dot(dqkv[0, rows], wqkv[0])
            + dot(dqkv[1, rows], wqkv[1])
            + dot(dqkv[2, rows], wqkv[2])
        )

    def attention_back_rows(t):
        gathered[3, t].wait_recv()
        rows = pl.ds(chunk * t, chunk)
        dmix[rows] = dot_lanes(dfull[0, rows], wao[...]).astype(BF16)
        grad_queries = jnp.zeros((chunk, hw), F32)
        for i in range(local_heads):
            chances = probs[i, rows]
            grad_chances = dot_lanes(dmix[rows] * head_low[i], qkv[2])
            grad_scores = chances * (
                grad_chances - jnp.sum(grad_chances * chances, axis=-1, keepdims=True)
            )
            grad_scores = grad_scores.astype(BF16)
            on = head_lanes[i]
            grad_queries = grad_queries + jnp.where(on, dot(grad_scores, qkv[1]), 0.0)
            dkv[0] += jnp.where(on, dot_rows(grad_scores, qkv[0, rows]), 0.0)
            dkv[1] += jnp.where(on, dot_rows(chances.astype(BF16), dmix[rows]), 0.0)
        dqkv[0, rows] = (grad_queries * scale).astype(BF16)

    waits = {}

    def backward():
        cross(2, 1)
        for j in range(2):
            grads[pl.ds(lay.conv_at + j * hw, hw)] = dot_rows(dgates[j], hid[2]).astype(BF16)
        grads[pl.ds(lay.conv_at + 2 * hw, hw)] = dot_rows(conv_marked, df2).astype(BF16)
        launch(*lay.groups["c"])
        yield
        end(2, 0, conv_back_finish)
        begin(3, 0, ffn0_back_work)
        yield
        end(2, 1, conv_back_finish)
        cross(3, 0)
        begin(3, 1, ffn0_back_work)
        cross(3, 1)
        yield
        end(3, 0, ffn0_back_finish)
        yield
        end(3, 1, ffn0_back_finish)
        summed.add("norms")
        yield
        dkv[...] = jnp.zeros_like(dkv)
        attention_back_rows(0)
        yield
        attention_back_rows(1)
        dqkv[1] = (dkv[0] * scale).astype(BF16)
        dqkv[2] = dkv[1].astype(BF16)
        for t in range(2):
            begin(4, t, attention_back_work)
        for t in range(2):
            sums_across(4, t, core_copies[4, t], start=False)
        waits["input"] = send_half(4)
        yield
        for j in range(3):
            grads[pl.ds(lay.attn_at + j * hw, hw)] = dot_rows(dqkv[j], hid[0]).astype(BF16)
        grads[pl.ds(lay.attn_at + 3 * hw, hw)] = dot_rows(mix[...], dfull[0]).astype(BF16)
        launch(*lay.groups["a"])

    def feed_forward_weights():
        own_weights()
        yield
        pass_on(1)
        yield
        pair_weights()

    def input_body(i, carry):
        rows = block(i * TILE, TILE)
        total = total_tile(4, high, rows)
        input_rows[section, rows] = (normed[0, high, rows] + total).astype(BF16)
        return carry

    def input_gradient():
        waits["input"].wait_recv()
        tiles(part // TILE, input_body)
        yield from line_gather(lambda at: input_rows.at[at])

    group_rows = GROUP * marked
    groups = SECTIONS * per_section // group_rows

    def last_block():
        assert not {"main", "pw", "fa"} & set(running)
        for group in range(groups):
            rows = pl.ds(group * group_rows, group_rows)

            def recompute(j, carry, rows=rows):
                lanes = block(j * LANES, LANES)
                unit, slope_here = gelu_parts(dot(factors[0, rows], wup[1, :, lanes]))
                units[0:group_rows, lanes] = unit.astype(BF16)
                grad_units = dot_lanes(factors[1, rows], wdown[1, lanes])
                dbefore[0:group_rows, lanes] = (grad_units * slope_here).astype(BF16)
                return carry

            tiles(lay.hidden // LANES, recompute)

            def last_weights(i, carry, rows=rows, group=group):
                lanes = block(i * LANES, LANES)
                by_up = dot_rows(factors[0, rows, lanes], dbefore[0:group_rows])
                by_down = dot_rows(units[0:group_rows, lanes], factors[1, rows])
                wide, rest = probs.shape[2], width - probs.shape[2]
                held = [
                    (
                        probs.at[i, pl.ds(j * LANES, LANES)],
                        slope.at[pl.ds(j * LANES, LANES), block(i * rest, rest)],
                    )
                    for j in range(2)
                ]
                if group > 0:
                    by_up = by_up + jnp.concatenate([held[0][0][...], held[0][1][...]], axis=1)
                    by_down = by_down + jnp.concatenate([held[1][0][...], held[1][1][...]], axis=1)
                if group < groups - 1:
                    for (left, right), total in zip(held, (by_up, by_down)):
                        left[...] = total[:, :wide]
                        right[...] = total[:, wide:]
                else:
                    at = pl.multiple_of(i * LANES, LANES)
                    final[pl.ds(lay.up1_at + at, LANES)] = by_up.astype(BF16)
                    final[pl.ds(lay.down1_at + at, LANES)] = by_down.astype(BF16)
                return carry

            tiles(width // LANES, last_weights)
            yield

    def small_sums():
        assert summed >= {"norms", "rows"}
        hops = [side, across] + [replica_bit(bit)[0] for bit in range(lay.bits)]
        for at, peer in enumerate(hops):
            misc_in[2 * at] = misc[...]
            copy = send(misc_in.at[2 * at], misc_in.at[2 * at + 1], peer)
            yield
            copy.wait_recv()
            misc[...] = misc_in[2 * at] + misc_in[2 * at + 1]
        at = 2 * len(hops)
        slot_a, slot_b = slots(), slots()
        to_inner = remote(misc_in.at[at], misc_in.at[at + 1], (inner_of, replica, member), slot_a)
        to_other = remote(
            misc_in.at[at + 2], misc_in.at[at + 3], (other_inner, replica, member), slot_b
        )
        to_end = remote(misc_out, misc_out, (end_of, replica, member), slot_a)

        @pl.when(is_end)
        def _():
            misc_in[at] = misc[...]
            to_inner.start()

        yield

        @pl.when(is_inner)
        def _():
            to_inner.wait_recv()
            misc_in[at + 2] = misc[...] + misc_in[at + 1]
            to_other.start()

        yield

        @pl.when(is_inner)
        def _():
            to_other.wait_recv()
            misc_out[...] = misc_in[at + 2] + misc_in[at + 3]
            to_end.start()

        yield

        @pl.when(is_end)
        def _():
            to_end.wait_recv()
            to_inner.wait_send()

        @pl.when(is_inner)
        def _():
            to_other.wait_send()
            to_end.wait_send()

    later = {
        "main": backward,
        "pw": feed_forward_weights,
        "ig": input_gradient,
        "w1": last_block,
        "ms": small_sums,
    }
    for name in TAIL:
        if name in later:
            start(name, later.pop(name)())
        else:
            pump(name)
    assert not later
    while running:
        pump(*list(running))
    closing.extend(leaving.values())
    settle()
    assert counter[0] <= lay.arrivals and counter[1] <= lay.departures


def widen_kernel(
    lay,
    final,
    input_rows,
    layer_rows,
    misc,
    plan,
    layer_out,
    input_grad,
    qkv,
    out,
    cin,
    cout,
    up,
    down,
    kernel,
    gains,
    biases,
    rms,
    wide,
    wide_input,
    store_sem,
):
    hw, width, hidden = lay.heads_width, lay.width, lay.hidden
    blocks = []

    def cover(start, rows, target, step):
        for at in range(0, rows, step):
            blocks.append((start + at, step, target.at[pl.ds(at, step)]))

    for layer, (up_at, down_at) in enumerate(
        ((lay.up_at, lay.down_at), (lay.up1_at, lay.down1_at))
    ):
        cover(up_at, width, up.at[layer], width // 2)
        cover(down_at, hidden, down.at[layer], hidden // 2)
    for j in range(3):
        cover(lay.attn_at + j * hw, hw, qkv.at[j], hw)
    cover(lay.attn_at + 3 * hw, hw, out, hw)
    for j in range(2):
        cover(lay.conv_at + j * hw, hw, cin.at[j], hw)
    cover(lay.conv_at + 2 * hw, hw, cout, hw)

    def store(at):
        start, rows, target = blocks[at]
        return pltpu.make_async_copy(wide.at[pl.ds(start, rows)], target, store_sem.at[at])

    extra = len(blocks)
    inputs_out = pltpu.make_async_copy(wide_input, input_grad, store_sem.at[extra])
    layer_done = pltpu.make_async_copy(layer_rows, layer_out, store_sem.at[extra + 1])
    layer_done.start()
    gains[...] = misc[0:4]
    biases[...] = misc[4:8]
    row = lax.broadcasted_iota(jnp.int32, rms.shape, 0)
    counts = jnp.zeros(rms.shape, F32)
    for r in range(rms.shape[0]):
        total = jnp.float32(lay.micro)
        for i in range(lay.micro):
            total = total + jnp.where(plan[r, i, 1] >= 0, 1.0, 0.0).astype(F32)
        counts = jnp.where(row == r, total, counts)
    rms[...] = jnp.sqrt(misc[8 : 8 + rms.shape[0], 0:8] / (counts * (lay.seq * width)))
    half = width // 2
    for at, (start, rows, _) in enumerate(blocks):
        def body(i, carry, start=start, at=at):
            here = pl.ds(pl.multiple_of(start + i * 32, 16), 32)
            if at >= 2:
                wide[here] = final[here].astype(F32)
            else:
                for q in range(2):
                    there = pl.ds(pl.multiple_of(lay.up_at + q * half + i * 32, 16), 32)
                    wide[here, q * half : (q + 1) * half] = final[
                        there, at * half : (at + 1) * half
                    ].astype(F32)
            return carry

        lax.fori_loop(0, rows // 32, body, 0)
        store(at).start()
    for slot in range(input_rows.shape[0]):
        wide_input[slot] = input_rows[slot].astype(F32)
    inputs_out.start()
    taps = final[pl.ds(lay.kernel_at, 16)].astype(F32)
    kernel[...] = taps[0:TAPS, 0:hw]
    for at in range(len(blocks)):
        store(at).wait()
    inputs_out.wait()
    layer_done.wait()


def on_device(
    inputs,
    attn_qkv,
    attn_out,
    conv_in,
    conv_kernel,
    conv_out,
    ffn_up,
    ffn_down,
    norm_gain,
    norm_bias,
    kernel_half,
    batch_plan,
    masked_positions,
    out_grad,
):
    section = lax.axis_index("section")
    replica = lax.axis_index("dp")
    dp = lax.axis_size("dp")
    slot_count, part, width = inputs.shape
    micro_count = batch_plan.shape[1]
    count = masked_positions.shape[1]
    marked = round_up(count, 16)
    assert slot_count == SECTIONS == lax.axis_size("section") and lax.axis_size("mp") == GROUP
    hw = attn_out.shape[0]
    hidden = ffn_up.shape[2]
    lay = Layout(dp, micro_count, part * GROUP, width, hw, hidden, marked)
    assert hidden == width and width % LANES == 0 and hw % HEAD == 0

    seq, chunk = lay.seq, lay.chunk
    any_spec = pl.BlockSpec(memory_space=pl.ANY)
    vmem_spec = pl.BlockSpec(memory_space=pltpu.VMEM)
    hops = 2 + lay.bits
    all_marked = SECTIONS * dp * marked
    scratch = [
        pltpu.VMEM((8, hw), F32),
        pltpu.VMEM((8, hw), F32),
        pltpu.VMEM((8, marked), jnp.int32),
        pltpu.VMEM(norm_gain.shape, F32),
        pltpu.VMEM(norm_bias.shape, F32),
        pltpu.VMEM((marked, width), F32),
        pltpu.VMEM((count, slot_count, width), BF16),
        pltpu.VMEM((3, hw, width), BF16),
        pltpu.VMEM(attn_out.shape, BF16),
        pltpu.VMEM((2, hw, width), BF16),
        pltpu.VMEM(conv_out.shape, BF16),
        pltpu.VMEM(ffn_up.shape, BF16),
        pltpu.VMEM(ffn_down.shape, BF16),
        pltpu.VMEM((4, seq, width), BF16),
        pltpu.VMEM((2, seq, width), BF16),
        pltpu.VMEM((2, 2, part, width), F32),
        pltpu.VMEM((2, 2, part, 1), F32),
        pltpu.VMEM((3, seq, hw), BF16),
        pltpu.VMEM((hw // HEAD, seq, seq), F32),
        pltpu.VMEM((seq, hw), BF16),
        pltpu.VMEM((seq, hw), BF16),
        pltpu.VMEM((3, seq, hw), BF16),
        pltpu.VMEM((2, seq, hw), F32),
        pltpu.VMEM((seq, hidden), BF16),
        pltpu.VMEM((seq, hidden), F32),
        pltpu.VMEM((seq, hidden), BF16),
        pltpu.VMEM((chunk, hidden), BF16),
        pltpu.VMEM((seq, hw), F32),
        pltpu.VMEM((seq, hw), F32),
        pltpu.VMEM((seq + 2 * PAD, hw), F32),
        pltpu.VMEM((seq, hw), BF16),
        pltpu.VMEM((seq + 2 * PAD, hw), F32),
        pltpu.VMEM((2, seq, hw), BF16),
        pltpu.VMEM((seq, marked), BF16),
        pltpu.VMEM((marked, width), BF16),
        pltpu.VMEM((1, marked, width), F32),
        pltpu.VMEM((marked, hidden), F32),
        pltpu.VMEM((marked, hidden), BF16),
        pltpu.VMEM((chunk, width), F32),
        pltpu.VMEM((4, 2, part, width), BF16),
        pltpu.VMEM((4, 2, part, width), BF16),
        pltpu.VMEM((4, 2, part, width), BF16),
        pltpu.VMEM((4, 2, part, width), BF16),
        pltpu.VMEM((3, marked, width), BF16),
        pltpu.VMEM((3, marked, width), BF16),
        pltpu.VMEM((3, marked, width), BF16),
        pltpu.VMEM((3, marked, width), BF16),
        pltpu.VMEM((lay.rows, width), BF16),
        pltpu.VMEM((lay.xr_rows, width), BF16),
        pltpu.VMEM((lay.z_rows, width), BF16),
        pltpu.VMEM((lay.z_rows, width), BF16),
        pltpu.VMEM((2, all_marked, width), BF16),
        pltpu.VMEM((2, seq, width), BF16),
        pltpu.VMEM((seq, hidden // 2), BF16),
        pltpu.VMEM((seq, hidden // 2), F32),
        pltpu.VMEM((seq, hidden // 2), BF16),
        pltpu.VMEM((lay.misc_rows, width), F32),
        pltpu.VMEM((2 * hops + 4, lay.misc_rows, width), F32),
        pltpu.SemaphoreType.DMA((10,)),
        pltpu.SemaphoreType.DMA((lay.departures,)),
        pltpu.SemaphoreType.DMA((lay.arrivals,)),
    ]
    smem_spec = pl.BlockSpec(memory_space=pltpu.SMEM)
    final, layer_rows, input_rows, misc = pl.pallas_call(
        functools.partial(main_kernel, lay),
        out_shape=(
            pltpu.VMEM((lay.all_rows, width), BF16),
            pltpu.VMEM((slot_count, part, width), BF16),
            pltpu.VMEM((slot_count, part, width), BF16),
            pltpu.VMEM((lay.misc_rows, width), F32),
        ),
        in_specs=[any_spec] * 9 + [vmem_spec] * 2 + [any_spec] + [smem_spec] * 2,
        out_specs=(vmem_spec,) * 4,
        scratch_shapes=scratch,
        compiler_params=pltpu.CompilerParams(
            collective_id=0, has_side_effects=True, vmem_limit_bytes=VMEM_BYTES
        ),
        name="layers",
    )(
        inputs,
        jnp.swapaxes(attn_qkv, 1, 2),
        attn_out,
        jnp.swapaxes(conv_in, 1, 2),
        conv_out,
        ffn_up,
        ffn_down,
        norm_gain,
        norm_bias,
        conv_kernel,
        masked_positions,
        jnp.swapaxes(out_grad, 0, 1),
        kernel_half,
        batch_plan,
    )
    shapes = [
        (slot_count, part, width),
        (3, hw, width),
        (hw, width),
        (2, hw, width),
        (hw, width),
        (2, width, hidden),
        (2, hidden, width),
        (TAPS, hw),
        (4, width),
        (4, width),
        (dp, 8),
    ]
    widened = pl.pallas_call(
        functools.partial(widen_kernel, lay),
        out_shape=(jax.ShapeDtypeStruct(shapes[0], BF16),)
        + tuple(jax.ShapeDtypeStruct(shape, F32) for shape in shapes),
        in_specs=[vmem_spec] * 4 + [smem_spec],
        out_specs=(any_spec,) * 8 + (vmem_spec,) * 4,
        scratch_shapes=[
            pltpu.VMEM((lay.all_rows, width), F32),
            pltpu.VMEM((slot_count, part, width), F32),
            pltpu.SemaphoreType.DMA((17,)),
        ],
        compiler_params=pltpu.CompilerParams(vmem_limit_bytes=VMEM_BYTES),
        name="widen",
    )(
        *[
            pltpu.with_memory_space_constraint(result, pltpu.VMEM)
            for result in (final, input_rows, layer_rows, misc)
        ],
        batch_plan,
    )
    (layer_out, input_grad, qkv, out, cin, cout, up, down, kernel, gains, biases, rms) = widened
    return (
        layer_out,
        input_grad,
        jnp.swapaxes(qkv, 1, 2),
        out,
        jnp.swapaxes(cin, 1, 2),
        kernel,
        cout,
        up,
        down,
        gains,
        biases,
        rms,
    )


def solution(mesh):
    return jax.shard_map(
        on_device,
        mesh=mesh,
        in_specs=(
            P("dp", "mp", None),
            P(None, None, "mp"),
            P("mp", None),
            P(None, None, "mp"),
            P(None, "mp"),
            P("mp", None),
            P(None, None, "mp"),
            P(None, "mp", None),
            P(),
            P(),
            P(),
            P(),
            P("dp", None),
            P("dp", None, None),
        ),
        out_specs=(
            P("dp", "mp", None),
            P("dp", "mp", None),
            P(None, None, "mp"),
            P("mp", None),
            P(None, None, "mp"),
            P(None, "mp"),
            P("mp", None),
            P(None, None, "mp"),
            P(None, "mp", None),
            P(),
            P(),
            P(),
        ),
        check_vma=False,
    )
```

```python
import functools
import math

import jax
import jax.numpy as jnp
from jax import lax
from jax.experimental import pallas as pl
from jax.experimental.pallas import tpu as pltpu
from jax.sharding import PartitionSpec as P

HEAD = 64
TAPS = 7
MARGIN = TAPS // 2
EPSILON = 1e-05
SECTIONS = 4
GROUP = 4
PAD = 8
TILE = 32
VMEM_BYTES = 55 * 2**20 + 2**17
SETS = (0, 1, 0, 1, 2, 2, 3)
LANES = 256

KEEP = 12
C_CUT, U_CUT, D_CUT, A_CUT = (2, 1, 2), (1, 1, 2, 2), (2, 2, 2), (2, 2, 1, 1)
TAIL = (
    "main", "fa", "lo", "lo", "c0", "fa", "main", "c0", "c1", "lo", "main", "c0", "fa", "fa", "c1",
    "pw", "c2", "main", "lo", "pw", "pw", "c0", "c1", "c2", "main", "main", "c0", "lo", "u0", "c1",
    "main", "c1", "lo", "u0", "u2", "c2", "u3", "u0", "u1", "u2", "ms", "d0", "u3", "d1", "u1",
    "d2", "d0", "d1", "c2", "ms", "a0", "a0", "u2", "u3", "u0", "a3", "a3", "a1", "c2", "u1", "d2",
    "ms", "a2", "a1", "u2", "d0", "d1", "u3", "u1", "d2", "a2", "a0", "a3", "ig", "d0", "d1", "a3",
    "a1", "a0", "a2", "d2", "ms", "a1", "ig", "w1", "a2", "ms", "a3", "ms", "a0", "ms", "ig", "w1",
    "a1", "w1", "a2", "ig",
)

F32 = jnp.float32
BF16 = jnp.bfloat16
MESH = pl.DeviceIdType.MESH


def dot(left, right):
    return jnp.dot(left, right, preferred_element_type=F32)


def dot_lanes(left, right):
    return lax.dot_general(left, right, (((1,), (1,)), ((), ())), preferred_element_type=F32)


def dot_rows(left, right):
    return lax.dot_general(left, right, (((0,), (0,)), ((), ())), preferred_element_type=F32)


def round_up(value, step):
    return (value + step - 1) // step * step


def normalise(summed):
    centre = summed - jnp.mean(summed, axis=-1, keepdims=True)
    variance = jnp.mean(centre * centre, axis=-1, keepdims=True)
    inverse = lax.rsqrt(variance + EPSILON)
    return centre * inverse, inverse


def norm_pull(grad_out, normed, inverse, gain_row):
    scaled = grad_out * gain_row
    first = jnp.mean(scaled, axis=-1, keepdims=True)
    second = jnp.mean(scaled * normed, axis=-1, keepdims=True)
    return inverse * (scaled - first - normed * second)


def gelu_parts(before):
    cdf = 0.5 * (1.0 + lax.erf(before * math.sqrt(0.5)))
    slope = cdf + before * jnp.exp(-0.5 * before * before) * (1.0 / math.sqrt(2.0 * math.pi))
    return before * cdf, slope


def two_terms(values):
    high = values.astype(BF16)
    return high, (values - high.astype(F32)).astype(BF16)


def fold(rows):
    count, width = rows.shape
    return jnp.sum(rows.reshape(count // 8, 8, width), axis=0)


def whole_sum(values):
    return jnp.sum(values, axis=(0, 1), keepdims=True)


class Layout:
    def __init__(self, dp, micro, seq, width, heads_width, hidden, marked):
        self.dp, self.micro, self.seq, self.width = dp, micro, seq, width
        self.heads_width, self.hidden = heads_width, hidden
        self.marked = marked
        self.part = seq // GROUP
        self.chunk = 2 * self.part
        unit = 16 * dp
        conv_rows = round_up(3 * heads_width + 16, max(unit, 128))
        self.conv_at, at = 0, conv_rows
        self.up_at, at = at, at + width
        self.down_at, at = at, at + hidden
        self.attn_at, at = at, at + 4 * heads_width
        self.rows = at
        self.up1_at, at = at, at + width
        self.down1_at, at = at, at + hidden
        self.all_rows = at
        self.kernel_at = self.conv_at + 3 * heads_width
        half, step = width // 2, width // 6
        self.pieces, self.groups = {}, {}

        def cut(name, start, stride, sizes):
            at = start
            self.groups[name] = []
            for i, size in enumerate(sizes):
                size = step * size // 2
                key = name + str(i)
                self.pieces[key] = (at, stride or size, size, stride > 0)
                self.groups[name].append(key)
                at += size if stride else 2 * size

        cut("c", self.conv_at, 0, C_CUT)
        cut("u", self.up_at, half, U_CUT)
        cut("d", self.down_at, half, D_CUT)
        cut("a", self.attn_at, 0, A_CUT)
        self.xr_rows = self.z_rows = 0
        for _, _, size, paired in self.pieces.values():
            least = size // (dp // 2)
            assert least * (dp // 2) == size and least % 16 == 0
            self.xr_rows += size - least + (0 if paired else size)
            self.z_rows += least
        self.bits = dp.bit_length() - 1
        assert dp == 1 << self.bits and dp <= 8
        self.misc_rows = 16
        self.arrivals = 127 + (2 * len(self.pieces) + 1) * (self.bits - 1) + dp - 2
        self.departures = self.arrivals * 4 // 7


def main_kernel(
    lay,
    x_in,
    qkv_in,
    ao_in,
    cin_in,
    co_in,
    up_in,
    down_in,
    gain_in,
    bias_in,
    taps_in,
    positions,
    out_grads_in,
    half_size,
    plan,
    final,
    layer_rows,
    input_rows,
    misc_out,
    tap_weight,
    tap_on,
    where,
    gain,
    bias,
    cotangent,
    out_grads,
    wqkv,
    wao,
    wcin,
    wco,
    wup,
    wdown,
    hid,
    dfull,
    normed,
    inverse,
    qkv,
    probs,
    mix,
    dmix,
    dqkv,
    dkv,
    units,
    slope,
    dbefore,
    last_units,
    value,
    sig,
    gated,
    conv,
    dconv,
    dgates,
    hits,
    mh,
    mnorm,
    mslope,
    munits,
    cs,
    cr,
    ys,
    yr,
    ms,
    mr,
    mys,
    myr,
    grads,
    xr,
    za,
    zb,
    factors,
    pair,
    punits,
    pslope,
    pdbefore,
    misc,
    misc_in,
    load_sem,
    send_sem,
    recv_sem,
):
    section, replica, member = (
        lax.axis_index("section"),
        lax.axis_index("dp"),
        lax.axis_index("mp"),
    )
    low = lax.rem(member, 2)
    high = lax.div(member, 2)
    part, chunk, width = lay.part, lay.chunk, lay.width
    hw, marked = lay.heads_width, lay.marked
    local_heads = hw // HEAD
    scale = HEAD ** (-0.5)
    side = (section, replica, member + 1 - 2 * low)
    across = (section, replica, lax.rem(member + 2, GROUP))
    is_end = (section == 0) | (section == SECTIONS - 1)
    is_inner = jnp.logical_not(is_end)
    inner_of = jnp.where(section == 0, 1, SECTIONS - 2)
    end_of = jnp.where(section == 1, 0, SECTIONS - 1)
    other_inner = SECTIONS - 1 - section
    counter = [0, 0]
    closing = []
    leaving = {}

    def section_peer(by):
        return (lax.rem(section + by, SECTIONS), replica, member)

    def replica_peer(by):
        return (section, lax.rem(replica + by, lay.dp), member)

    def replica_bit(bit):
        on = lax.rem(lax.div(replica, 1 << bit), 2)
        return (section, replica + (1 - 2 * on) * (1 << bit), member), on

    free, departures = [], {}

    def slots():
        at = counter[0]
        counter[0] += 1
        if not free:
            free.append(counter[1])
            counter[1] += 1
        departures[at] = free.pop()
        return at

    def settle(keep=0):
        while len(closing) > keep:
            wait, done = closing.pop(0)
            wait()
            free.extend(departures[slot] for slot in done)

    def remote(src, dst, target, slot):
        return pltpu.make_async_remote_copy(
            src_ref=src,
            dst_ref=dst,
            send_sem=send_sem.at[departures[slot]],
            recv_sem=recv_sem.at[slot],
            device_id=target,
            device_id_type=MESH,
        )

    def send(src, dst, target, slot=None):
        slot = slots() if slot is None else slot
        copy = remote(src, dst, target, slot)
        copy.start()
        closing.append((copy.wait_send, (slot,)))
        return copy

    def send_slot(name, ref, e, t, dst, target):
        slot = slots()
        copy = remote(ref.at[SETS[e], t], dst.at[SETS[e], t], target, slot)
        copy.start()
        leaving[name, SETS[e], t] = copy.wait_send, (slot,)
        return copy

    def reuse(name, e, t):
        entry = leaving.pop((name, SETS[e], t), None)
        if entry is not None:
            closing.insert(0, entry)
            settle(len(closing) - 1)

    barrier = pltpu.get_barrier_semaphore()
    peers = (
        [side, across]
        + [section_peer(by) for by in range(1, SECTIONS)]
        + [replica_peer(by) for by in range(1, lay.dp)]
    )
    for peer in peers:
        pl.semaphore_signal(barrier, inc=1, device_id=peer, device_id_type=MESH)

    loads = {}
    for at, (name, src, dst) in enumerate(
        [
            ("x", x_in.at[section], hid.at[0, pl.ds(pl.multiple_of(member * part, part), part)]),
            ("qkv", qkv_in, wqkv),
            ("ao", ao_in, wao),
            ("gain", gain_in, gain),
            ("out_grads", out_grads_in, out_grads),
            ("bias", bias_in, bias),
            ("up", up_in, wup),
            ("down", down_in, wdown),
            ("cin", cin_in, wcin),
            ("co", co_in, wco),
        ]
    ):
        copy = pltpu.make_async_copy(src, dst, load_sem.at[at])
        copy.start()
        loads[name] = copy

    misc[...] = jnp.zeros_like(misc)
    holds = section < lay.micro
    for i in range(lay.micro):
        holds = holds | (plan[replica, i, 1] == section)
    used = jnp.where(holds, 1.0, 0.0).astype(F32)
    tap_row = lax.broadcasted_iota(jnp.int32, (TAPS, hw), 0)
    tap_mask = jnp.where(jnp.abs(tap_row - MARGIN) <= half_size[0], 1.0, 0.0)
    tap_on[...] = jnp.zeros_like(tap_on)
    tap_on[0:TAPS] = tap_mask
    tap_weight[0:TAPS] = taps_in[...].astype(F32) * tap_mask
    where[...] = jnp.full(where.shape, -1, jnp.int32)
    where[0:1, 0 : positions.shape[1]] = positions[pl.ds(section, 1)]
    lane = lax.broadcasted_iota(jnp.int32, (1, hw), 1)
    head_lanes = [(lane >= HEAD * i) & (lane < HEAD * (i + 1)) for i in range(local_heads)]
    head_low = [jnp.where(on, 1.0, 0.0).astype(BF16) for on in head_lanes]

    def block(at, size):
        return pl.ds(pl.multiple_of(at, size), size)

    def own_rows(t):
        return block(chunk * t + part * low, part)

    def other_rows(t):
        return block(chunk * t + part * (1 - low), part)

    def tiles(count, body, init=0):
        return lax.fori_loop(0, count, body, init)

    def exchange_send(e, t, product):
        reuse("cs", e, t)
        reuse("ys", e, t)
        cs[SETS[e], t] = product(1 - low).astype(BF16)
        copy = send_slot("cs", cs, e, t, cr, side)
        ys[SETS[e], t] = product(low).astype(BF16)
        return copy

    def half_rows(t, core):
        return block(chunk * t + part * core, part)

    def sums_across(e, t, core_copy, start=True):
        core_copy.wait_recv()
        at = SETS[e]

        def body(i, carry):
            rows = block(i * TILE, TILE)
            ys[at, t, rows] = (ys[at, t, rows].astype(F32) + cr[at, t, rows].astype(F32)).astype(BF16)
            return carry

        tiles(part // TILE, body)
        if start:
            return send_slot("ys", ys, e, t, yr, across)

    def total_tile(e, t, rows):
        return ys[SETS[e], t, rows].astype(F32) + yr[SETS[e], t, rows].astype(F32)

    def send_half(e):
        slot = slots()
        at = SETS[e]
        out = remote(ys.at[at, 1 - high], yr.at[at, 1 - high], across, slot)
        out.start()
        leaving["ys", at, 0] = out.wait_send, (slot,)
        return remote(ys.at[at, high], yr.at[at, high], across, slot)

    def add_stat(column, amount):
        cell = (lax.broadcasted_iota(jnp.int32, (8, width), 0) == replica) & (
            lax.broadcasted_iota(jnp.int32, (8, width), 1) == column
        )
        misc[8:16] += jnp.where(cell, amount, 0.0)

    core_copies, y_copies, gathered = {}, {}, {}

    def begin(e, t, work):
        core_copies[e, t] = exchange_send(e, t, work(t))

    def cross(e, t):
        y_copies[e, t] = sums_across(e, t, core_copies[e, t])

    def end(e, t, finish):
        y_copies[e, t].wait_recv()
        gathered[e, t] = finish(t)

    pair_peer, pair_on = replica_bit(lay.bits - 1)
    pair_copies = {}
    halfway = lay.hidden // 2
    half_lanes = pl.ds(pl.multiple_of(pair_on * halfway, 128), halfway)

    def to_pair(which, t, src):
        rows = own_rows(t)
        pair_copies[which, t] = send(src.at[rows], pair.at[which, rows], pair_peer)

    def pass_on(which):
        for t in range(2):
            pair_copies[which, t].wait_recv()
            rows = own_rows(t)
            pair_copies[which, t] = send(pair.at[which, rows], pair.at[which, rows], side)

    def forward_finish(e, k, keep_normed):
        def finish(t):
            at = chunk * t + part * low

            def body(i, carry):
                rows = block(i * TILE, TILE)
                place = block(at + i * TILE, TILE)
                stream = hid[k, place].astype(F32)
                branch = total_tile(e, t, rows)
                norm, inv = normalise(stream + branch)
                if keep_normed:
                    normed[k, t, rows] = norm
                    inverse[k, t, rows] = inv
                hid[k + 1, place] = (norm * gain[k : k + 1] + bias[k : k + 1]).astype(BF16)
                return (carry[0] + fold(stream * stream), carry[1] + fold(branch * branch))

            zero = jnp.zeros((8, width), F32)
            squares = tiles(part // TILE, body, (zero, zero))

            @pl.when(high == t)
            def _():
                add_stat(k, whole_sum(squares[0]) * used)
                add_stat(4 + k, whole_sum(squares[1]) * used)

            rows = own_rows(t)
            copy = send(hid.at[k + 1, rows], hid.at[k + 1, rows], side)
            if k == 0:
                to_pair(0, t, hid.at[1])
            return copy

        return finish

    def norm_back_rows(k, t, grad_tile):
        at = chunk * t + part * low

        def body(i, carry):
            rows = block(i * TILE, TILE)
            dy = grad_tile(rows, block(at + i * TILE, TILE))
            norm = normed[k, t, rows]
            result = norm_pull(dy, norm, inverse[k, t, rows], gain[k : k + 1])
            normed[k, t, rows] = result
            dfull[k, block(at + i * TILE, TILE)] = result.astype(BF16)
            return (carry[0] + fold(dy * norm), carry[1] + fold(dy))

        zero = jnp.zeros((8, width), F32)
        terms = tiles(part // TILE, body, (zero, zero))

        @pl.when(high == t)
        def _():
            misc[k : k + 1] += jnp.sum(terms[0], axis=0, keepdims=True)
            misc[4 + k : 5 + k] += jnp.sum(terms[1], axis=0, keepdims=True)

        rows = own_rows(t)
        copy = send(dfull.at[k, rows], dfull.at[k, rows], side)
        if k == 1:
            to_pair(1, t, dfull.at[1])
        return copy

    def marked_total(e, values, during=None):
        ms[e] = values.astype(BF16)
        core = send(ms.at[e], mr.at[e], side)
        core.wait_recv()
        mys[e] = (ms[e].astype(F32) + mr[e].astype(F32)).astype(BF16)
        y = send(mys.at[e], myr.at[e], across)
        if during is not None:
            during()
        y.wait_recv()
        return mys[e].astype(F32) + myr[e].astype(F32)

    def reduce_piece(base, stride, size, paired):
        steps = []
        first, bit = base, lay.bits - 1
        while bit >= 0:
            peer, on = replica_bit(bit)
            keep = first + on * stride
            give = first + (1 - on) * stride
            if not paired:
                xr_at = reduce_piece.xr_at
                reduce_piece.xr_at += size
                copy = send(
                    grads.at[pl.ds(pl.multiple_of(give, 16), size)],
                    xr.at[pl.ds(xr_at, size)],
                    peer,
                )
                yield
                copy.wait_recv()
                step = math.gcd(size, 64)

                def body(i, carry, keep=keep, xr_at=xr_at, step=step):
                    here = pl.ds(pl.multiple_of(keep + i * step, 16), step)
                    there = pl.ds(pl.multiple_of(xr_at + i * step, 16), step)
                    grads[here] = (grads[here].astype(F32) + xr[there].astype(F32)).astype(BF16)
                    return carry

                tiles(size // step, body)
            steps.append((keep, give, size, peer))
            paired = False
            first, bit = keep, bit - 1
            if bit >= 0:
                size = size // 2
                stride = size
        z_at = reduce_piece.z_at
        reduce_piece.z_at += size
        mine = pl.ds(pl.multiple_of(first, 16), size)
        z_rows = pl.ds(z_at, size)
        step = math.gcd(size, 64)
        slot_a, slot_b = slots(), slots()

        def z_copy(kind):
            if kind == "a":
                return remote(
                    grads.at[mine], za.at[z_rows], (inner_of, replica, member), slot_a
                )
            if kind == "b":
                return remote(
                    grads.at[mine], zb.at[z_rows], (other_inner, replica, member), slot_b
                )
            return remote(final.at[mine], final.at[mine], (end_of, replica, member), slot_a)

        steps.reverse()
        gather_slots = [slots() for _ in steps]

        def gather(at, arriving=False):
            keep, give, half, peer = steps[at]
            rows = pl.ds(pl.multiple_of(give if arriving else keep, 16), half)
            return remote(final.at[rows], final.at[rows], peer, gather_slots[at])

        @pl.when(is_end)
        def _():
            z_copy("a").start()

        yield

        @pl.when(is_inner)
        def _():
            z_copy("a").wait_recv()

            def body(i, carry):
                here = pl.ds(pl.multiple_of(first + i * step, 16), step)
                there = pl.ds(pl.multiple_of(z_at + i * step, 16), step)
                grads[here] = (grads[here].astype(F32) + za[there].astype(F32)).astype(BF16)
                return carry

            tiles(size // step, body)
            z_copy("b").start()

        yield

        @pl.when(is_inner)
        def _():
            z_copy("b").wait_recv()

            def body(i, carry):
                here = pl.ds(pl.multiple_of(first + i * step, 16), step)
                there = pl.ds(pl.multiple_of(z_at + i * step, 16), step)
                final[here] = (grads[here].astype(F32) + zb[there].astype(F32)).astype(BF16)
                return carry

            tiles(size // step, body)
            z_copy("c").start()
            gather(0).start()

        yield

        @pl.when(is_end)
        def _():
            z_copy("c").wait_recv()
            gather(0).start()

        yield
        for at in range(len(steps)):
            if at > 0:
                gather(at).start()
                yield
            gather(at, True).wait_recv()
            closing.append((gather(at).wait_send, (gather_slots[at],)))

        def close():
            @pl.when(is_end)
            def _():
                z_copy("a").wait_send()

            @pl.when(is_inner)
            def _():
                z_copy("b").wait_send()
                z_copy("c").wait_send()

        closing.append((close, (slot_a, slot_b)))

    reduce_piece.xr_at = 0
    reduce_piece.z_at = 0
    running = {}
    summed = set()

    def launch(*names):
        for name in names:
            spec = lay.pieces.get(name)
            running[name] = reduce_piece(*spec)
            next(running[name])

    def start(name, task):
        running[name] = task
        next(task)

    def pump(*names):
        settle(KEEP)
        for name in names:
            if name in running:
                try:
                    next(running[name])
                except StopIteration:
                    del running[name]

    def line_gather(view):
        right, left = [slots() for _ in range(3)], [slots() for _ in range(3)]

        def hop(k, to_right, at):
            origin = at - k if to_right else at + k
            target = (section + (1 if to_right else -1), replica, member)
            return remote(view(origin), view(origin), target, (right if to_right else left)[k])

        def sends(k, action):
            @pl.when((section >= k) & (section < SECTIONS - 1))
            def _():
                getattr(hop(k, True, section), action)()

            @pl.when((section + k < SECTIONS) & (section > 0))
            def _():
                getattr(hop(k, False, section), action)()

        def arrivals(k):
            @pl.when(section > k)
            def _():
                hop(k, True, section - 1).wait_recv()

            @pl.when(section + k < SECTIONS - 1)
            def _():
                hop(k, False, section + 1).wait_recv()

        for k in range(SECTIONS - 1):
            sends(k, "start")
            closing.append((functools.partial(sends, k, "wait_send"), (right[k], left[k])))
            yield
            arrivals(k)

    pl.semaphore_wait(barrier, len(peers))
    mine = block(member * part, part)
    to_across = send(x_in.at[section], hid.at[0, mine], across)
    to_side = send(x_in.at[section], hid.at[0, mine], side)
    loads["x"].wait()
    hits[...] = jnp.where(
        lax.broadcasted_iota(jnp.int32, hits.shape, 0) == where[0:1, 0 : hits.shape[1]], 1.0, 0.0
    ).astype(BF16)
    loads["qkv"].wait()

    def project(at):
        rows = block(at, part)
        for j in range(3):
            qkv[j, rows] = dot_lanes(hid[0, rows], wqkv[j]).astype(BF16)

    project(member * part)
    to_side.wait_recv()
    project(side[2] * part)
    to_across.wait_recv()
    theirs = block(across[2] * part, part)
    onward = send(hid.at[0, theirs], hid.at[0, theirs], side)
    project(across[2] * part)
    onward.wait_recv()
    project(lax.rem(side[2] + 2, GROUP) * part)
    loads["ao"].wait()

    def attention_work(t):
        rows = pl.ds(chunk * t, chunk)
        mixture = jnp.zeros((chunk, hw), F32)
        for i in range(local_heads):
            if t == 1 and i == 1:
                cross(0, 0)
            scores = dot_lanes(qkv[0, rows] * head_low[i], qkv[1]) * scale
            top = jnp.max(scores, axis=-1, keepdims=True)
            powers = jnp.exp(scores - top)
            chances = powers * (1.0 / jnp.sum(powers, axis=-1, keepdims=True))
            probs[i, rows] = chances
            mixture = mixture + jnp.where(head_lanes[i], dot(chances.astype(BF16), qkv[2]), 0.0)
        mix[rows] = mixture.astype(BF16)
        return lambda core: dot(mix[half_rows(t, core)], wao[...])

    begin(0, 0, attention_work)
    begin(0, 1, attention_work)
    cross(0, 1)
    loads["up"].wait()
    loads["down"].wait()

    def ffn_forward(layer, src, rows, units_here, slope_here=None):
        def body(i, carry):
            lanes = block(i * LANES, LANES)
            unit, steep = gelu_parts(dot(src[rows], wup[layer, :, lanes]))
            units_here[:, lanes] = unit.astype(BF16)
            if slope_here is not None:
                slope_here[:, lanes] = steep
            return carry

        tiles(lay.hidden // LANES, body)

    def ffn0_work(t):
        for core in (low, 1 - low):
            if core is not low:
                gathered[0, t].wait_recv()
            rows = half_rows(t, core)
            ffn_forward(0, hid.at[1], rows, units.at[rows], slope.at[rows])
        return lambda core: dot(units[half_rows(t, core)], wdown[0])

    for name in ("gain", "bias"):
        loads[name].wait()
    attention_finish = forward_finish(0, 0, True)
    end(0, 0, attention_finish)
    begin(1, 0, ffn0_work)
    end(0, 1, attention_finish)
    cross(1, 0)
    begin(1, 1, ffn0_work)
    cross(1, 1)

    loads["cin"].wait()
    loads["co"].wait()
    edge = jnp.zeros((PAD, hw), F32)
    for buffer in (gated, dconv):
        buffer[0:PAD] = edge
        buffer[PAD + lay.seq : 2 * PAD + lay.seq] = edge

    def conv_gates(t):
        for core in (low, 1 - low):
            if core is not low:
                gathered[1, t].wait_recv()
            rows = half_rows(t, core)
            value_here = dot_lanes(hid[2, rows], wcin[0])
            sig_here = jax.nn.sigmoid(dot_lanes(hid[2, rows], wcin[1]))
            value[rows] = value_here
            sig[rows] = sig_here
            place = pl.ds(pl.multiple_of(PAD + chunk * t + part * core, 8), part)
            gated[place] = value_here * sig_here

    ffn0_finish = forward_finish(1, 1, True)
    pass_on(0)
    end(1, 0, ffn0_finish)
    conv_gates(0)
    end(1, 1, ffn0_finish)
    conv_gates(1)
    tap_tile = 64

    def taps(i, carry):
        total = jnp.zeros((tap_tile, hw), F32)
        window = gated[pl.ds(pl.multiple_of(i * tap_tile, 8), tap_tile + 2 * PAD)]
        for j in range(TAPS):
            at = PAD - MARGIN + j
            total = total + tap_weight[j : j + 1] * window[at : at + tap_tile]
        conv[block(i * tap_tile, tap_tile)] = total.astype(BF16)
        return carry

    tiles(lay.seq // tap_tile, taps)

    spots = hits[...]
    conv_marked = dot_rows(spots, conv[...]).astype(BF16)
    stream = dot_rows(spots, hid[2])

    def pair_up(t):
        pair_copies[0, t].wait_recv()
        rows = pl.ds(chunk * t, chunk)
        unit, slope_here = gelu_parts(dot(pair[0, rows], wup[0, :, half_lanes]))
        punits[rows] = unit.astype(BF16)
        pslope[rows] = slope_here


    def conv_work(t):
        return lambda core: dot(conv[half_rows(t, core)], wco[...])

    def ffn1_work(t):
        gathered[5, t].wait_recv()
        ffn_forward(1, hid.at[3], pl.ds(chunk * t, chunk), last_units)
        return lambda core: dot(last_units[block(part * core, part)], wdown[1])

    def layer_output():
        last_finish = forward_finish(5, 2, False)
        begin(5, 0, conv_work)
        begin(5, 1, conv_work)
        cross(5, 0)
        yield
        cross(5, 1)
        yield
        end(5, 0, last_finish)
        yield
        end(5, 1, last_finish)
        yield
        begin(6, 0, ffn1_work)
        yield
        begin(6, 1, ffn1_work)
        for t in range(2):
            sums_across(6, t, core_copies[6, t], start=False)
        last = send_half(6)
        yield
        last.wait_recv()

        def layer_body(i, carry):
            rows = block(i * TILE, TILE)
            stream = hid[3, block(member * part + i * TILE, TILE)].astype(F32)
            branch = total_tile(6, high, rows)
            norm, _ = normalise(stream + branch)
            result = (norm * gain[3:4] + bias[3:4]) * used
            layer_rows[section, rows] = result.astype(BF16)
            return (carry[0] + fold(stream * stream), carry[1] + fold(branch * branch))

        zero = jnp.zeros((8, width), F32)
        squares = tiles(part // TILE, layer_body, (zero, zero))
        add_stat(3, whole_sum(squares[0]) * used)
        add_stat(7, whole_sum(squares[1]) * used)
        summed.add("rows")
        yield from line_gather(lambda at: layer_rows.at[at])

    branch = marked_total(
        0, dot(conv_marked, wco[...]), lambda: start("lo", layer_output())
    )
    norm2, inv2 = normalise(stream + branch)
    mnorm[0] = norm2
    mh[...] = (norm2 * gain[2:3] + bias[2:3]).astype(BF16)

    def pick_cotangent():
        loads["out_grads"].wait()
        count = out_grads.shape[0]
        slot = lax.broadcasted_iota(jnp.int32, (1, out_grads.shape[1], 1), 1)
        mine = jnp.where(slot == section, used, 0.0)
        cotangent[...] = jnp.zeros_like(cotangent)
        cotangent[0:count] = jnp.sum(out_grads[...].astype(F32) * mine, axis=1)

    def marked_up(i, carry):
        lanes = block(i * LANES, LANES)
        unit, slope_here = gelu_parts(dot(mh[...], wup[1, :, lanes]))
        munits[:, lanes] = unit.astype(BF16)
        mslope[:, lanes] = slope_here
        return carry

    tiles(lay.hidden // LANES, marked_up)

    def beside_units():
        pump("lo")
        pick_cotangent()
        pair_up(0)

    branch = marked_total(1, dot(munits[...], wdown[1]), beside_units)
    norm3, inv3 = normalise(mh[...].astype(F32) + branch)
    once = jnp.where(member == 0, 1.0, 0.0).astype(F32)
    dy = cotangent[...]
    misc[3:4] += once * jnp.sum(dy * norm3, axis=0, keepdims=True)
    misc[7:8] += once * jnp.sum(dy, axis=0, keepdims=True)
    dz3 = norm_pull(dy, norm3, inv3, gain[3:4])
    cotangent[...] = dz3
    df3 = dz3.astype(BF16)

    per_section = lay.dp * marked
    here = pl.ds(pl.multiple_of(section * per_section + replica * marked, 16), marked)
    factors[0, here] = mh[...]
    factors[1, here] = df3

    def spread_factors():
        copies = [
            send(factors.at[low, here], factors.at[low, here], replica_peer(by))
            for by in range(1, lay.dp)
        ]
        yield
        for copy in copies:
            copy.wait_recv()
        def of_section(at):
            return factors.at[low, pl.ds(pl.multiple_of(at * per_section, 16), per_section)]

        yield from line_gather(of_section)
        slot = slots()
        send(factors.at[low], factors.at[low], side, slot)
        yield
        remote(factors.at[1 - low], factors.at[1 - low], side, slot).wait_recv()

    start("fa", spread_factors())

    def marked_down(i, carry):
        lanes = block(i * LANES, LANES)
        grad_units = dot_lanes(factors[1, here], wdown[1, lanes])
        munits[:, lanes] = (grad_units * mslope[:, lanes]).astype(BF16)
        return carry

    tiles(lay.hidden // LANES, marked_down)
    def beside_down():
        pump("lo")
        pump("lo")
        pair_up(1)

    dy = cotangent[...] + marked_total(2, dot_lanes(munits[...], wup[1]), beside_down)
    pump("fa")
    norm2 = mnorm[0]
    misc[2:3] += once * jnp.sum(dy * norm2, axis=0, keepdims=True)
    misc[6:7] += once * jnp.sum(dy, axis=0, keepdims=True)
    dz2 = norm_pull(dy, norm2, inv2, gain[2:3])
    dz2_terms = two_terms(dz2)
    df2 = dz2.astype(BF16)

    def spread(rows, terms):
        where_rows = hits[rows]
        return dot(where_rows, terms[0]) + dot(where_rows, terms[1])

    dconv_terms = two_terms(dot_lanes(df2, wco[...]))
    dconv[pl.ds(PAD, lay.seq)] = spread(pl.ds(0, lay.seq), dconv_terms)

    def taps_back(i, carry):
        total = jnp.zeros((tap_tile, hw), F32)
        place = pl.ds(pl.multiple_of(i * tap_tile, 8), tap_tile + 2 * PAD)
        window = dconv[place]
        around = gated[place]
        middle = window[PAD : PAD + tap_tile]
        sums = []
        for j in range(TAPS):
            at = PAD + MARGIN - j
            total = total + tap_weight[j : j + 1] * window[at : at + tap_tile]
            at = PAD - MARGIN + j
            sums.append(jnp.sum(around[at : at + tap_tile] * middle, axis=0, keepdims=True))
        rows = block(i * tap_tile, tap_tile)
        s = sig[rows]
        by_value = total * s
        dgates[0, rows] = by_value.astype(BF16)
        dgates[1, rows] = (by_value * value[rows] * (1.0 - s)).astype(BF16)
        sums.append(jnp.zeros((1, hw), F32))
        return carry + jnp.concatenate(sums, axis=0)

    def conv_back_work(t):
        def product(core):
            rows = half_rows(t, core)
            return dot(dgates[0, rows], wcin[0]) + dot(dgates[1, rows], wcin[1])

        return product

    half_tiles = chunk // tap_tile
    kernel_rows = lax.fori_loop(0, half_tiles, taps_back, jnp.zeros((8, hw), F32))
    begin(2, 0, conv_back_work)
    kernel_rows = lax.fori_loop(half_tiles, 2 * half_tiles, taps_back, kernel_rows)
    cross(2, 0)
    begin(2, 1, conv_back_work)
    kernel_rows = kernel_rows * tap_on[...]
    grads[pl.ds(lay.kernel_at, lay.up_at - lay.kernel_at)] = jnp.zeros(
        (lay.up_at - lay.kernel_at, width), BF16
    )
    grads[pl.ds(lay.kernel_at, 16), 0:hw] = jnp.concatenate(
        [kernel_rows, jnp.zeros((8, hw), F32)], axis=0
    ).astype(BF16)

    def conv_back_finish(t):
        def grad_tile(rows, place):
            return total_tile(2, t, rows) + spread(place, dz2_terms)

        return norm_back_rows(1, t, grad_tile)

    def ffn0_back_work(t):
        for core in (low, 1 - low):
            if core is not low:
                gathered[2, t].wait_recv()
            rows = half_rows(t, core)

            def body(i, carry, rows=rows):
                lanes = block(i * LANES, LANES)
                grad_units = dot_lanes(dfull[1, rows], wdown[0, lanes])
                dbefore[rows, lanes] = (grad_units * slope[rows, lanes]).astype(BF16)
                return carry

            tiles(lay.hidden // LANES, body)
        return lambda core: dot_lanes(dbefore[half_rows(t, core)], wup[0])

    def ffn0_back_finish(t):
        return norm_back_rows(
            0, t, lambda rows, place: normed[1, t, rows] + total_tile(3, t, rows)
        )

    up_rows = pl.ds(pl.multiple_of(lay.up_at + pair_on * halfway, 16), halfway)
    down_rows = pl.ds(pl.multiple_of(lay.down_at + pair_on * halfway, 16), halfway)

    def own_weights():
        left = dbefore[:, half_lanes]
        for q in range(2):
            lanes = pl.ds(q * halfway, halfway)
            grads[up_rows, lanes] = dot_rows(hid[1, :, lanes], left).astype(BF16)
        grads[down_rows] = dot_rows(units[:, half_lanes], dfull[1]).astype(BF16)

    def pair_weights():
        for t in range(2):
            pair_copies[1, t].wait_recv()
            rows = pl.ds(chunk * t, chunk)
            grad_units = dot_lanes(pair[1, rows], wdown[0, half_lanes])
            pdbefore[rows] = (grad_units * pslope[rows]).astype(BF16)
        left = pdbefore[...]
        for q in range(2):
            lanes = pl.ds(q * halfway, halfway)
            total = grads[up_rows, lanes].astype(F32) + dot_rows(pair[0, :, lanes], left)
            grads[up_rows, lanes] = total.astype(BF16)
        launch(*lay.groups["u"])
        total = grads[down_rows].astype(F32) + dot_rows(punits[...], pair[1])
        grads[down_rows] = total.astype(BF16)
        launch(*lay.groups["d"])

    def attention_back_work(t):
        def product(core):
            rows = half_rows(t, core)
            return (
                dot(dqkv[0, rows], wqkv[0])
                + dot(dqkv[1, rows], wqkv[1])
                + dot(dqkv[2, rows], wqkv[2])
            )

        return product

    def attention_back_rows(t):
        gathered[3, t].wait_recv()
        rows = pl.ds(chunk * t, chunk)
        dmix[rows] = dot_lanes(dfull[0, rows], wao[...]).astype(BF16)
        grad_queries = jnp.zeros((chunk, hw), F32)
        for i in range(local_heads):
            chances = probs[i, rows]
            grad_chances = dot_lanes(dmix[rows] * head_low[i], qkv[2])
            grad_scores = chances * (
                grad_chances - jnp.sum(grad_chances * chances, axis=-1, keepdims=True)
            )
            grad_scores = grad_scores.astype(BF16)
            on = head_lanes[i]
            grad_queries = grad_queries + jnp.where(on, dot(grad_scores, qkv[1]), 0.0)
            dkv[0] += jnp.where(on, dot_rows(grad_scores, qkv[0, rows]), 0.0)
            dkv[1] += jnp.where(on, dot_rows(chances.astype(BF16), dmix[rows]), 0.0)
        dqkv[0, rows] = (grad_queries * scale).astype(BF16)

    waits = {}

    def backward():
        cross(2, 1)
        for j in range(2):
            grads[pl.ds(lay.conv_at + j * hw, hw)] = dot_rows(dgates[j], hid[2]).astype(BF16)
        grads[pl.ds(lay.conv_at + 2 * hw, hw)] = dot_rows(conv_marked, df2).astype(BF16)
        launch(*lay.groups["c"])
        yield
        end(2, 0, conv_back_finish)
        begin(3, 0, ffn0_back_work)
        yield
        end(2, 1, conv_back_finish)
        cross(3, 0)
        begin(3, 1, ffn0_back_work)
        cross(3, 1)
        yield
        end(3, 0, ffn0_back_finish)
        yield
        end(3, 1, ffn0_back_finish)
        summed.add("norms")
        yield
        dkv[...] = jnp.zeros_like(dkv)
        attention_back_rows(0)
        yield
        attention_back_rows(1)
        dqkv[1] = (dkv[0] * scale).astype(BF16)
        dqkv[2] = dkv[1].astype(BF16)
        for j in range(3):
            grads[pl.ds(lay.attn_at + j * hw, hw)] = dot_rows(dqkv[j], hid[0]).astype(BF16)
        grads[pl.ds(lay.attn_at + 3 * hw, hw)] = dot_rows(mix[...], dfull[0]).astype(BF16)
        launch(*lay.groups["a"])
        for t in range(2):
            begin(4, t, attention_back_work)
        for t in range(2):
            sums_across(4, t, core_copies[4, t], start=False)
        waits["input"] = send_half(4)

    def feed_forward_weights():
        own_weights()
        yield
        pass_on(1)
        yield
        pair_weights()

    def input_body(i, carry):
        rows = block(i * TILE, TILE)
        total = total_tile(4, high, rows)
        input_rows[section, rows] = (normed[0, high, rows] + total).astype(BF16)
        return carry

    def input_gradient():
        waits["input"].wait_recv()
        tiles(part // TILE, input_body)
        yield from line_gather(lambda at: input_rows.at[at])

    group_rows = GROUP * marked
    groups = SECTIONS * per_section // group_rows

    def last_block():
        assert not {"main", "pw", "fa"} & set(running)
        for group in range(groups):
            rows = pl.ds(group * group_rows, group_rows)

            def recompute(j, carry, rows=rows):
                lanes = block(j * LANES, LANES)
                unit, slope_here = gelu_parts(dot(factors[0, rows], wup[1, :, lanes]))
                units[0:group_rows, lanes] = unit.astype(BF16)
                grad_units = dot_lanes(factors[1, rows], wdown[1, lanes])
                dbefore[0:group_rows, lanes] = (grad_units * slope_here).astype(BF16)
                return carry

            tiles(lay.hidden // LANES, recompute)

            def last_weights(i, carry, rows=rows, group=group):
                lanes = block(i * LANES, LANES)
                by_up = dot_rows(factors[0, rows, lanes], dbefore[0:group_rows])
                by_down = dot_rows(units[0:group_rows, lanes], factors[1, rows])
                wide, rest = probs.shape[2], width - probs.shape[2]
                held = [
                    (
                        probs.at[i, pl.ds(j * LANES, LANES)],
                        slope.at[pl.ds(j * LANES, LANES), block(i * rest, rest)],
                    )
                    for j in range(2)
                ]
                if group > 0:
                    by_up = by_up + jnp.concatenate([held[0][0][...], held[0][1][...]], axis=1)
                    by_down = by_down + jnp.concatenate([held[1][0][...], held[1][1][...]], axis=1)
                if group < groups - 1:
                    for (left, right), total in zip(held, (by_up, by_down)):
                        left[...] = total[:, :wide]
                        right[...] = total[:, wide:]
                else:
                    at = pl.multiple_of(i * LANES, LANES)
                    final[pl.ds(lay.up1_at + at, LANES)] = by_up.astype(BF16)
                    final[pl.ds(lay.down1_at + at, LANES)] = by_down.astype(BF16)
                return carry

            tiles(width // LANES, last_weights)
            yield

    def small_sums():
        assert summed >= {"norms", "rows"}
        hops = [side, across] + [replica_bit(bit)[0] for bit in range(lay.bits)]
        for at, peer in enumerate(hops):
            misc_in[2 * at] = misc[...]
            copy = send(misc_in.at[2 * at], misc_in.at[2 * at + 1], peer)
            yield
            copy.wait_recv()
            misc[...] = misc_in[2 * at] + misc_in[2 * at + 1]
        at = 2 * len(hops)
        slot_a, slot_b = slots(), slots()
        to_inner = remote(misc_in.at[at], misc_in.at[at + 1], (inner_of, replica, member), slot_a)
        to_other = remote(
            misc_in.at[at + 2], misc_in.at[at + 3], (other_inner, replica, member), slot_b
        )
        to_end = remote(misc_out, misc_out, (end_of, replica, member), slot_a)

        @pl.when(is_end)
        def _():
            misc_in[at] = misc[...]
            to_inner.start()

        yield

        @pl.when(is_inner)
        def _():
            to_inner.wait_recv()
            misc_in[at + 2] = misc[...] + misc_in[at + 1]
            to_other.start()

        yield

        @pl.when(is_inner)
        def _():
            to_other.wait_recv()
            misc_out[...] = misc_in[at + 2] + misc_in[at + 3]
            to_end.start()

        yield

        @pl.when(is_end)
        def _():
            to_end.wait_recv()
            to_inner.wait_send()

        @pl.when(is_inner)
        def _():
            to_other.wait_send()
            to_end.wait_send()

    later = {
        "main": backward,
        "pw": feed_forward_weights,
        "ig": input_gradient,
        "w1": last_block,
        "ms": small_sums,
    }
    for name in TAIL:
        if name in later:
            start(name, later.pop(name)())
        else:
            pump(name)
    assert not later
    while running:
        pump(*list(running))
    closing.extend(leaving.values())
    settle()
    assert counter[0] <= lay.arrivals and counter[1] <= lay.departures


def widen_kernel(
    lay,
    final,
    input_rows,
    layer_rows,
    misc,
    plan,
    layer_out,
    input_grad,
    qkv,
    out,
    cin,
    cout,
    up,
    down,
    kernel,
    gains,
    biases,
    rms,
    wide,
    wide_input,
    store_sem,
):
    hw, width, hidden = lay.heads_width, lay.width, lay.hidden
    blocks = []

    def cover(start, rows, target, step):
        for at in range(0, rows, step):
            blocks.append((start + at, step, target.at[pl.ds(at, step)]))

    for layer, (up_at, down_at) in enumerate(
        ((lay.up_at, lay.down_at), (lay.up1_at, lay.down1_at))
    ):
        cover(up_at, width, up.at[layer], width // 2)
        cover(down_at, hidden, down.at[layer], hidden // 2)
    for j in range(3):
        cover(lay.attn_at + j * hw, hw, qkv.at[j], hw)
    cover(lay.attn_at + 3 * hw, hw, out, hw)
    for j in range(2):
        cover(lay.conv_at + j * hw, hw, cin.at[j], hw)
    cover(lay.conv_at + 2 * hw, hw, cout, hw)

    def store(at):
        start, rows, target = blocks[at]
        return pltpu.make_async_copy(wide.at[pl.ds(start, rows)], target, store_sem.at[at])

    extra = len(blocks)
    inputs_out = pltpu.make_async_copy(wide_input, input_grad, store_sem.at[extra])
    layer_done = pltpu.make_async_copy(layer_rows, layer_out, store_sem.at[extra + 1])
    layer_done.start()
    gains[...] = misc[0:4]
    biases[...] = misc[4:8]
    row = lax.broadcasted_iota(jnp.int32, rms.shape, 0)
    counts = jnp.zeros(rms.shape, F32)
    for r in range(rms.shape[0]):
        total = jnp.float32(lay.micro)
        for i in range(lay.micro):
            total = total + jnp.where(plan[r, i, 1] >= 0, 1.0, 0.0).astype(F32)
        counts = jnp.where(row == r, total, counts)
    rms[...] = jnp.sqrt(misc[8 : 8 + rms.shape[0], 0:8] / (counts * (lay.seq * width)))
    half = width // 2
    for at, (start, rows, _) in enumerate(blocks):
        def body(i, carry, start=start, at=at):
            here = pl.ds(pl.multiple_of(start + i * 32, 16), 32)
            if at >= 2:
                wide[here] = final[here].astype(F32)
            else:
                for q in range(2):
                    there = pl.ds(pl.multiple_of(lay.up_at + q * half + i * 32, 16), 32)
                    wide[here, q * half : (q + 1) * half] = final[
                        there, at * half : (at + 1) * half
                    ].astype(F32)
            return carry

        lax.fori_loop(0, rows // 32, body, 0)
        store(at).start()
    for slot in range(input_rows.shape[0]):
        wide_input[slot] = input_rows[slot].astype(F32)
    inputs_out.start()
    taps = final[pl.ds(lay.kernel_at, 16)].astype(F32)
    kernel[...] = taps[0:TAPS, 0:hw]
    for at in range(len(blocks)):
        store(at).wait()
    inputs_out.wait()
    layer_done.wait()


def on_device(
    inputs,
    attn_qkv,
    attn_out,
    conv_in,
    conv_kernel,
    conv_out,
    ffn_up,
    ffn_down,
    norm_gain,
    norm_bias,
    kernel_half,
    batch_plan,
    masked_positions,
    out_grad,
):
    section = lax.axis_index("section")
    replica = lax.axis_index("dp")
    dp = lax.axis_size("dp")
    slot_count, part, width = inputs.shape
    micro_count = batch_plan.shape[1]
    count = masked_positions.shape[1]
    marked = round_up(count, 16)
    assert slot_count == SECTIONS == lax.axis_size("section") and lax.axis_size("mp") == GROUP
    hw = attn_out.shape[0]
    hidden = ffn_up.shape[2]
    lay = Layout(dp, micro_count, part * GROUP, width, hw, hidden, marked)
    assert hidden == width and width % LANES == 0 and hw % HEAD == 0

    seq, chunk = lay.seq, lay.chunk
    any_spec = pl.BlockSpec(memory_space=pl.ANY)
    vmem_spec = pl.BlockSpec(memory_space=pltpu.VMEM)
    hops = 2 + lay.bits
    all_marked = SECTIONS * dp * marked
    scratch = [
        pltpu.VMEM((8, hw), F32),
        pltpu.VMEM((8, hw), F32),
        pltpu.VMEM((8, marked), jnp.int32),
        pltpu.VMEM(norm_gain.shape, F32),
        pltpu.VMEM(norm_bias.shape, F32),
        pltpu.VMEM((marked, width), F32),
        pltpu.VMEM((count, slot_count, width), BF16),
        pltpu.VMEM((3, hw, width), BF16),
        pltpu.VMEM(attn_out.shape, BF16),
        pltpu.VMEM((2, hw, width), BF16),
        pltpu.VMEM(conv_out.shape, BF16),
        pltpu.VMEM(ffn_up.shape, BF16),
        pltpu.VMEM(ffn_down.shape, BF16),
        pltpu.VMEM((4, seq, width), BF16),
        pltpu.VMEM((2, seq, width), BF16),
        pltpu.VMEM((2, 2, part, width), F32),
        pltpu.VMEM((2, 2, part, 1), F32),
        pltpu.VMEM((3, seq, hw), BF16),
        pltpu.VMEM((hw // HEAD, seq, seq), F32),
        pltpu.VMEM((seq, hw), BF16),
        pltpu.VMEM((seq, hw), BF16),
        pltpu.VMEM((3, seq, hw), BF16),
        pltpu.VMEM((2, seq, hw), F32),
        pltpu.VMEM((seq, hidden), BF16),
        pltpu.VMEM((seq, hidden), F32),
        pltpu.VMEM((seq, hidden), BF16),
        pltpu.VMEM((chunk, hidden), BF16),
        pltpu.VMEM((seq, hw), F32),
        pltpu.VMEM((seq, hw), F32),
        pltpu.VMEM((seq + 2 * PAD, hw), F32),
        pltpu.VMEM((seq, hw), BF16),
        pltpu.VMEM((seq + 2 * PAD, hw), F32),
        pltpu.VMEM((2, seq, hw), BF16),
        pltpu.VMEM((seq, marked), BF16),
        pltpu.VMEM((marked, width), BF16),
        pltpu.VMEM((1, marked, width), F32),
        pltpu.VMEM((marked, hidden), F32),
        pltpu.VMEM((marked, hidden), BF16),
        pltpu.VMEM((4, 2, part, width), BF16),
        pltpu.VMEM((4, 2, part, width), BF16),
        pltpu.VMEM((4, 2, part, width), BF16),
        pltpu.VMEM((4, 2, part, width), BF16),
        pltpu.VMEM((3, marked, width), BF16),
        pltpu.VMEM((3, marked, width), BF16),
        pltpu.VMEM((3, marked, width), BF16),
        pltpu.VMEM((3, marked, width), BF16),
        pltpu.VMEM((lay.rows, width), BF16),
        pltpu.VMEM((lay.xr_rows, width), BF16),
        pltpu.VMEM((lay.z_rows, width), BF16),
        pltpu.VMEM((lay.z_rows, width), BF16),
        pltpu.VMEM((2, all_marked, width), BF16),
        pltpu.VMEM((2, seq, width), BF16),
        pltpu.VMEM((seq, hidden // 2), BF16),
        pltpu.VMEM((seq, hidden // 2), F32),
        pltpu.VMEM((seq, hidden // 2), BF16),
        pltpu.VMEM((lay.misc_rows, width), F32),
        pltpu.VMEM((2 * hops + 4, lay.misc_rows, width), F32),
        pltpu.SemaphoreType.DMA((10,)),
        pltpu.SemaphoreType.DMA((lay.departures,)),
        pltpu.SemaphoreType.DMA((lay.arrivals,)),
    ]
    smem_spec = pl.BlockSpec(memory_space=pltpu.SMEM)
    final, layer_rows, input_rows, misc = pl.pallas_call(
        functools.partial(main_kernel, lay),
        out_shape=(
            pltpu.VMEM((lay.all_rows, width), BF16),
            pltpu.VMEM((slot_count, part, width), BF16),
            pltpu.VMEM((slot_count, part, width), BF16),
            pltpu.VMEM((lay.misc_rows, width), F32),
        ),
        in_specs=[any_spec] * 9 + [vmem_spec] * 2 + [any_spec] + [smem_spec] * 2,
        out_specs=(vmem_spec,) * 4,
        scratch_shapes=scratch,
        compiler_params=pltpu.CompilerParams(
            collective_id=0, has_side_effects=True, vmem_limit_bytes=VMEM_BYTES
        ),
        name="layers",
    )(
        inputs,
        jnp.swapaxes(attn_qkv, 1, 2),
        attn_out,
        jnp.swapaxes(conv_in, 1, 2),
        conv_out,
        ffn_up,
        ffn_down,
        norm_gain,
        norm_bias,
        conv_kernel,
        masked_positions,
        jnp.swapaxes(out_grad, 0, 1),
        kernel_half,
        batch_plan,
    )
    shapes = [
        (slot_count, part, width),
        (3, hw, width),
        (hw, width),
        (2, hw, width),
        (hw, width),
        (2, width, hidden),
        (2, hidden, width),
        (TAPS, hw),
        (4, width),
        (4, width),
        (dp, 8),
    ]
    widened = pl.pallas_call(
        functools.partial(widen_kernel, lay),
        out_shape=(jax.ShapeDtypeStruct(shapes[0], BF16),)
        + tuple(jax.ShapeDtypeStruct(shape, F32) for shape in shapes),
        in_specs=[vmem_spec] * 4 + [smem_spec],
        out_specs=(any_spec,) * 8 + (vmem_spec,) * 4,
        scratch_shapes=[
            pltpu.VMEM((lay.all_rows, width), F32),
            pltpu.VMEM((slot_count, part, width), F32),
            pltpu.SemaphoreType.DMA((17,)),
        ],
        compiler_params=pltpu.CompilerParams(vmem_limit_bytes=VMEM_BYTES),
        name="widen",
    )(
        *[
            pltpu.with_memory_space_constraint(result, pltpu.VMEM)
            for result in (final, input_rows, layer_rows, misc)
        ],
        batch_plan,
    )
    (layer_out, input_grad, qkv, out, cin, cout, up, down, kernel, gains, biases, rms) = widened
    return (
        layer_out,
        input_grad,
        jnp.swapaxes(qkv, 1, 2),
        out,
        jnp.swapaxes(cin, 1, 2),
        kernel,
        cout,
        up,
        down,
        gains,
        biases,
        rms,
    )


def solution(mesh):
    return jax.shard_map(
        on_device,
        mesh=mesh,
        in_specs=(
            P("dp", "mp", None),
            P(None, None, "mp"),
            P("mp", None),
            P(None, None, "mp"),
            P(None, "mp"),
            P("mp", None),
            P(None, None, "mp"),
            P(None, "mp", None),
            P(),
            P(),
            P(),
            P(),
            P("dp", None),
            P("dp", None, None),
        ),
        out_specs=(
            P("dp", "mp", None),
            P("dp", "mp", None),
            P(None, None, "mp"),
            P("mp", None),
            P(None, None, "mp"),
            P(None, "mp"),
            P("mp", None),
            P(None, None, "mp"),
            P(None, "mp", None),
            P(),
            P(),
            P(),
        ),
        check_vma=False,
    )
```

```python
import functools
import math

import jax
import jax.numpy as jnp
from jax import lax
from jax.experimental import pallas as pl
from jax.experimental.pallas import tpu as pltpu
from jax.sharding import PartitionSpec as P

HEAD = 64
TAPS = 7
MARGIN = TAPS // 2
EPSILON = 1e-05
SECTIONS = 4
GROUP = 4
PAD = 8
TILE = 32
VMEM_BYTES = 55 * 2**20 + 2**17
SETS = (0, 1, 0, 1, 2, 2, 3)
LANES = 256

KEEP = 12
C_CUT, U_CUT, D_CUT, A_CUT = (2, 1, 2), (1, 1, 2, 2), (2, 2, 2), (2, 2, 1, 1)
TAIL = (
    "main", "fa", "lo", "lo", "c0", "fa", "main", "c1", "c0", "lo", "c2", "fa", "fa", "main", "c0",
    "c1", "pw", "main", "lo", "pw", "c2", "pw", "c0", "c1", "main", "main", "u0", "lo", "main",
    "c0", "c2", "u0", "c1", "u1", "lo", "u2", "ms", "a0", "u3", "u1", "ms", "d0", "u2", "a1", "ig",
    "a2", "c2", "u0", "u1", "a3", "d1", "u3", "ms", "c1", "u2", "d2", "d0", "a0", "a1", "d1", "d2",
    "a2", "a3", "a0", "a1", "a2", "a3", "c2", "ig", "u0", "u1", "u3", "ms", "ms", "d0", "u2", "w1",
    "d1", "u3", "d0", "d2", "w1", "a0", "d1", "a1", "d2", "a2", "a0", "a3", "a1", "ig", "a2", "ig",
    "ms", "a3", "ms", "w1",
)

F32 = jnp.float32
BF16 = jnp.bfloat16
MESH = pl.DeviceIdType.MESH


def dot(left, right):
    return jnp.dot(left, right, preferred_element_type=F32)


def dot_lanes(left, right):
    return lax.dot_general(left, right, (((1,), (1,)), ((), ())), preferred_element_type=F32)


def dot_rows(left, right):
    return lax.dot_general(left, right, (((0,), (0,)), ((), ())), preferred_element_type=F32)


def round_up(value, step):
    return (value + step - 1) // step * step


def normalise(summed):
    centre = summed - jnp.mean(summed, axis=-1, keepdims=True)
    variance = jnp.mean(centre * centre, axis=-1, keepdims=True)
    inverse = lax.rsqrt(variance + EPSILON)
    return centre * inverse, inverse


def norm_pull(grad_out, normed, inverse, gain_row):
    scaled = grad_out * gain_row
    first = jnp.mean(scaled, axis=-1, keepdims=True)
    second = jnp.mean(scaled * normed, axis=-1, keepdims=True)
    return inverse * (scaled - first - normed * second)


def gelu_parts(before):
    cdf = 0.5 * (1.0 + lax.erf(before * math.sqrt(0.5)))
    slope = cdf + before * jnp.exp(-0.5 * before * before) * (1.0 / math.sqrt(2.0 * math.pi))
    return before * cdf, slope


def two_terms(values):
    high = values.astype(BF16)
    return high, (values - high.astype(F32)).astype(BF16)


def fold(rows):
    count, width = rows.shape
    return jnp.sum(rows.reshape(count // 8, 8, width), axis=0)


def whole_sum(values):
    return jnp.sum(values, axis=(0, 1), keepdims=True)


class Layout:
    def __init__(self, dp, micro, seq, width, heads_width, hidden, marked):
        self.dp, self.micro, self.seq, self.width = dp, micro, seq, width
        self.heads_width, self.hidden = heads_width, hidden
        self.marked = marked
        self.part = seq // GROUP
        self.chunk = 2 * self.part
        unit = 16 * dp
        conv_rows = round_up(3 * heads_width + 16, max(unit, 128))
        self.conv_at, at = 0, conv_rows
        self.up_at, at = at, at + width
        self.down_at, at = at, at + hidden
        self.attn_at, at = at, at + 4 * heads_width
        self.rows = at
        self.up1_at, at = at, at + width
        self.down1_at, at = at, at + hidden
        self.all_rows = at
        self.kernel_at = self.conv_at + 3 * heads_width
        half, step = width // 2, width // 6
        self.pieces, self.groups = {}, {}

        def cut(name, start, stride, sizes):
            at = start
            self.groups[name] = []
            for i, size in enumerate(sizes):
                size = step * size // 2
                key = name + str(i)
                self.pieces[key] = (at, stride or size, size, stride > 0)
                self.groups[name].append(key)
                at += size if stride else 2 * size

        cut("c", self.conv_at, 0, C_CUT)
        cut("u", self.up_at, half, U_CUT)
        cut("d", self.down_at, half, D_CUT)
        cut("a", self.attn_at, 0, A_CUT)
        self.xr_rows = self.z_rows = 0
        for _, _, size, paired in self.pieces.values():
            least = size // (dp // 2)
            assert least * (dp // 2) == size and least % 16 == 0
            self.xr_rows += size - least + (0 if paired else size)
            self.z_rows += least
        self.bits = dp.bit_length() - 1
        assert dp == 1 << self.bits and dp <= 8
        self.misc_rows = 16
        self.arrivals = 127 + (2 * len(self.pieces) + 1) * (self.bits - 1) + dp - 2
        self.departures = self.arrivals * 3 // 5


def main_kernel(
    lay,
    x_in,
    qkv_in,
    ao_in,
    cin_in,
    co_in,
    up_in,
    down_in,
    gain_in,
    bias_in,
    taps_in,
    positions,
    out_grads_in,
    half_size,
    plan,
    final,
    layer_rows,
    input_rows,
    misc_out,
    tap_weight,
    tap_on,
    where,
    gain,
    bias,
    cotangent,
    out_grads,
    wqkv,
    wao,
    wcin,
    wco,
    wup,
    wdown,
    hid,
    dfull,
    normed,
    inverse,
    qkv,
    probs,
    mix,
    dmix,
    dqkv,
    dkv,
    units,
    slope,
    dbefore,
    last_units,
    value,
    sig,
    gated,
    conv,
    dconv,
    dgates,
    hits,
    mh,
    mnorm,
    mslope,
    munits,
    cs,
    cr,
    ys,
    yr,
    ms,
    mr,
    mys,
    myr,
    grads,
    xr,
    za,
    zb,
    factors,
    pair,
    punits,
    pslope,
    pdbefore,
    misc,
    misc_in,
    load_sem,
    send_sem,
    recv_sem,
):
    section, replica, member = (
        lax.axis_index("section"),
        lax.axis_index("dp"),
        lax.axis_index("mp"),
    )
    low = lax.rem(member, 2)
    high = lax.div(member, 2)
    part, chunk, width = lay.part, lay.chunk, lay.width
    hw, marked = lay.heads_width, lay.marked
    local_heads = hw // HEAD
    scale = HEAD ** (-0.5)
    side = (section, replica, member + 1 - 2 * low)
    across = (section, replica, lax.rem(member + 2, GROUP))
    is_end = (section == 0) | (section == SECTIONS - 1)
    is_inner = jnp.logical_not(is_end)
    inner_of = jnp.where(section == 0, 1, SECTIONS - 2)
    end_of = jnp.where(section == 1, 0, SECTIONS - 1)
    other_inner = SECTIONS - 1 - section
    counter = [0, 0]
    closing = []
    leaving = {}

    def section_peer(by):
        return (lax.rem(section + by, SECTIONS), replica, member)

    def replica_peer(by):
        return (section, lax.rem(replica + by, lay.dp), member)

    def replica_bit(bit):
        on = lax.rem(lax.div(replica, 1 << bit), 2)
        return (section, replica + (1 - 2 * on) * (1 << bit), member), on

    free, departures = [], {}

    def slots():
        at = counter[0]
        counter[0] += 1
        if not free:
            free.append(counter[1])
            counter[1] += 1
        departures[at] = free.pop()
        return at

    def settle(keep=0):
        while len(closing) > keep:
            wait, done = closing.pop(0)
            wait()
            free.extend(departures[slot] for slot in done)

    def remote(src, dst, target, slot):
        return pltpu.make_async_remote_copy(
            src_ref=src,
            dst_ref=dst,
            send_sem=send_sem.at[departures[slot]],
            recv_sem=recv_sem.at[slot],
            device_id=target,
            device_id_type=MESH,
        )

    def send(src, dst, target, slot=None):
        slot = slots() if slot is None else slot
        copy = remote(src, dst, target, slot)
        copy.start()
        closing.append((copy.wait_send, (slot,)))
        return copy

    def send_slot(name, ref, e, t, dst, target):
        slot = slots()
        copy = remote(ref.at[SETS[e], t], dst.at[SETS[e], t], target, slot)
        copy.start()
        leaving[name, SETS[e], t] = copy.wait_send, (slot,)
        return copy

    def reuse(name, e, t):
        entry = leaving.pop((name, SETS[e], t), None)
        if entry is not None:
            closing.insert(0, entry)
            settle(len(closing) - 1)

    barrier = pltpu.get_barrier_semaphore()
    peers = (
        [side, across]
        + [section_peer(by) for by in range(1, SECTIONS)]
        + [replica_peer(by) for by in range(1, lay.dp)]
    )
    for peer in peers:
        pl.semaphore_signal(barrier, inc=1, device_id=peer, device_id_type=MESH)

    loads = {}
    for at, (name, src, dst) in enumerate(
        [
            ("x", x_in.at[section], hid.at[0, pl.ds(pl.multiple_of(member * part, part), part)]),
            ("qkv", qkv_in, wqkv),
            ("ao", ao_in, wao),
            ("gain", gain_in, gain),
            ("out_grads", out_grads_in, out_grads),
            ("bias", bias_in, bias),
            ("up", up_in, wup),
            ("down", down_in, wdown),
            ("cin", cin_in, wcin),
            ("co", co_in, wco),
        ]
    ):
        copy = pltpu.make_async_copy(src, dst, load_sem.at[at])
        copy.start()
        loads[name] = copy

    misc[...] = jnp.zeros_like(misc)
    holds = section < lay.micro
    for i in range(lay.micro):
        holds = holds | (plan[replica, i, 1] == section)
    used = jnp.where(holds, 1.0, 0.0).astype(F32)
    tap_row = lax.broadcasted_iota(jnp.int32, (TAPS, hw), 0)
    tap_mask = jnp.where(jnp.abs(tap_row - MARGIN) <= half_size[0], 1.0, 0.0)
    tap_on[...] = jnp.zeros_like(tap_on)
    tap_on[0:TAPS] = tap_mask
    tap_weight[0:TAPS] = taps_in[...].astype(F32) * tap_mask
    where[...] = jnp.full(where.shape, -1, jnp.int32)
    where[0:1, 0 : positions.shape[1]] = positions[pl.ds(section, 1)]
    lane = lax.broadcasted_iota(jnp.int32, (1, hw), 1)
    head_lanes = [(lane >= HEAD * i) & (lane < HEAD * (i + 1)) for i in range(local_heads)]
    head_low = [jnp.where(on, 1.0, 0.0).astype(BF16) for on in head_lanes]

    def block(at, size):
        return pl.ds(pl.multiple_of(at, size), size)

    def own_rows(t):
        return block(chunk * t + part * low, part)

    def other_rows(t):
        return block(chunk * t + part * (1 - low), part)

    def tiles(count, body, init=0):
        return lax.fori_loop(0, count, body, init)

    def exchange_send(e, t, product):
        reuse("cs", e, t)
        reuse("ys", e, t)
        cs[SETS[e], t] = product(1 - low).astype(BF16)
        copy = send_slot("cs", cs, e, t, cr, side)
        ys[SETS[e], t] = product(low).astype(BF16)
        return copy

    def half_rows(t, core):
        return block(chunk * t + part * core, part)

    def sums_across(e, t, core_copy, start=True):
        core_copy.wait_recv()
        at = SETS[e]

        def body(i, carry):
            rows = block(i * TILE, TILE)
            ys[at, t, rows] = (ys[at, t, rows].astype(F32) + cr[at, t, rows].astype(F32)).astype(BF16)
            return carry

        tiles(part // TILE, body)
        if start:
            return send_slot("ys", ys, e, t, yr, across)

    def total_tile(e, t, rows):
        return ys[SETS[e], t, rows].astype(F32) + yr[SETS[e], t, rows].astype(F32)

    def send_half(e):
        slot = slots()
        at = SETS[e]
        out = remote(ys.at[at, 1 - high], yr.at[at, 1 - high], across, slot)
        out.start()
        leaving["ys", at, 0] = out.wait_send, (slot,)
        return remote(ys.at[at, high], yr.at[at, high], across, slot)

    def add_stat(column, amount):
        cell = (lax.broadcasted_iota(jnp.int32, (8, width), 0) == replica) & (
            lax.broadcasted_iota(jnp.int32, (8, width), 1) == column
        )
        misc[8:16] += jnp.where(cell, amount, 0.0)

    core_copies, y_copies, gathered = {}, {}, {}

    def begin(e, t, work):
        core_copies[e, t] = exchange_send(e, t, work(t))

    def cross(e, t):
        y_copies[e, t] = sums_across(e, t, core_copies[e, t])

    def end(e, t, finish):
        y_copies[e, t].wait_recv()
        gathered[e, t] = finish(t)

    pair_peer, pair_on = replica_bit(lay.bits - 1)
    pair_copies = {}
    halfway = lay.hidden // 2
    half_lanes = pl.ds(pl.multiple_of(pair_on * halfway, 128), halfway)

    def to_pair(which, t, src):
        rows = own_rows(t)
        pair_copies[which, t] = send(src.at[rows], pair.at[which, rows], pair_peer)

    def pass_on(which):
        for t in range(2):
            pair_copies[which, t].wait_recv()
            rows = own_rows(t)
            pair_copies[which, t] = send(pair.at[which, rows], pair.at[which, rows], side)

    def forward_finish(e, k, keep_normed):
        def finish(t):
            at = chunk * t + part * low

            def body(i, carry):
                rows = block(i * TILE, TILE)
                place = block(at + i * TILE, TILE)
                stream = hid[k, place].astype(F32)
                branch = total_tile(e, t, rows)
                norm, inv = normalise(stream + branch)
                if keep_normed:
                    normed[k, t, rows] = norm
                    inverse[k, t, rows] = inv
                hid[k + 1, place] = (norm * gain[k : k + 1] + bias[k : k + 1]).astype(BF16)
                return (carry[0] + fold(stream * stream), carry[1] + fold(branch * branch))

            zero = jnp.zeros((8, width), F32)
            squares = tiles(part // TILE, body, (zero, zero))

            @pl.when(high == t)
            def _():
                add_stat(k, whole_sum(squares[0]) * used)
                add_stat(4 + k, whole_sum(squares[1]) * used)

            rows = own_rows(t)
            copy = send(hid.at[k + 1, rows], hid.at[k + 1, rows], side)
            if k == 0:
                to_pair(0, t, hid.at[1])
            return copy

        return finish

    def norm_back_rows(k, t, grad_tile):
        at = chunk * t + part * low

        def body(i, carry):
            rows = block(i * TILE, TILE)
            dy = grad_tile(rows, block(at + i * TILE, TILE))
            norm = normed[k, t, rows]
            result = norm_pull(dy, norm, inverse[k, t, rows], gain[k : k + 1])
            normed[k, t, rows] = result
            dfull[k, block(at + i * TILE, TILE)] = result.astype(BF16)
            return (carry[0] + fold(dy * norm), carry[1] + fold(dy))

        zero = jnp.zeros((8, width), F32)
        terms = tiles(part // TILE, body, (zero, zero))

        @pl.when(high == t)
        def _():
            misc[k : k + 1] += jnp.sum(terms[0], axis=0, keepdims=True)
            misc[4 + k : 5 + k] += jnp.sum(terms[1], axis=0, keepdims=True)

        rows = own_rows(t)
        copy = send(dfull.at[k, rows], dfull.at[k, rows], side)
        if k == 1:
            to_pair(1, t, dfull.at[1])
        return copy

    def marked_total(e, values, during=None):
        ms[e] = values.astype(BF16)
        core = send(ms.at[e], mr.at[e], side)
        core.wait_recv()
        mys[e] = (ms[e].astype(F32) + mr[e].astype(F32)).astype(BF16)
        y = send(mys.at[e], myr.at[e], across)
        if during is not None:
            during()
        y.wait_recv()
        return mys[e].astype(F32) + myr[e].astype(F32)

    def reduce_piece(base, stride, size, paired):
        steps = []
        first, bit = base, lay.bits - 1
        while bit >= 0:
            peer, on = replica_bit(bit)
            keep = first + on * stride
            give = first + (1 - on) * stride
            if not paired:
                xr_at = reduce_piece.xr_at
                reduce_piece.xr_at += size
                copy = send(
                    grads.at[pl.ds(pl.multiple_of(give, 16), size)],
                    xr.at[pl.ds(xr_at, size)],
                    peer,
                )
                yield
                copy.wait_recv()
                step = math.gcd(size, 64)

                def body(i, carry, keep=keep, xr_at=xr_at, step=step):
                    here = pl.ds(pl.multiple_of(keep + i * step, 16), step)
                    there = pl.ds(pl.multiple_of(xr_at + i * step, 16), step)
                    grads[here] = (grads[here].astype(F32) + xr[there].astype(F32)).astype(BF16)
                    return carry

                tiles(size // step, body)
            steps.append((keep, give, size, peer))
            paired = False
            first, bit = keep, bit - 1
            if bit >= 0:
                size = size // 2
                stride = size
        z_at = reduce_piece.z_at
        reduce_piece.z_at += size
        mine = pl.ds(pl.multiple_of(first, 16), size)
        z_rows = pl.ds(z_at, size)
        step = math.gcd(size, 64)
        slot_a, slot_b = slots(), slots()

        def z_copy(kind):
            if kind == "a":
                return remote(
                    grads.at[mine], za.at[z_rows], (inner_of, replica, member), slot_a
                )
            if kind == "b":
                return remote(
                    grads.at[mine], zb.at[z_rows], (other_inner, replica, member), slot_b
                )
            return remote(final.at[mine], final.at[mine], (end_of, replica, member), slot_a)

        steps.reverse()
        gather_slots = [slots() for _ in steps]

        def gather(at, arriving=False):
            keep, give, half, peer = steps[at]
            rows = pl.ds(pl.multiple_of(give if arriving else keep, 16), half)
            return remote(final.at[rows], final.at[rows], peer, gather_slots[at])

        @pl.when(is_end)
        def _():
            z_copy("a").start()

        yield

        @pl.when(is_inner)
        def _():
            z_copy("a").wait_recv()

            def body(i, carry):
                here = pl.ds(pl.multiple_of(first + i * step, 16), step)
                there = pl.ds(pl.multiple_of(z_at + i * step, 16), step)
                grads[here] = (grads[here].astype(F32) + za[there].astype(F32)).astype(BF16)
                return carry

            tiles(size // step, body)
            z_copy("b").start()

        yield

        @pl.when(is_inner)
        def _():
            z_copy("b").wait_recv()

            def body(i, carry):
                here = pl.ds(pl.multiple_of(first + i * step, 16), step)
                there = pl.ds(pl.multiple_of(z_at + i * step, 16), step)
                final[here] = (grads[here].astype(F32) + zb[there].astype(F32)).astype(BF16)
                return carry

            tiles(size // step, body)
            z_copy("c").start()
            gather(0).start()

        yield

        @pl.when(is_end)
        def _():
            z_copy("c").wait_recv()
            gather(0).start()

        yield
        for at in range(len(steps)):
            if at > 0:
                gather(at).start()
                yield
            gather(at, True).wait_recv()
            closing.append((gather(at).wait_send, (gather_slots[at],)))

        def close():
            @pl.when(is_end)
            def _():
                z_copy("a").wait_send()

            @pl.when(is_inner)
            def _():
                z_copy("b").wait_send()
                z_copy("c").wait_send()

        closing.append((close, (slot_a, slot_b)))

    reduce_piece.xr_at = 0
    reduce_piece.z_at = 0
    running = {}
    summed = set()

    def launch(*names):
        for name in names:
            spec = lay.pieces.get(name)
            running[name] = reduce_piece(*spec)
            next(running[name])

    def start(name, task):
        running[name] = task
        next(task)

    def pump(*names):
        settle(KEEP)
        for name in names:
            if name in running:
                try:
                    next(running[name])
                except StopIteration:
                    del running[name]

    def line_gather(view):
        right, left = [slots() for _ in range(3)], [slots() for _ in range(3)]

        def hop(k, to_right, at):
            origin = at - k if to_right else at + k
            target = (section + (1 if to_right else -1), replica, member)
            return remote(view(origin), view(origin), target, (right if to_right else left)[k])

        def sends(k, action):
            @pl.when((section >= k) & (section < SECTIONS - 1))
            def _():
                getattr(hop(k, True, section), action)()

            @pl.when((section + k < SECTIONS) & (section > 0))
            def _():
                getattr(hop(k, False, section), action)()

        def arrivals(k):
            @pl.when(section > k)
            def _():
                hop(k, True, section - 1).wait_recv()

            @pl.when(section + k < SECTIONS - 1)
            def _():
                hop(k, False, section + 1).wait_recv()

        for k in range(SECTIONS - 1):
            sends(k, "start")
            closing.append((functools.partial(sends, k, "wait_send"), (right[k], left[k])))
            yield
            arrivals(k)

    pl.semaphore_wait(barrier, len(peers))
    mine = block(member * part, part)
    to_across = send(x_in.at[section], hid.at[0, mine], across)
    to_side = send(x_in.at[section], hid.at[0, mine], side)
    loads["x"].wait()
    hits[...] = jnp.where(
        lax.broadcasted_iota(jnp.int32, hits.shape, 0) == where[0:1, 0 : hits.shape[1]], 1.0, 0.0
    ).astype(BF16)
    loads["qkv"].wait()

    def project(at):
        rows = block(at, part)
        for j in range(3):
            qkv[j, rows] = dot_lanes(hid[0, rows], wqkv[j]).astype(BF16)

    project(member * part)
    to_side.wait_recv()
    project(side[2] * part)
    to_across.wait_recv()
    theirs = block(across[2] * part, part)
    onward = send(hid.at[0, theirs], hid.at[0, theirs], side)
    project(across[2] * part)
    onward.wait_recv()
    project(lax.rem(side[2] + 2, GROUP) * part)
    loads["ao"].wait()

    def attention_work(t):
        rows = pl.ds(chunk * t, chunk)
        mixture = jnp.zeros((chunk, hw), F32)
        for i in range(local_heads):
            if t == 1 and i == 1:
                cross(0, 0)
            scores = dot_lanes(qkv[0, rows] * head_low[i], qkv[1]) * scale
            top = jnp.max(scores, axis=-1, keepdims=True)
            powers = jnp.exp(scores - top)
            chances = powers * (1.0 / jnp.sum(powers, axis=-1, keepdims=True))
            probs[i, rows] = chances
            mixture = mixture + jnp.where(head_lanes[i], dot(chances.astype(BF16), qkv[2]), 0.0)
        mix[rows] = mixture.astype(BF16)
        return lambda core: dot(mix[half_rows(t, core)], wao[...])

    begin(0, 0, attention_work)
    begin(0, 1, attention_work)
    cross(0, 1)
    loads["up"].wait()
    loads["down"].wait()

    def ffn_forward(layer, src, rows, units_here, slope_here=None):
        def body(i, carry):
            lanes = block(i * LANES, LANES)
            unit, steep = gelu_parts(dot(src[rows], wup[layer, :, lanes]))
            units_here[:, lanes] = unit.astype(BF16)
            if slope_here is not None:
                slope_here[:, lanes] = steep
            return carry

        tiles(lay.hidden // LANES, body)

    def ffn0_work(t):
        for core in (low, 1 - low):
            if core is not low:
                gathered[0, t].wait_recv()
            rows = half_rows(t, core)
            ffn_forward(0, hid.at[1], rows, units.at[rows], slope.at[rows])
        return lambda core: dot(units[half_rows(t, core)], wdown[0])

    for name in ("gain", "bias"):
        loads[name].wait()
    attention_finish = forward_finish(0, 0, True)
    end(0, 0, attention_finish)
    begin(1, 0, ffn0_work)
    end(0, 1, attention_finish)
    cross(1, 0)
    begin(1, 1, ffn0_work)
    cross(1, 1)

    loads["cin"].wait()
    loads["co"].wait()
    edge = jnp.zeros((PAD, hw), F32)
    for buffer in (gated, dconv):
        buffer[0:PAD] = edge
        buffer[PAD + lay.seq : 2 * PAD + lay.seq] = edge

    def conv_gates(t):
        for core in (low, 1 - low):
            if core is not low:
                gathered[1, t].wait_recv()
            rows = half_rows(t, core)
            value_here = dot_lanes(hid[2, rows], wcin[0])
            sig_here = jax.nn.sigmoid(dot_lanes(hid[2, rows], wcin[1]))
            value[rows] = value_here
            sig[rows] = sig_here
            place = pl.ds(pl.multiple_of(PAD + chunk * t + part * core, 8), part)
            gated[place] = value_here * sig_here

    ffn0_finish = forward_finish(1, 1, True)
    pass_on(0)
    end(1, 0, ffn0_finish)
    conv_gates(0)
    end(1, 1, ffn0_finish)
    conv_gates(1)
    tap_tile = 64

    def taps(i, carry):
        total = jnp.zeros((tap_tile, hw), F32)
        window = gated[pl.ds(pl.multiple_of(i * tap_tile, 8), tap_tile + 2 * PAD)]
        for j in range(TAPS):
            at = PAD - MARGIN + j
            total = total + tap_weight[j : j + 1] * window[at : at + tap_tile]
        conv[block(i * tap_tile, tap_tile)] = total.astype(BF16)
        return carry

    tiles(lay.seq // tap_tile, taps)

    spots = hits[...]
    conv_marked = dot_rows(spots, conv[...]).astype(BF16)
    stream = dot_rows(spots, hid[2])

    def pair_up(t):
        pair_copies[0, t].wait_recv()
        rows = pl.ds(chunk * t, chunk)
        unit, slope_here = gelu_parts(dot(pair[0, rows], wup[0, :, half_lanes]))
        punits[rows] = unit.astype(BF16)
        pslope[rows] = slope_here


    def conv_work(t):
        return lambda core: dot(conv[half_rows(t, core)], wco[...])

    def ffn1_work(t):
        gathered[5, t].wait_recv()
        ffn_forward(1, hid.at[3], pl.ds(chunk * t, chunk), last_units)
        return lambda core: dot(last_units[block(part * core, part)], wdown[1])

    def layer_output():
        last_finish = forward_finish(5, 2, False)
        begin(5, 0, conv_work)
        begin(5, 1, conv_work)
        cross(5, 0)
        yield
        cross(5, 1)
        yield
        end(5, 0, last_finish)
        yield
        end(5, 1, last_finish)
        yield
        begin(6, 0, ffn1_work)
        yield
        begin(6, 1, ffn1_work)
        for t in range(2):
            sums_across(6, t, core_copies[6, t], start=False)
        last = send_half(6)
        yield
        last.wait_recv()

        def layer_body(i, carry):
            rows = block(i * TILE, TILE)
            stream = hid[3, block(member * part + i * TILE, TILE)].astype(F32)
            branch = total_tile(6, high, rows)
            norm, _ = normalise(stream + branch)
            result = (norm * gain[3:4] + bias[3:4]) * used
            layer_rows[section, rows] = result.astype(BF16)
            return (carry[0] + fold(stream * stream), carry[1] + fold(branch * branch))

        zero = jnp.zeros((8, width), F32)
        squares = tiles(part // TILE, layer_body, (zero, zero))
        add_stat(3, whole_sum(squares[0]) * used)
        add_stat(7, whole_sum(squares[1]) * used)
        summed.add("rows")
        yield from line_gather(lambda at: layer_rows.at[at])

    branch = marked_total(
        0, dot(conv_marked, wco[...]), lambda: start("lo", layer_output())
    )
    norm2, inv2 = normalise(stream + branch)
    mnorm[0] = norm2
    mh[...] = (norm2 * gain[2:3] + bias[2:3]).astype(BF16)

    def pick_cotangent():
        loads["out_grads"].wait()
        count = out_grads.shape[0]
        slot = lax.broadcasted_iota(jnp.int32, (1, out_grads.shape[1], 1), 1)
        mine = jnp.where(slot == section, used, 0.0)
        cotangent[...] = jnp.zeros_like(cotangent)
        cotangent[0:count] = jnp.sum(out_grads[...].astype(F32) * mine, axis=1)

    def marked_up(i, carry):
        lanes = block(i * LANES, LANES)
        unit, slope_here = gelu_parts(dot(mh[...], wup[1, :, lanes]))
        munits[:, lanes] = unit.astype(BF16)
        mslope[:, lanes] = slope_here
        return carry

    tiles(lay.hidden // LANES, marked_up)

    def beside_units():
        pump("lo")
        pick_cotangent()
        pair_up(0)

    branch = marked_total(1, dot(munits[...], wdown[1]), beside_units)
    norm3, inv3 = normalise(mh[...].astype(F32) + branch)
    once = jnp.where(member == 0, 1.0, 0.0).astype(F32)
    dy = cotangent[...]
    misc[3:4] += once * jnp.sum(dy * norm3, axis=0, keepdims=True)
    misc[7:8] += once * jnp.sum(dy, axis=0, keepdims=True)
    dz3 = norm_pull(dy, norm3, inv3, gain[3:4])
    cotangent[...] = dz3
    df3 = dz3.astype(BF16)

    per_section = lay.dp * marked
    here = pl.ds(pl.multiple_of(section * per_section + replica * marked, 16), marked)
    factors[0, here] = mh[...]
    factors[1, here] = df3

    def spread_factors():
        copies = [
            send(factors.at[low, here], factors.at[low, here], replica_peer(by))
            for by in range(1, lay.dp)
        ]
        yield
        for copy in copies:
            copy.wait_recv()
        def of_section(at):
            return factors.at[low, pl.ds(pl.multiple_of(at * per_section, 16), per_section)]

        yield from line_gather(of_section)
        slot = slots()
        send(factors.at[low], factors.at[low], side, slot)
        yield
        remote(factors.at[1 - low], factors.at[1 - low], side, slot).wait_recv()

    start("fa", spread_factors())

    def marked_down(i, carry):
        lanes = block(i * LANES, LANES)
        grad_units = dot_lanes(factors[1, here], wdown[1, lanes])
        munits[:, lanes] = (grad_units * mslope[:, lanes]).astype(BF16)
        return carry

    tiles(lay.hidden // LANES, marked_down)
    def beside_down():
        pair_up(1)
        pump("lo")
        pump("lo")

    dy = cotangent[...] + marked_total(2, dot_lanes(munits[...], wup[1]), beside_down)
    pump("fa")
    norm2 = mnorm[0]
    misc[2:3] += once * jnp.sum(dy * norm2, axis=0, keepdims=True)
    misc[6:7] += once * jnp.sum(dy, axis=0, keepdims=True)
    dz2 = norm_pull(dy, norm2, inv2, gain[2:3])
    dz2_terms = two_terms(dz2)
    df2 = dz2.astype(BF16)

    def spread(rows, terms):
        where_rows = hits[rows]
        return dot(where_rows, terms[0]) + dot(where_rows, terms[1])

    dconv_terms = two_terms(dot_lanes(df2, wco[...]))
    dconv[pl.ds(PAD, lay.seq)] = spread(pl.ds(0, lay.seq), dconv_terms)

    def taps_back(i, carry):
        total = jnp.zeros((tap_tile, hw), F32)
        place = pl.ds(pl.multiple_of(i * tap_tile, 8), tap_tile + 2 * PAD)
        window = dconv[place]
        around = gated[place]
        middle = window[PAD : PAD + tap_tile]
        sums = []
        for j in range(TAPS):
            at = PAD + MARGIN - j
            total = total + tap_weight[j : j + 1] * window[at : at + tap_tile]
            at = PAD - MARGIN + j
            sums.append(jnp.sum(around[at : at + tap_tile] * middle, axis=0, keepdims=True))
        rows = block(i * tap_tile, tap_tile)
        s = sig[rows]
        by_value = total * s
        dgates[0, rows] = by_value.astype(BF16)
        dgates[1, rows] = (by_value * value[rows] * (1.0 - s)).astype(BF16)
        sums.append(jnp.zeros((1, hw), F32))
        return carry + jnp.concatenate(sums, axis=0)

    def conv_back_work(t):
        def product(core):
            rows = half_rows(t, core)
            return dot(dgates[0, rows], wcin[0]) + dot(dgates[1, rows], wcin[1])

        return product

    half_tiles = chunk // tap_tile
    kernel_rows = lax.fori_loop(0, half_tiles, taps_back, jnp.zeros((8, hw), F32))
    begin(2, 0, conv_back_work)
    kernel_rows = lax.fori_loop(half_tiles, 2 * half_tiles, taps_back, kernel_rows)
    cross(2, 0)
    begin(2, 1, conv_back_work)
    kernel_rows = kernel_rows * tap_on[...]
    grads[pl.ds(lay.kernel_at, lay.up_at - lay.kernel_at)] = jnp.zeros(
        (lay.up_at - lay.kernel_at, width), BF16
    )
    grads[pl.ds(lay.kernel_at, 16), 0:hw] = jnp.concatenate(
        [kernel_rows, jnp.zeros((8, hw), F32)], axis=0
    ).astype(BF16)

    def conv_back_finish(t):
        def grad_tile(rows, place):
            return total_tile(2, t, rows) + spread(place, dz2_terms)

        return norm_back_rows(1, t, grad_tile)

    def ffn0_back_work(t):
        for core in (low, 1 - low):
            if core is not low:
                gathered[2, t].wait_recv()
            rows = half_rows(t, core)

            def body(i, carry, rows=rows):
                lanes = block(i * LANES, LANES)
                grad_units = dot_lanes(dfull[1, rows], wdown[0, lanes])
                dbefore[rows, lanes] = (grad_units * slope[rows, lanes]).astype(BF16)
                return carry

            tiles(lay.hidden // LANES, body)
        return lambda core: dot_lanes(dbefore[half_rows(t, core)], wup[0])

    def ffn0_back_finish(t):
        return norm_back_rows(
            0, t, lambda rows, place: normed[1, t, rows] + total_tile(3, t, rows)
        )

    up_rows = pl.ds(pl.multiple_of(lay.up_at + pair_on * halfway, 16), halfway)
    down_rows = pl.ds(pl.multiple_of(lay.down_at + pair_on * halfway, 16), halfway)

    def own_weights():
        left = dbefore[:, half_lanes]
        for q in range(2):
            lanes = pl.ds(q * halfway, halfway)
            grads[up_rows, lanes] = dot_rows(hid[1, :, lanes], left).astype(BF16)
        grads[down_rows] = dot_rows(units[:, half_lanes], dfull[1]).astype(BF16)

    def pair_weights():
        for t in range(2):
            pair_copies[1, t].wait_recv()
            rows = pl.ds(chunk * t, chunk)
            grad_units = dot_lanes(pair[1, rows], wdown[0, half_lanes])
            pdbefore[rows] = (grad_units * pslope[rows]).astype(BF16)
        left = pdbefore[...]
        for q in range(2):
            lanes = pl.ds(q * halfway, halfway)
            total = grads[up_rows, lanes].astype(F32) + dot_rows(pair[0, :, lanes], left)
            grads[up_rows, lanes] = total.astype(BF16)
        launch(*lay.groups["u"])
        total = grads[down_rows].astype(F32) + dot_rows(punits[...], pair[1])
        grads[down_rows] = total.astype(BF16)
        launch(*lay.groups["d"])

    def attention_back_work(t):
        def product(core):
            rows = half_rows(t, core)
            return (
                dot(dqkv[0, rows], wqkv[0])
                + dot(dqkv[1, rows], wqkv[1])
                + dot(dqkv[2, rows], wqkv[2])
            )

        return product

    def attention_back_rows(t):
        gathered[3, t].wait_recv()
        rows = pl.ds(chunk * t, chunk)
        dmix[rows] = dot_lanes(dfull[0, rows], wao[...]).astype(BF16)
        grad_queries = jnp.zeros((chunk, hw), F32)
        for i in range(local_heads):
            chances = probs[i, rows]
            grad_chances = dot_lanes(dmix[rows] * head_low[i], qkv[2])
            grad_scores = chances * (
                grad_chances - jnp.sum(grad_chances * chances, axis=-1, keepdims=True)
            )
            grad_scores = grad_scores.astype(BF16)
            on = head_lanes[i]
            grad_queries = grad_queries + jnp.where(on, dot(grad_scores, qkv[1]), 0.0)
            dkv[0] += jnp.where(on, dot_rows(grad_scores, qkv[0, rows]), 0.0)
            dkv[1] += jnp.where(on, dot_rows(chances.astype(BF16), dmix[rows]), 0.0)
        dqkv[0, rows] = (grad_queries * scale).astype(BF16)

    waits = {}

    def backward():
        cross(2, 1)
        for j in range(2):
            grads[pl.ds(lay.conv_at + j * hw, hw)] = dot_rows(dgates[j], hid[2]).astype(BF16)
        grads[pl.ds(lay.conv_at + 2 * hw, hw)] = dot_rows(conv_marked, df2).astype(BF16)
        launch(*lay.groups["c"])
        yield
        end(2, 0, conv_back_finish)
        begin(3, 0, ffn0_back_work)
        yield
        end(2, 1, conv_back_finish)
        cross(3, 0)
        begin(3, 1, ffn0_back_work)
        cross(3, 1)
        yield
        end(3, 0, ffn0_back_finish)
        yield
        end(3, 1, ffn0_back_finish)
        summed.add("norms")
        yield
        dkv[...] = jnp.zeros_like(dkv)
        attention_back_rows(0)
        yield
        attention_back_rows(1)
        dqkv[1] = (dkv[0] * scale).astype(BF16)
        dqkv[2] = dkv[1].astype(BF16)
        for j in range(3):
            grads[pl.ds(lay.attn_at + j * hw, hw)] = dot_rows(dqkv[j], hid[0]).astype(BF16)
        grads[pl.ds(lay.attn_at + 3 * hw, hw)] = dot_rows(mix[...], dfull[0]).astype(BF16)
        launch(*lay.groups["a"])
        for t in range(2):
            begin(4, t, attention_back_work)
        for t in range(2):
            sums_across(4, t, core_copies[4, t], start=False)
        waits["input"] = send_half(4)

    def feed_forward_weights():
        own_weights()
        yield
        pass_on(1)
        yield
        pair_weights()

    def input_body(i, carry):
        rows = block(i * TILE, TILE)
        total = total_tile(4, high, rows)
        input_rows[section, rows] = (normed[0, high, rows] + total).astype(BF16)
        return carry

    def input_gradient():
        waits["input"].wait_recv()
        tiles(part // TILE, input_body)
        yield from line_gather(lambda at: input_rows.at[at])

    group_rows = GROUP * marked
    groups = SECTIONS * per_section // group_rows

    def last_block():
        assert not {"main", "pw", "fa"} & set(running)
        for group in range(groups):
            rows = pl.ds(group * group_rows, group_rows)

            def recompute(j, carry, rows=rows):
                lanes = block(j * LANES, LANES)
                unit, slope_here = gelu_parts(dot(factors[0, rows], wup[1, :, lanes]))
                units[0:group_rows, lanes] = unit.astype(BF16)
                grad_units = dot_lanes(factors[1, rows], wdown[1, lanes])
                dbefore[0:group_rows, lanes] = (grad_units * slope_here).astype(BF16)
                return carry

            tiles(lay.hidden // LANES, recompute)

            def last_weights(i, carry, rows=rows, group=group):
                lanes = block(i * LANES, LANES)
                by_up = dot_rows(factors[0, rows, lanes], dbefore[0:group_rows])
                by_down = dot_rows(units[0:group_rows, lanes], factors[1, rows])
                wide, rest = probs.shape[2], width - probs.shape[2]
                held = [
                    (
                        probs.at[i, pl.ds(j * LANES, LANES)],
                        slope.at[pl.ds(j * LANES, LANES), block(i * rest, rest)],
                    )
                    for j in range(2)
                ]
                if group > 0:
                    by_up = by_up + jnp.concatenate([held[0][0][...], held[0][1][...]], axis=1)
                    by_down = by_down + jnp.concatenate([held[1][0][...], held[1][1][...]], axis=1)
                if group < groups - 1:
                    for (left, right), total in zip(held, (by_up, by_down)):
                        left[...] = total[:, :wide]
                        right[...] = total[:, wide:]
                else:
                    at = pl.multiple_of(i * LANES, LANES)
                    final[pl.ds(lay.up1_at + at, LANES)] = by_up.astype(BF16)
                    final[pl.ds(lay.down1_at + at, LANES)] = by_down.astype(BF16)
                return carry

            tiles(width // LANES, last_weights)
            yield

    def small_sums():
        assert summed >= {"norms", "rows"}
        hops = [side, across] + [replica_bit(bit)[0] for bit in range(lay.bits)]
        for at, peer in enumerate(hops):
            misc_in[2 * at] = misc[...]
            copy = send(misc_in.at[2 * at], misc_in.at[2 * at + 1], peer)
            yield
            copy.wait_recv()
            misc[...] = misc_in[2 * at] + misc_in[2 * at + 1]
        at = 2 * len(hops)
        slot_a, slot_b = slots(), slots()
        to_inner = remote(misc_in.at[at], misc_in.at[at + 1], (inner_of, replica, member), slot_a)
        to_other = remote(
            misc_in.at[at + 2], misc_in.at[at + 3], (other_inner, replica, member), slot_b
        )
        to_end = remote(misc_out, misc_out, (end_of, replica, member), slot_a)

        @pl.when(is_end)
        def _():
            misc_in[at] = misc[...]
            to_inner.start()

        yield

        @pl.when(is_inner)
        def _():
            to_inner.wait_recv()
            misc_in[at + 2] = misc[...] + misc_in[at + 1]
            to_other.start()

        yield

        @pl.when(is_inner)
        def _():
            to_other.wait_recv()
            misc_out[...] = misc_in[at + 2] + misc_in[at + 3]
            to_end.start()

        yield

        @pl.when(is_end)
        def _():
            to_end.wait_recv()
            to_inner.wait_send()

        @pl.when(is_inner)
        def _():
            to_other.wait_send()
            to_end.wait_send()

    later = {
        "main": backward,
        "pw": feed_forward_weights,
        "ig": input_gradient,
        "w1": last_block,
        "ms": small_sums,
    }
    for name in TAIL:
        if name in later:
            start(name, later.pop(name)())
        else:
            pump(name)
    assert not later
    while running:
        pump(*list(running))
    closing.extend(leaving.values())
    settle()
    assert counter[0] <= lay.arrivals and counter[1] <= lay.departures


def widen_kernel(
    lay,
    final,
    input_rows,
    layer_rows,
    misc,
    plan,
    layer_out,
    input_grad,
    qkv,
    out,
    cin,
    cout,
    up,
    down,
    kernel,
    gains,
    biases,
    rms,
    wide,
    wide_input,
    store_sem,
):
    hw, width, hidden = lay.heads_width, lay.width, lay.hidden
    blocks = []

    def cover(start, rows, target, step):
        for at in range(0, rows, step):
            blocks.append((start + at, step, target.at[pl.ds(at, step)]))

    for layer, (up_at, down_at) in enumerate(
        ((lay.up_at, lay.down_at), (lay.up1_at, lay.down1_at))
    ):
        cover(up_at, width, up.at[layer], width // 2)
        cover(down_at, hidden, down.at[layer], hidden // 2)
    for j in range(3):
        cover(lay.attn_at + j * hw, hw, qkv.at[j], hw)
    cover(lay.attn_at + 3 * hw, hw, out, hw)
    for j in range(2):
        cover(lay.conv_at + j * hw, hw, cin.at[j], hw)
    cover(lay.conv_at + 2 * hw, hw, cout, hw)

    def store(at):
        start, rows, target = blocks[at]
        return pltpu.make_async_copy(wide.at[pl.ds(start, rows)], target, store_sem.at[at])

    extra = len(blocks)
    inputs_out = pltpu.make_async_copy(wide_input, input_grad, store_sem.at[extra])
    layer_done = pltpu.make_async_copy(layer_rows, layer_out, store_sem.at[extra + 1])
    layer_done.start()
    gains[...] = misc[0:4]
    biases[...] = misc[4:8]
    row = lax.broadcasted_iota(jnp.int32, rms.shape, 0)
    counts = jnp.zeros(rms.shape, F32)
    for r in range(rms.shape[0]):
        total = jnp.float32(lay.micro)
        for i in range(lay.micro):
            total = total + jnp.where(plan[r, i, 1] >= 0, 1.0, 0.0).astype(F32)
        counts = jnp.where(row == r, total, counts)
    rms[...] = jnp.sqrt(misc[8 : 8 + rms.shape[0], 0:8] / (counts * (lay.seq * width)))
    half = width // 2
    for at, (start, rows, _) in enumerate(blocks):
        def body(i, carry, start=start, at=at):
            here = pl.ds(pl.multiple_of(start + i * 32, 16), 32)
            if at >= 2:
                wide[here] = final[here].astype(F32)
            else:
                for q in range(2):
                    there = pl.ds(pl.multiple_of(lay.up_at + q * half + i * 32, 16), 32)
                    wide[here, q * half : (q + 1) * half] = final[
                        there, at * half : (at + 1) * half
                    ].astype(F32)
            return carry

        lax.fori_loop(0, rows // 32, body, 0)
        store(at).start()
    for slot in range(input_rows.shape[0]):
        wide_input[slot] = input_rows[slot].astype(F32)
    inputs_out.start()
    taps = final[pl.ds(lay.kernel_at, 16)].astype(F32)
    kernel[...] = taps[0:TAPS, 0:hw]
    for at in range(len(blocks)):
        store(at).wait()
    inputs_out.wait()
    layer_done.wait()


def on_device(
    inputs,
    attn_qkv,
    attn_out,
    conv_in,
    conv_kernel,
    conv_out,
    ffn_up,
    ffn_down,
    norm_gain,
    norm_bias,
    kernel_half,
    batch_plan,
    masked_positions,
    out_grad,
):
    section = lax.axis_index("section")
    replica = lax.axis_index("dp")
    dp = lax.axis_size("dp")
    slot_count, part, width = inputs.shape
    micro_count = batch_plan.shape[1]
    count = masked_positions.shape[1]
    marked = round_up(count, 16)
    assert slot_count == SECTIONS == lax.axis_size("section") and lax.axis_size("mp") == GROUP
    hw = attn_out.shape[0]
    hidden = ffn_up.shape[2]
    lay = Layout(dp, micro_count, part * GROUP, width, hw, hidden, marked)
    assert hidden == width and width % LANES == 0 and hw % HEAD == 0

    seq, chunk = lay.seq, lay.chunk
    any_spec = pl.BlockSpec(memory_space=pl.ANY)
    vmem_spec = pl.BlockSpec(memory_space=pltpu.VMEM)
    hops = 2 + lay.bits
    all_marked = SECTIONS * dp * marked
    scratch = [
        pltpu.VMEM((8, hw), F32),
        pltpu.VMEM((8, hw), F32),
        pltpu.VMEM((8, marked), jnp.int32),
        pltpu.VMEM(norm_gain.shape, F32),
        pltpu.VMEM(norm_bias.shape, F32),
        pltpu.VMEM((marked, width), F32),
        pltpu.VMEM((count, slot_count, width), BF16),
        pltpu.VMEM((3, hw, width), BF16),
        pltpu.VMEM(attn_out.shape, BF16),
        pltpu.VMEM((2, hw, width), BF16),
        pltpu.VMEM(conv_out.shape, BF16),
        pltpu.VMEM(ffn_up.shape, BF16),
        pltpu.VMEM(ffn_down.shape, BF16),
        pltpu.VMEM((4, seq, width), BF16),
        pltpu.VMEM((2, seq, width), BF16),
        pltpu.VMEM((2, 2, part, width), F32),
        pltpu.VMEM((2, 2, part, 1), F32),
        pltpu.VMEM((3, seq, hw), BF16),
        pltpu.VMEM((hw // HEAD, seq, seq), F32),
        pltpu.VMEM((seq, hw), BF16),
        pltpu.VMEM((seq, hw), BF16),
        pltpu.VMEM((3, seq, hw), BF16),
        pltpu.VMEM((2, seq, hw), F32),
        pltpu.VMEM((seq, hidden), BF16),
        pltpu.VMEM((seq, hidden), F32),
        pltpu.VMEM((seq, hidden), BF16),
        pltpu.VMEM((chunk, hidden), BF16),
        pltpu.VMEM((seq, hw), F32),
        pltpu.VMEM((seq, hw), F32),
        pltpu.VMEM((seq + 2 * PAD, hw), F32),
        pltpu.VMEM((seq, hw), BF16),
        pltpu.VMEM((seq + 2 * PAD, hw), F32),
        pltpu.VMEM((2, seq, hw), BF16),
        pltpu.VMEM((seq, marked), BF16),
        pltpu.VMEM((marked, width), BF16),
        pltpu.VMEM((1, marked, width), F32),
        pltpu.VMEM((marked, hidden), F32),
        pltpu.VMEM((marked, hidden), BF16),
        pltpu.VMEM((4, 2, part, width), BF16),
        pltpu.VMEM((4, 2, part, width), BF16),
        pltpu.VMEM((4, 2, part, width), BF16),
        pltpu.VMEM((4, 2, part, width), BF16),
        pltpu.VMEM((3, marked, width), BF16),
        pltpu.VMEM((3, marked, width), BF16),
        pltpu.VMEM((3, marked, width), BF16),
        pltpu.VMEM((3, marked, width), BF16),
        pltpu.VMEM((lay.rows, width), BF16),
        pltpu.VMEM((lay.xr_rows, width), BF16),
        pltpu.VMEM((lay.z_rows, width), BF16),
        pltpu.VMEM((lay.z_rows, width), BF16),
        pltpu.VMEM((2, all_marked, width), BF16),
        pltpu.VMEM((2, seq, width), BF16),
        pltpu.VMEM((seq, hidden // 2), BF16),
        pltpu.VMEM((seq, hidden // 2), F32),
        pltpu.VMEM((seq, hidden // 2), BF16),
        pltpu.VMEM((lay.misc_rows, width), F32),
        pltpu.VMEM((2 * hops + 4, lay.misc_rows, width), F32),
        pltpu.SemaphoreType.DMA((10,)),
        pltpu.SemaphoreType.DMA((lay.departures,)),
        pltpu.SemaphoreType.DMA((lay.arrivals,)),
    ]
    smem_spec = pl.BlockSpec(memory_space=pltpu.SMEM)
    final, layer_rows, input_rows, misc = pl.pallas_call(
        functools.partial(main_kernel, lay),
        out_shape=(
            pltpu.VMEM((lay.all_rows, width), BF16),
            pltpu.VMEM((slot_count, part, width), BF16),
            pltpu.VMEM((slot_count, part, width), BF16),
            pltpu.VMEM((lay.misc_rows, width), F32),
        ),
        in_specs=[any_spec] * 9 + [vmem_spec] * 2 + [any_spec] + [smem_spec] * 2,
        out_specs=(vmem_spec,) * 4,
        scratch_shapes=scratch,
        compiler_params=pltpu.CompilerParams(
            collective_id=0, has_side_effects=True, vmem_limit_bytes=VMEM_BYTES
        ),
        name="layers",
    )(
        inputs,
        jnp.swapaxes(attn_qkv, 1, 2),
        attn_out,
        jnp.swapaxes(conv_in, 1, 2),
        conv_out,
        ffn_up,
        ffn_down,
        norm_gain,
        norm_bias,
        conv_kernel,
        masked_positions,
        jnp.swapaxes(out_grad, 0, 1),
        kernel_half,
        batch_plan,
    )
    shapes = [
        (slot_count, part, width),
        (3, hw, width),
        (hw, width),
        (2, hw, width),
        (hw, width),
        (2, width, hidden),
        (2, hidden, width),
        (TAPS, hw),
        (4, width),
        (4, width),
        (dp, 8),
    ]
    widened = pl.pallas_call(
        functools.partial(widen_kernel, lay),
        out_shape=(jax.ShapeDtypeStruct(shapes[0], BF16),)
        + tuple(jax.ShapeDtypeStruct(shape, F32) for shape in shapes),
        in_specs=[vmem_spec] * 4 + [smem_spec],
        out_specs=(any_spec,) * 8 + (vmem_spec,) * 4,
        scratch_shapes=[
            pltpu.VMEM((lay.all_rows, width), F32),
            pltpu.VMEM((slot_count, part, width), F32),
            pltpu.SemaphoreType.DMA((17,)),
        ],
        compiler_params=pltpu.CompilerParams(vmem_limit_bytes=VMEM_BYTES),
        name="widen",
    )(
        *[
            pltpu.with_memory_space_constraint(result, pltpu.VMEM)
            for result in (final, input_rows, layer_rows, misc)
        ],
        batch_plan,
    )
    (layer_out, input_grad, qkv, out, cin, cout, up, down, kernel, gains, biases, rms) = widened
    return (
        layer_out,
        input_grad,
        jnp.swapaxes(qkv, 1, 2),
        out,
        jnp.swapaxes(cin, 1, 2),
        kernel,
        cout,
        up,
        down,
        gains,
        biases,
        rms,
    )


def solution(mesh):
    return jax.shard_map(
        on_device,
        mesh=mesh,
        in_specs=(
            P("dp", "mp", None),
            P(None, None, "mp"),
            P("mp", None),
            P(None, None, "mp"),
            P(None, "mp"),
            P("mp", None),
            P(None, None, "mp"),
            P(None, "mp", None),
            P(),
            P(),
            P(),
            P(),
            P("dp", None),
            P("dp", None, None),
        ),
        out_specs=(
            P("dp", "mp", None),
            P("dp", "mp", None),
            P(None, None, "mp"),
            P("mp", None),
            P(None, None, "mp"),
            P(None, "mp"),
            P("mp", None),
            P(None, None, "mp"),
            P(None, "mp", None),
            P(),
            P(),
            P(),
        ),
        check_vma=False,
    )
```
